256 devices in a mesh: gz: 32 (over y_lo, z, core), gy: 8 (over x, y_hi).
Axes of the slice: x: 4, y: 4 (y_hi: 2, y_lo: 2; y = y_hi * 2 + y_lo), z: 8, core: 2. Of those that a mesh axis runs over, the one named last changes fastest.
Arguments:
- wave_now: float32 [128, 256, 512], P('gz', 'gy'), may hold values from -6 to 6
- wave_later: float32 [128, 256, 512], P('gz', 'gy'), may hold values from -6 to 6
- adjoint_now: float32 [128, 256, 512], P('gz', 'gy'), may hold values from -6 to 6
- adjoint_later: float32 [128, 256, 512], P('gz', 'gy'), may hold values from -6 to 6
- velocity: float32 [128, 256, 512], P('gz', 'gy'), may hold values from 1.5 to 4.5
- observed: float32 [2, 4096], P(None, ('gz', 'gy')), may hold values from -6 to 6
- receivers: int32 [3, 4096], replicated, may hold values from 0 to 511, as said below
- sources: int32 [3, 4], replicated, may hold values from 0 to 511, as said below
- wavelet: float32 [2, 4], replicated, may hold values from -40 to 40
Outputs:
- wave_first: float32 [128, 256, 512], P('gz', 'gy')
- wave_second: float32 [128, 256, 512], P('gz', 'gy')
- adjoint_first: float32 [128, 256, 512], P('gz', 'gy')
- adjoint_second: float32 [128, 256, 512], P('gz', 'gy')
- gradient: float32 [128, 256, 512], P('gz', 'gy')
The draws below stay inside these ranges and needn't reach their ends.
Inputs may be any that keep to these rules, and one draw needn't show every extreme that they name: `receivers`: row 0 holds depth indices below 128, row 1 y indices below 256, row 2 x indices below 512. `sources`: row 0 holds depth indices below 128, row 1 y indices below 256, row 2 x indices below 512.
All inputs are finite; a program needn't handle non-finite values.
Results may differ from the reference program's by a relative error of at most 0.00015.
Values sent between devices are 32-bit elements; how exact they have to be, the bound alone decides.
No kernel may reach another device: no remote copies, remote signals or barrier semaphores. Data moves between devices by JAX's collectives and lax.ppermute only.
A program may use at most 64 MiB of HBM per device.

```python
import jax
import jax.numpy as jnp

CZ = 4
NX = 512
NSRC = 4
STEPS = 2
NZ = 128
NY = 256
R = 4096


def grid_points(key, count):
    keys = jax.random.split(key, 3)
    depth = jax.random.randint(keys[0], (count,), 0, NZ)
    across = jax.random.randint(keys[1], (count,), 0, NY)
    along = jax.random.randint(keys[2], (count,), 0, NX)
    points = jnp.stack([depth, across, along]).astype(jnp.int32)
    corner = jnp.array([NZ - 1, NY - 1, NX - 1], jnp.int32)
    points = points.at[:, 0].set(corner)
    points = points.at[:, 1].set(jnp.zeros((3,), jnp.int32))
    return points


def draw_receivers(key, part):
    key = jax.random.fold_in(key, 11)
    return grid_points(key, R)


def draw_sources(key, part):
    key = jax.random.fold_in(key, 23)
    return grid_points(key, NSRC)


def block_scale(rng, dims, cuts, smallest, high):
    gain = 1.0
    for dim, parts in cuts:
        steps = jax.random.uniform(jax.random.fold_in(jax.random.fold_in(rng, 6), dim), (parts,), jnp.float32, smallest / len(cuts), high / len(cuts))
        gain = gain * jnp.repeat(jnp.exp(steps), dims[dim] // parts).reshape((-1,) + (1,) * (len(dims) - 1 - dim))
    return gain


def normal_values(own_key, shape, deviation, most, cuts=(), kind=jnp.bfloat16):
    values = deviation * jax.random.normal(own_key, shape, jnp.float32)
    if cuts:
        values = values * block_scale(own_key, shape, cuts, -0.22, 0.18)
    return jnp.clip(values, -most, most).astype(kind)


def setup_inputs(seed: int = 0) -> dict:
    arg_keys = jax.random.split(jax.random.key(seed), 10)
    wave_now = normal_values(arg_keys[0], (NZ, NY, NX), 1.0, 6.0, ((0, 32), (1, 8)), jnp.float32)
    wave_later = normal_values(arg_keys[1], (NZ, NY, NX), 1.0, 6.0, ((0, 32), (1, 8)), jnp.float32)
    adjoint_now = normal_values(arg_keys[2], (NZ, NY, NX), 1.0, 6.0, ((0, 32), (1, 8)), jnp.float32)
    adjoint_later = normal_values(arg_keys[3], (NZ, NY, NX), 1.0, 6.0, ((0, 32), (1, 8)), jnp.float32)
    velocity = jnp.clip(1.5 + 3.0 * jax.random.uniform(arg_keys[4], (NZ, NY, NX), jnp.float32) ** block_scale(arg_keys[4], (NZ, NY, NX), ((0, 32), (1, 8)), -0.2, 0.2), 1.5, 4.5)
    observed = normal_values(arg_keys[5], (STEPS, R), 1.0, 6.0, ((1, 256),), jnp.float32)
    receivers = draw_receivers(jax.random.fold_in(arg_keys[9], 71), 0)
    sources = draw_sources(jax.random.fold_in(arg_keys[9], 71), 0)
    wavelet = normal_values(arg_keys[8], (STEPS, NSRC), 8.0, 40.0, (), jnp.float32)
    return {"wave_now": wave_now, "wave_later": wave_later, "adjoint_now": adjoint_now, "adjoint_later": adjoint_later, "velocity": velocity, "observed": observed, "receivers": receivers, "sources": sources, "wavelet": wavelet}


centre_coef = -7.5
near_coef = 4.0 / 3.0
far_coef = -1.0 / 12.0
time_ratio = 0.1
damp_peak = 0.3


def laplace(padded):
    centre = padded[..., 2:-2, 2:-2, :]
    widths = [(0, 0)] * (centre.ndim - 1) + [(2, 2)]
    x_padded = jnp.pad(centre, widths)
    near_sum = padded[..., 3:-1, 2:-2, :] + padded[..., 1:-3, 2:-2, :] + padded[..., 2:-2, 3:-1, :] + padded[..., 2:-2, 1:-3, :] + x_padded[..., 3:-1] + x_padded[..., 1:-3]
    far_sum = padded[..., 4:, 2:-2, :] + padded[..., :-4, 2:-2, :] + padded[..., 2:-2, 4:, :] + padded[..., 2:-2, :-4, :] + x_padded[..., 4:] + x_padded[..., :-4]
    return centre_coef * centre + near_coef * near_sum + far_coef * far_sum


def damping(z_index, z_total, sponge):
    z_float = jnp.clip(z_index, 0, z_total - 1).astype(jnp.float32)
    near_low = jnp.maximum(sponge - z_float, 0.0) / sponge
    near_high = jnp.maximum(z_float - (z_total - 1 - sponge), 0.0) / sponge
    return damp_peak * (near_low * near_low + near_high * near_high)


def update(wave_cur, adjoint_cur, wave_after, adjoint_after, lap_wave, lap_adjoint, speed_field, absorb, source, inject):
    courant = (speed_field * time_ratio) ** 2
    wave_before = (2.0 * wave_cur - (1.0 + absorb) * wave_after + courant * (lap_wave + source)) / (1.0 - absorb)
    adjoint_before = (2.0 * adjoint_cur - (1.0 - absorb) * adjoint_after + courant * lap_adjoint + inject) / (1.0 + absorb)
    grad_term = (2.0 / speed_field) * adjoint_cur * (wave_after - 2.0 * wave_cur + wave_before)
    return wave_before, adjoint_before, grad_term


def reference(wave_now, wave_later, adjoint_now, adjoint_later, velocity, observed, receivers, sources, wavelet):
    z_index = jnp.arange(NZ, dtype=jnp.int32)[:, None, None]
    absorb = damping(z_index, NZ, CZ)
    gradient = jnp.zeros(wave_now.shape, jnp.float32)
    wave_cur, wave_after = wave_now, wave_later
    adjoint_cur, adjoint_after = adjoint_now, adjoint_later
    for step_index in range(STEPS):
        predicted = wave_cur[receivers[0], receivers[1], receivers[2]]
        residual = predicted - observed[step_index]
        stacked = jnp.stack([wave_cur, adjoint_cur])
        wrapped = jnp.concatenate([stacked[:, :, -2:], stacked, stacked[:, :, :2]], axis=2)
        padded = jnp.pad(wrapped, ((0, 0), (2, 2), (0, 0), (0, 0)))
        lapped = laplace(padded)
        empty_grid = jnp.zeros(wave_now.shape, jnp.float32)
        source = empty_grid.at[sources[0], sources[1], sources[2]].add(wavelet[step_index])
        inject = empty_grid.at[receivers[0], receivers[1], receivers[2]].add(residual)
        wave_before, adjoint_before, grad_term = update(wave_cur, adjoint_cur, wave_after, adjoint_after, lapped[0], lapped[1], velocity, absorb, source, inject)
        gradient = gradient + grad_term
        wave_after, wave_cur = wave_cur, wave_before
        adjoint_after, adjoint_cur = adjoint_cur, adjoint_before
    return wave_cur, wave_after, adjoint_cur, adjoint_after, gradient
```

```python
import jax
import jax.numpy as jnp
import numpy as np
from jax import lax
from jax.experimental import pallas as pl
from jax.experimental.pallas import tpu as pltpu
from jax.sharding import Mesh
from jax.sharding import PartitionSpec as P

CENTRE = -7.5
NEAR = 4.0 / 3.0
FAR = -1.0 / 12.0
RATIO = 0.1
DAMP = 0.3

GZ = ("yl", "z", "c")
GY = ("x", "yh")
O = 16
NZ_DEV, NY_DEV = 32, 8
CZ, CY, NX = 4, 32, 512
NZ, NY = NZ_DEV * CZ, NY_DEV * CY
FR = CY + 2 * O
VMEM_LIMIT = 48 * 1024 * 1024
ZROWS = 5 * CY + 8


def coefficient_table():
    z = np.clip(np.arange(-2, NZ + 2), 0, NZ - 1).astype(np.float32)
    low = np.maximum(np.float32(CZ) - z, np.float32(0)) / np.float32(CZ)
    high = np.maximum(z - np.float32(NZ - 1 - CZ), np.float32(0)) / np.float32(CZ)
    a = np.float32(DAMP) * (low * low + high * high)
    one = np.float32(1)
    return np.stack([one + a, one - a, one / (one - a), one / (one + a)]).astype(np.float32)


def smem():
    return pl.BlockSpec(memory_space=pltpu.SMEM)


def vmem():
    return pl.BlockSpec(memory_space=pltpu.VMEM)


def x_terms(u):
    lane = lax.broadcasted_iota(jnp.int32, u.shape, 1)
    a = jnp.where(lane >= 1, pltpu.roll(u, 1, 1), 0.0)
    b = jnp.where(lane < NX - 1, pltpu.roll(u, NX - 1, 1), 0.0)
    c = jnp.where(lane >= 2, pltpu.roll(u, 2, 1), 0.0)
    d = jnp.where(lane < NX - 2, pltpu.roll(u, NX - 2, 1), 0.0)
    return a + b, c + d


def laplace(f, k, s):
    rows = lambda layer, shift: f[layer, s + shift : s + shift + 8, :]
    u = rows(k, 0)
    near, far = x_terms(u)
    near = near + ((rows(k, -1) + rows(k, 1)) + (rows(k - 1, 0) + rows(k + 1, 0)))
    far = far + ((rows(k, -2) + rows(k, 2)) + (rows(k - 2, 0) + rows(k + 2, 0)))
    return u, CENTRE * u + NEAR * near + FAR * far


def pack_y(meta, u, a, u1, a1, v, h, g):
    def pack(dst, high):
        four = slice(CY - 4, CY) if high else slice(0, 4)
        two = slice(CY - 2, CY) if high else slice(0, 2)
        dst[:, 0:4, :] = u[:, four, :]
        dst[:, 4:8, :] = a[:, four, :]
        dst[:, 8:10, :] = u1[:, two, :]
        dst[:, 10:12, :] = a1[:, two, :]
        dst[:, 12:14, :] = v[:, two, :]
        dst[:, 14:16, :] = v[:, two, :]

    @pl.when(meta[2] == 0)
    def _():
        pack(h, True)
        pack(g, False)

    @pl.when(meta[2] != 0)
    def _():
        pack(h, False)
        pack(g, True)


def fill_y(meta, rh, rg, low, high):
    @pl.when(meta[2] == 0)
    def _():
        high(rh)
        low(rg)

    @pl.when(meta[2] != 0)
    def _():
        low(rh)
        high(rg)


def local_step(meta, coef, u, a, u1, a1, v, rh, rg, u0p, a0p, zc, zb, uf, af, u1f, a1f, vf):
    for f, own in ((uf, u), (af, a)):
        f[2:6, O : O + CY, :] = own[...]
        for k in (0, 1, 6, 7):
            f[k, :, :] = jnp.zeros((FR, NX), jnp.float32)
    for f, own in ((u1f, u1), (a1f, a1), (vf, v)):
        f[:, O : O + CY, :] = own[...]

    def low(r):
        uf[2:6, O - 4 : O, :] = r[:, 0:4, :]
        af[2:6, O - 4 : O, :] = r[:, 4:8, :]
        u1f[:, O - 2 : O, :] = r[:, 8:10, :]
        a1f[:, O - 2 : O, :] = r[:, 10:12, :]
        vf[:, O - 2 : O, :] = r[:, 12:14, :]

    def high(r):
        e = O + CY
        uf[2:6, e : e + 4, :] = r[:, 0:4, :]
        af[2:6, e : e + 4, :] = r[:, 4:8, :]
        u1f[:, e : e + 2, :] = r[:, 8:10, :]
        a1f[:, e : e + 2, :] = r[:, 10:12, :]
        vf[:, e : e + 2, :] = r[:, 12:14, :]

    fill_y(meta, rh, rg, low, high)
    z0 = meta[0]

    def layer(l, carry):
        i = z0 + l + 2
        up, dn, iu, ia = coef[0, i], coef[1, i], coef[2, i], coef[3, i]
        for s in range(O - 8, O + CY + 8, 8):
            c = vf[l, s : s + 8, :] * RATIO
            c = c * c
            u, lu = laplace(uf, l + 2, s)
            u0p[l, s : s + 8, :] = (2.0 * u - up * u1f[l, s : s + 8, :] + c * lu) * iu
            w, lw = laplace(af, l + 2, s)
            a0p[l, s : s + 8, :] = (2.0 * w - dn * a1f[l, s : s + 8, :] + c * lw) * ia
        return carry

    lax.fori_loop(0, CZ, layer, 0)

    def pack(dst, l):
        e = O + CY
        own = (uf, l + 2, u0p, l), (af, l + 2, a0p, l)
        dst[:, 0:CY, :] = uf[l + 2 : l + 4, O:e, :]
        dst[:, CY : 2 * CY, :] = af[l + 2 : l + 4, O:e, :]
        dst[:, 2 * CY : 3 * CY, :] = u0p[l : l + 2, O:e, :]
        dst[:, 3 * CY : 4 * CY, :] = a0p[l : l + 2, O:e, :]
        dst[:, 4 * CY : 5 * CY, :] = vf[l : l + 2, O:e, :]
        b = 5 * CY
        dst[:, b : b + 2, :] = uf[l + 2 : l + 4, O - 2 : O, :]
        dst[:, b + 2 : b + 4, :] = uf[l + 2 : l + 4, e : e + 2, :]
        dst[:, b + 4 : b + 6, :] = af[l + 2 : l + 4, O - 2 : O, :]
        dst[:, b + 6 : b + 8, :] = af[l + 2 : l + 4, e : e + 2, :]

    @pl.when(meta[3] == 0)
    def _():
        pack(zc, 2)
        pack(zb, 0)

    @pl.when(meta[3] != 0)
    def _():
        pack(zc, 0)
        pack(zb, 2)


def list_receivers(meta, rec, out, bits, words_v, words, sem):
    z0, y0 = meta[0], meta[1]
    lz = rec[0:1, :] - z0
    ly = ((rec[1:2, :] - y0 + O) & (NY - 1)) - O
    own_z = (lz >= 0) & (lz < CZ)
    own_y = (ly >= 0) & (ly < CY)
    near = (lz >= -2) & (lz < CZ + 2) & (ly >= -2) & (ly < CY + 2) & (own_z | own_y)
    m = near.astype(jnp.int32)
    for i in range(32):
        bits[i : i + 1, :] = m[:, 128 * i : 128 * i + 128] << i
    words_v[...] = jnp.sum(bits[...], axis=0, keepdims=True)
    copy = pltpu.make_async_copy(words_v, words, sem)
    copy.start()
    copy.wait()

    def word_step(w, count):
        def bit_step(carry):
            word, count = carry
            low = word & (-word)
            out[0, count + 1] = (31 - lax.clz(low)) * 128 + w
            return word ^ low, count + 1

        return lax.while_loop(lambda carry: carry[0] != 0, bit_step, (words[0, w], count))[1]

    out[0, 0] = lax.fori_loop(0, 128, word_step, 0)


def last_step(
    meta, coef, u, a, u1, a1, v, rh, rg, u0p, a0p, rc, rb, found, rec, table, src, amp,
    u2, u0o, a2, a0o, grad,
    uf, af, vf, u0f, a0f,
):
    e = O + CY
    z0, y0 = meta[0], meta[1]
    uf[2:6, O:e, :] = u[...]
    vf[2:6, O:e, :] = v[...]

    def low(r):
        uf[2:6, O - 2 : O, :] = r[:, 2:4, :]
        vf[2:6, O - 2 : O, :] = r[:, 12:14, :]

    def high(r):
        uf[2:6, e : e + 2, :] = r[:, 0:2, :]
        vf[2:6, e : e + 2, :] = r[:, 12:14, :]

    fill_y(meta, rh, rg, low, high)

    def fill_z(r, k):
        b = 5 * CY
        uf[k : k + 2, O:e, :] = r[:, 0:CY, :]
        af[k : k + 2, O:e, :] = r[:, CY : 2 * CY, :]
        u0f[k : k + 2, O:e, :] = r[:, 2 * CY : 3 * CY, :]
        a0f[k : k + 2, O:e, :] = r[:, 3 * CY : 4 * CY, :]
        vf[k : k + 2, O:e, :] = r[:, 4 * CY : 5 * CY, :]
        uf[k : k + 2, O - 2 : O, :] = r[:, b : b + 2, :]
        uf[k : k + 2, e : e + 2, :] = r[:, b + 2 : b + 4, :]
        af[k : k + 2, O - 2 : O, :] = r[:, b + 4 : b + 6, :]
        af[k : k + 2, e : e + 2, :] = r[:, b + 6 : b + 8, :]

    @pl.when(meta[3] == 0)
    def _():
        fill_z(rb, 0)
        fill_z(rc, 6)

    @pl.when(meta[3] != 0)
    def _():
        fill_z(rc, 0)
        fill_z(rb, 6)

    lacks = ((0, None, 2), (1, 2, 3), (2, 1, 0), (3, None, 1), (4, None, 6), (5, 6, 7), (6, 5, 4), (7, None, 5))
    for k, near, far in lacks:
        own = 2 <= k < 6
        iu, ia = coef[2, z0 + k], coef[3, z0 + k]

        def term(f, layer, s):
            if 2 <= layer < 6 and f is af:
                return a[layer - 2, pl.ds(s - O, 8), :]
            return f[layer, pl.ds(s, 8), :]

        def rows(t, carry):
            s = pl.multiple_of(t * 8, 8)
            c = vf[k, pl.ds(s, 8), :] * RATIO
            c = c * c
            for f, f0, p, scale in ((uf, u0f, u0p, iu), (af, a0f, a0p, ia)):
                lap = FAR * term(f, far, s)
                if near is not None:
                    lap = lap + NEAR * term(f, near, s)
                base = p[k - 2, pl.ds(s, 8), :] if own else f0[k, pl.ds(s, 8), :]
                f0[k, pl.ds(s, 8), :] = base + (c * scale) * lap
            return carry

        first = O // 8
        lax.fori_loop(first - own, first + CY // 8 + own, rows, 0)

    place = lax.broadcasted_iota(jnp.int32, (8, 128), 0) * 128 + lax.broadcasted_iota(jnp.int32, (8, 128), 1)

    def cell(z, y, x):
        lz = z - z0
        ly = ((y - y0 + O) & (NY - 1)) - O
        rows = (ly >> 3) << 3
        cols = pl.ds(pl.multiple_of((x >> 7) << 7, 128), 128)
        return lz, ly, rows, cols, place == ((ly & 7) * 128 + (x & 127))

    def add_source_0(i, carry):
        lz, ly, rows, cols, hit = cell(src[0, i], src[1, i], src[2, i])
        own_z = (lz >= 0) & (lz < CZ)
        own_y = (ly >= 0) & (ly < CY)
        near = (lz >= -2) & (lz < CZ + 2) & (ly >= -2) & (ly < CY + 2) & (own_z | own_y)

        @pl.when(near)
        def _():
            at = (lz + 2, pl.ds(pl.multiple_of(rows + O, 8), 8), cols)
            c = vf[at] * RATIO
            u0f[at] = u0f[at] + jnp.where(hit, (c * c) * (amp[0, i] * coef[2, z0 + lz + 2]), 0.0)

        return carry

    lax.fori_loop(0, src.shape[1], add_source_0, 0)

    def observed(step, r):
        return table[(r >> 7) * 2 + ((r >> 4) & 1), ((r >> 5) & 3) * 32 + step * 16 + (r & 15)]

    def add_receiver_0(n, carry):
        r = found[0, n + 1]
        lz, ly, rows, cols, hit = cell(rec[0, r], rec[1, r], rec[2, r])
        at = (lz + 2, pl.ds(pl.multiple_of(rows + O, 8), 8), cols)
        residual = (uf[at] - observed(0, r)) * coef[3, z0 + lz + 2]
        a0f[at] = a0f[at] + jnp.where(hit, residual, 0.0)
        return carry

    count = found[0, 0]
    lax.fori_loop(0, count, add_receiver_0, 0)

    def layer(l, carry):
        i = z0 + l + 2
        up, dn, iu, ia = coef[0, i], coef[1, i], coef[2, i], coef[3, i]
        for s in range(O, O + CY, 8):
            y = slice(s - O, s - O + 8)
            vel = v[l, y, :]
            c = vel * RATIO
            c = c * c
            un, an = u[l, y, :], a[l, y, :]
            q, lu = laplace(u0f, l + 2, s)
            new = (2.0 * q - up * un + c * lu) * iu
            u2[l, y, :] = new
            u0o[l, y, :] = q
            w, lw = laplace(a0f, l + 2, s)
            a2[l, y, :] = (2.0 * w - dn * an + c * lw) * ia
            a0o[l, y, :] = w
            grad[l, y, :] = (2.0 / vel) * (an * (u1[l, y, :] - 2.0 * un + q) + w * (un - 2.0 * q + new))
        return carry

    lax.fori_loop(0, CZ, layer, 0)

    def add_source_1(i, carry):
        lz, ly, rows, cols, hit = cell(src[0, i], src[1, i], src[2, i])

        @pl.when((lz >= 0) & (lz < CZ) & (ly >= 0) & (ly < CY))
        def _():
            at = (lz, pl.ds(pl.multiple_of(rows, 8), 8), cols)
            vel = v[at]
            c = vel * RATIO
            added = jnp.where(hit, (c * c) * (amp[1, i] * coef[2, z0 + lz + 2]), 0.0)
            u2[at] = u2[at] + added
            grad[at] = grad[at] + (2.0 / vel) * a0o[at] * added

        return carry

    lax.fori_loop(0, src.shape[1], add_source_1, 0)

    def add_receiver_1(n, carry):
        r = found[0, n + 1]
        lz, ly, rows, cols, hit = cell(rec[0, r], rec[1, r], rec[2, r])

        @pl.when((lz >= 0) & (lz < CZ) & (ly >= 0) & (ly < CY))
        def _():
            at = (lz, pl.ds(pl.multiple_of(rows, 8), 8), cols)
            residual = (u0o[at] - observed(1, r)) * coef[3, z0 + lz + 2]
            a2[at] = a2[at] + jnp.where(hit, residual, 0.0)

        return carry

    lax.fori_loop(0, count, add_receiver_1, 0)


def f32(*shape):
    return jax.ShapeDtypeStruct(shape, jnp.float32)


def params():
    return pltpu.CompilerParams(vmem_limit_bytes=VMEM_LIMIT)


def swap(value, axis, size, first):
    pairs = [(i, (first + ((i - first) % size ^ 1)) % size) for i in range(size)]
    return lax.ppermute(value, axis, pairs)


def swap_open(value, axis, size):
    pairs = [(i, i + 1) for i in range(1, size - 1, 2)]
    return lax.ppermute(value, axis, pairs + [(j, i) for i, j in pairs])


def shards(u, u1, a, a1, v, obs, rec, src, amp):
    assert u.shape == (CZ, CY, NX)
    gz, gy = lax.axis_index(GZ), lax.axis_index(GY)
    x, yh, core = lax.axis_index("x"), lax.axis_index("yh"), lax.axis_index("c")
    meta = jnp.stack([gz * CZ, gy * CY, yh, core]).astype(jnp.int32)
    coef = jnp.asarray(coefficient_table())

    lanes = jnp.arange(128, dtype=jnp.int32) // 32
    mine = jnp.where(lanes == x, jnp.tile(obs.reshape(32), 4), 0.0)[None]
    mine = mine + swap(mine, "x", 4, 0)
    mine = mine + swap(mine, "x", 4, 1)

    pack = f32(CZ, 16, NX)
    h, g = pl.pallas_call(
        pack_y,
        out_shape=(pack, pack),
        in_specs=[smem()] + [vmem()] * 5,
        out_specs=(vmem(), vmem()),
        compiler_params=params(),
        name="pack_y",
    )(meta, u, a, u1, a1, v)
    rh = swap(h, GY, NY_DEV, 0)
    rg = swap(g, GY, NY_DEV, 1)

    frame, zpack = f32(CZ, FR, NX), f32(2, ZROWS, NX)
    full = pltpu.VMEM((8, FR, NX), jnp.float32)
    part = pltpu.VMEM((CZ, FR, NX), jnp.float32)
    u0p, a0p, zc, zb = pl.pallas_call(
        local_step,
        out_shape=(frame, frame, zpack, zpack),
        in_specs=[smem()] * 2 + [vmem()] * 7,
        out_specs=(vmem(),) * 4,
        scratch_shapes=[full, full, part, part, part],
        compiler_params=params(),
        name="local_step",
    )(meta, coef, u, a, u1, a1, v, rh, rg)

    rc = swap(zc, GZ, NZ_DEV, 0)
    rb = swap_open(zb, GZ, NZ_DEV)

    found = pl.pallas_call(
        list_receivers,
        out_shape=jax.ShapeDtypeStruct((1, rec.shape[1] + 128), jnp.int32),
        in_specs=[smem(), vmem()],
        out_specs=smem(),
        scratch_shapes=[
            pltpu.VMEM((32, 128), jnp.int32),
            pltpu.VMEM((1, 128), jnp.int32),
            pltpu.SMEM((1, 128), jnp.int32),
            pltpu.SemaphoreType.DMA,
        ],
        compiler_params=params(),
        name="list_receivers",
    )(meta, rec)

    table = lax.all_to_all(jnp.broadcast_to(mine, (64, 128)), ("yl", "z", "c", "yh"), 0, 0, tiled=True)

    block = f32(CZ, CY, NX)
    return pl.pallas_call(
        last_step,
        out_shape=(block,) * 5,
        in_specs=[smem()] * 2 + [vmem()] * 11 + [smem()] * 5,
        out_specs=(vmem(),) * 5,
        scratch_shapes=[full] * 5,
        compiler_params=params(),
        name="last_step",
    )(meta, coef, u, a, u1, a1, v, rh, rg, u0p, a0p, rc, rb, found, rec, table, src, amp)


def solution(mesh):
    fine = Mesh(mesh.devices.reshape(2, 8, 2, 4, 2), ("yl", "z", "c", "x", "yh"))
    field = P(GZ, GY, None)
    return jax.shard_map(
        shards,
        mesh=fine,
        in_specs=(field,) * 5 + (P(None, GZ + GY), P(), P(), P()),
        out_specs=(field,) * 5,
        check_vma=False,
    )
```

```python
import jax
import jax.numpy as jnp
import numpy as np
from jax import lax
from jax.experimental import pallas as pl
from jax.experimental.pallas import tpu as pltpu
from jax.sharding import Mesh
from jax.sharding import PartitionSpec as P

CENTRE = -7.5
NEAR = 4.0 / 3.0
FAR = -1.0 / 12.0
RATIO = 0.1
DAMP = 0.3

GZ = ("yl", "z", "c")
GY = ("xh", "xl", "yh")
O = 8
NZ_DEV, NY_DEV = 32, 8
CZ, CY, NX = 4, 32, 512
NZ, NY = NZ_DEV * CZ, NY_DEV * CY
FR = CY + 2 * O
VMEM_LIMIT = 16 * 1024 * 1024
ZROWS = 5 * CY + 8


def coefficient_table():
    z = np.clip(np.arange(-2, NZ + 2), 0, NZ - 1).astype(np.float32)
    low = np.maximum(np.float32(CZ) - z, np.float32(0)) / np.float32(CZ)
    high = np.maximum(z - np.float32(NZ - 1 - CZ), np.float32(0)) / np.float32(CZ)
    a = np.float32(DAMP) * (low * low + high * high)
    one = np.float32(1)
    return np.stack([one + a, one - a, one / (one - a), one / (one + a)]).astype(np.float32)


def smem():
    return pl.BlockSpec(memory_space=pltpu.SMEM)


def vmem():
    return pl.BlockSpec(memory_space=pltpu.VMEM)


def x_terms(u):
    lane = lax.broadcasted_iota(jnp.int32, u.shape, 1)
    a = jnp.where(lane >= 1, pltpu.roll(u, 1, 1), 0.0)
    b = jnp.where(lane < NX - 1, pltpu.roll(u, NX - 1, 1), 0.0)
    c = jnp.where(lane >= 2, pltpu.roll(u, 2, 1), 0.0)
    d = jnp.where(lane < NX - 2, pltpu.roll(u, NX - 2, 1), 0.0)
    return a + b, c + d


def laplace(f, k, s):
    rows = lambda layer, shift: f[layer, s + shift : s + shift + 8, :]
    u = rows(k, 0)
    near, far = x_terms(u)
    near = near + ((rows(k, -1) + rows(k, 1)) + (rows(k - 1, 0) + rows(k + 1, 0)))
    far = far + ((rows(k, -2) + rows(k, 2)) + (rows(k - 2, 0) + rows(k + 2, 0)))
    return u, CENTRE * u + NEAR * near + FAR * far


def depth_factors(l):
    near_up = jnp.where(l >= 1, jnp.float32(NEAR), jnp.float32(0.0))
    near_dn = jnp.where(l < CZ - 1, jnp.float32(NEAR), jnp.float32(0.0))
    far_up = jnp.where(l >= 2, jnp.float32(FAR), jnp.float32(0.0))
    far_dn = jnp.where(l < CZ - 2, jnp.float32(FAR), jnp.float32(0.0))
    layers = jnp.maximum(l - 1, 0), jnp.minimum(l + 1, CZ - 1), jnp.maximum(l - 2, 0), jnp.minimum(l + 2, CZ - 1)
    return tuple(zip(layers, (near_up, near_dn, far_up, far_dn)))


def partial_laplace(f, l, s, size, factors):
    u = f[l, s : s + 8, :]

    def shifted(shift):
        if 0 <= s + shift and s + shift + 8 <= size:
            return f[l, s + shift : s + shift + 8, :]
        return pltpu.roll(u, (-shift) % 8, 0)

    near, far = x_terms(u)
    lap = CENTRE * u + NEAR * (near + (shifted(-1) + shifted(1))) + FAR * (far + (shifted(-2) + shifted(2)))
    for layer, factor in factors:
        lap = lap + factor * f[layer, s : s + 8, :]
    return u, lap


def pack_y(meta, u, a, u1, a1, v, obs, h, g, own, first, last, obs_v, row, sem):
    copies = []
    for i, ref in enumerate((u, a, u1, a1, v)):
        copies.append(pltpu.make_async_copy(ref.at[:, 0:8, :], first.at[i], sem.at[2 * i]))
        copies.append(pltpu.make_async_copy(ref.at[:, CY - 8 : CY, :], last.at[i], sem.at[2 * i + 1]))
    copies.append(pltpu.make_async_copy(obs, obs_v, sem.at[10]))
    for copy in copies:
        copy.start()
    for copy in copies:
        copy.wait()
    for k in range(4):
        for t in range(2):
            row[0:1, 32 * k + 16 * t : 32 * k + 16 * t + 16] = obs_v[t : t + 1, :]
    lane = lax.broadcasted_iota(jnp.int32, (1, 128), 1)
    mine = jnp.where((lane >> 5) == meta[4] * 2 + meta[2], row[0:1, :], 0.0)
    own[...] = mine

    def pack(dst, high):
        rows = last if high else first
        four = slice(4, 8) if high else slice(0, 4)
        two = slice(6, 8) if high else slice(0, 2)
        dst[:, 0:4, :] = rows[0, :, four, :]
        dst[:, 4:8, :] = rows[1, :, four, :]
        dst[:, 8:10, :] = rows[2, :, two, :]
        dst[:, 10:12, :] = rows[3, :, two, :]
        dst[:, 12:14, :] = rows[4, :, two, :]
        dst[:, 14:16, :] = jnp.zeros((CZ, 2, NX), jnp.float32)
        dst[0, 14:15, 0:128] = mine

    @pl.when(meta[2] == 0)
    def _():
        pack(h, True)
        pack(g, False)

    @pl.when(meta[2] != 0)
    def _():
        pack(h, False)
        pack(g, True)


def pick_y(meta, rh, rg, low, high):
    @pl.when(meta[2] == 0)
    def _():
        high(rh)
        low(rg)

    @pl.when(meta[2] != 0)
    def _():
        low(rh)
        high(rg)


def own_step(meta, coef, u, a, u1, a1, v, u0p, a0p):
    z0 = meta[0]

    def layer(l, carry):
        i = z0 + l + 2
        up, dn, iu, ia = coef[0, i], coef[1, i], coef[2, i], coef[3, i]
        factors = depth_factors(l)
        for s in range(0, CY, 8):
            y = slice(s, s + 8)
            c = v[l, y, :] * RATIO
            c = c * c
            p, lap = partial_laplace(u, l, s, CY, factors)
            u0p[l, y, :] = (2.0 * p - up * u1[l, y, :] + c * lap) * iu
            q, lap = partial_laplace(a, l, s, CY, factors)
            a0p[l, y, :] = (2.0 * q - dn * a1[l, y, :] + c * lap) * ia
        return carry

    lax.fori_loop(0, CZ, layer, 0)


def edge_step(
    meta, coef, u, a, u1, a1, v, rh, rg, own, u0p, a0p, ulo, uhi, alo, ahi, zc, zb, traces,
    pu, pa, pu1, pa1, pv,
):
    z0 = meta[0]
    pu[0, :, 4:8, :] = u[:, 0:4, :]
    pu[1, :, 0:4, :] = u[:, CY - 4 : CY, :]
    pa[0, :, 4:8, :] = a[:, 0:4, :]
    pa[1, :, 0:4, :] = a[:, CY - 4 : CY, :]
    for part, block in ((pu1, u1), (pa1, a1), (pv, v)):
        part[0, :, 4:6, :] = block[:, 0:2, :]
        part[1, :, 2:4, :] = block[:, CY - 2 : CY, :]

    def low(r):
        pu[0, :, 0:4, :] = r[:, 0:4, :]
        pa[0, :, 0:4, :] = r[:, 4:8, :]
        pu1[0, :, 2:4, :] = r[:, 8:10, :]
        pa1[0, :, 2:4, :] = r[:, 10:12, :]
        pv[0, :, 2:4, :] = r[:, 12:14, :]

    def high(r):
        pu[1, :, 4:8, :] = r[:, 0:4, :]
        pa[1, :, 4:8, :] = r[:, 4:8, :]
        pu1[1, :, 4:6, :] = r[:, 8:10, :]
        pa1[1, :, 4:6, :] = r[:, 10:12, :]
        pv[1, :, 4:6, :] = r[:, 12:14, :]

    pick_y(meta, rh, rg, low, high)

    def layer(l, carry):
        i = z0 + l + 2
        up, dn, iu, ia = coef[0, i], coef[1, i], coef[2, i], coef[3, i]
        factors = depth_factors(l)
        for side, uo, ao in ((0, ulo, alo), (1, uhi, ahi)):
            c = pv[side, l] * RATIO
            c = c * c
            p, lap = partial_laplace(pu.at[side], l, 0, 8, factors)
            uo[l] = (2.0 * p - up * pu1[side, l] + c * lap) * iu
            q, lap = partial_laplace(pa.at[side], l, 0, 8, factors)
            ao[l] = (2.0 * q - dn * pa1[side, l] + c * lap) * ia
        return carry

    lax.fori_loop(0, CZ, layer, 0)

    def pack(dst, l):
        m = slice(l, l + 2)
        dst[:, 0:CY, :] = u[m]
        dst[:, CY : 2 * CY, :] = a[m]
        dst[:, 4 * CY : 5 * CY, :] = v[m]
        for b, p, lo, hi in ((2 * CY, u0p, ulo, uhi), (3 * CY, a0p, alo, ahi)):
            dst[:, b : b + CY, :] = p[m]
            dst[:, b : b + 2, :] = lo[m, 4:6, :]
            dst[:, b + CY - 2 : b + CY, :] = hi[m, 2:4, :]
        b = 5 * CY
        dst[:, b : b + 2, :] = pu[0, m, 2:4, :]
        dst[:, b + 2 : b + 4, :] = pu[1, m, 4:6, :]
        dst[:, b + 4 : b + 6, :] = pa[0, m, 2:4, :]
        dst[:, b + 6 : b + 8, :] = pa[1, m, 4:6, :]

    @pl.when(meta[3] == 0)
    def _():
        pack(zc, 2)
        pack(zb, 0)

    @pl.when(meta[3] != 0)
    def _():
        pack(zc, 0)
        pack(zb, 2)

    mine = rg[0, 14:15, 0:128] + rg[0, 15:16, 0:128] + rh[0, 14:15, 0:128] + own[...]
    traces[...] = jnp.broadcast_to(mine, traces.shape)


def list_receivers(meta, rec, rec_s, out, bits, words_v, words, sem):
    z0, y0 = meta[0], meta[1]
    lz = rec[0:1, :] - z0
    ly = ((rec[1:2, :] - y0 + 16) & (NY - 1)) - 16
    own_z = (lz >= 0) & (lz < CZ)
    own_y = (ly >= 0) & (ly < CY)
    near = (lz >= -2) & (lz < CZ + 2) & (ly >= -2) & (ly < CY + 2) & (own_z | own_y)
    m = near.astype(jnp.int32)
    for i in range(32):
        bits[i : i + 1, :] = m[:, 128 * i : 128 * i + 128] << i
    words_v[...] = jnp.sum(bits[...], axis=0, keepdims=True)
    copy = pltpu.make_async_copy(words_v, words, sem)
    copy.start()
    copy.wait()

    def word_step(w, count):
        def bit_step(carry):
            word, count = carry
            low = word & (-word)
            r = (31 - lax.clz(low)) * 128 + w
            z = rec_s[0, r] - z0 + 2
            y = (rec_s[1, r] - y0 + 2) & (NY - 1)
            out[0, count + 1] = r | (rec_s[2, r] << 12) | (y << 21) | (z << 27)
            return word ^ low, count + 1

        return lax.while_loop(lambda carry: carry[0] != 0, bit_step, (words[0, w], count))[1]

    out[0, 0] = lax.fori_loop(0, 128, word_step, 0)


def cell_place():
    return lax.broadcasted_iota(jnp.int32, (8, 128), 0) * 128 + lax.broadcasted_iota(jnp.int32, (8, 128), 1)


def cell_at(place, layer, row, x):
    rows = pl.ds(pl.multiple_of((row >> 3) << 3, 8), 8)
    cols = pl.ds(pl.multiple_of((x >> 7) << 7, 128), 128)
    return (layer, rows, cols), place == ((row & 7) * 128 + (x & 127))


def wave_step(
    meta, coef, u, a, u1, v, rh, rg, u0p, a0p, ulo, uhi, alo, ahi, rc, rb, src, amp,
    u2, u0o, w, gp, uf, u0f, a0f,
    af, vf,
):
    e = O + CY
    z0, y0 = meta[0], meta[1]
    uf[2:6, O:e, :] = u[...]
    vf[2:6, O:e, :] = v[...]
    u0f[2:6, O:e, :] = u0p[...]
    a0f[2:6, O:e, :] = a0p[...]
    for f0, lo, hi in ((u0f, ulo, uhi), (a0f, alo, ahi)):
        f0[2:6, O - 2 : O + 2, :] = lo[:, 2:6, :]
        f0[2:6, e - 2 : e + 2, :] = hi[:, 2:6, :]

    def low(r):
        uf[2:6, O - 2 : O, :] = r[:, 2:4, :]
        vf[2:6, O - 2 : O, :] = r[:, 12:14, :]

    def high(r):
        uf[2:6, e : e + 2, :] = r[:, 0:2, :]
        vf[2:6, e : e + 2, :] = r[:, 12:14, :]

    pick_y(meta, rh, rg, low, high)

    def fill_z(r, k):
        b = 5 * CY
        m = slice(k, k + 2)
        uf[m, O:e, :] = r[:, 0:CY, :]
        af[m, O:e, :] = r[:, CY : 2 * CY, :]
        u0f[m, O:e, :] = r[:, 2 * CY : 3 * CY, :]
        a0f[m, O:e, :] = r[:, 3 * CY : 4 * CY, :]
        vf[m, O:e, :] = r[:, 4 * CY : 5 * CY, :]
        uf[m, O - 2 : O, :] = r[:, b : b + 2, :]
        uf[m, e : e + 2, :] = r[:, b + 2 : b + 4, :]
        af[m, O - 2 : O, :] = r[:, b + 4 : b + 6, :]
        af[m, e : e + 2, :] = r[:, b + 6 : b + 8, :]

    @pl.when(meta[3] == 0)
    def _():
        fill_z(rb, 0)
        fill_z(rc, 6)

    @pl.when(meta[3] != 0)
    def _():
        fill_z(rc, 0)
        fill_z(rb, 6)

    lacks = ((0, None, 2), (1, 2, 3), (2, 1, 0), (3, None, 1), (4, None, 6), (5, 6, 7), (6, 5, 4), (7, None, 5))
    for k, near, far in lacks:
        edge = 2 <= k < 6
        iu, ia = coef[2, z0 + k], coef[3, z0 + k]

        def rows(t, carry):
            s = pl.multiple_of(t * 8, 8)
            c = vf[k, pl.ds(s, 8), :] * RATIO
            c = c * c
            for f, own, f0, scale in ((uf, u, u0f, iu), (af, a, a0f, ia)):
                term = lambda j: own[j - 2, pl.ds(s - O, 8), :] if 2 <= j < 6 else f[j, pl.ds(s, 8), :]
                lap = FAR * term(far)
                if near is not None:
                    lap = lap + NEAR * term(near)
                f0[k, pl.ds(s, 8), :] = f0[k, pl.ds(s, 8), :] + (c * scale) * lap
            return carry

        first = O // 8
        lax.fori_loop(first - edge, first + CY // 8 + edge, rows, 0)

    place = cell_place()

    def source_cell(i):
        return src[0, i] - z0, ((src[1, i] - y0 + 16) & (NY - 1)) - 16, src[2, i]

    def add_source_0(i, carry):
        lz, ly, x = source_cell(i)
        own_z = (lz >= 0) & (lz < CZ)
        own_y = (ly >= 0) & (ly < CY)
        near = (lz >= -2) & (lz < CZ + 2) & (ly >= -2) & (ly < CY + 2) & (own_z | own_y)

        @pl.when(near)
        def _():
            at, hit = cell_at(place, lz + 2, ly + O, x)
            c = vf[at] * RATIO
            u0f[at] = u0f[at] + jnp.where(hit, (c * c) * (amp[0, i] * coef[2, z0 + lz + 2]), 0.0)

        return carry

    lax.fori_loop(0, src.shape[1], add_source_0, 0)

    def layer(l, carry):
        i = z0 + l + 2
        up, iu = coef[0, i], coef[2, i]
        for s in range(O, O + CY, 8):
            y = slice(s - O, s - O + 8)
            vel = v[l, y, :]
            c = vel * RATIO
            c = c * c
            un = u[l, y, :]
            q, lap = laplace(u0f, l + 2, s)
            new = (2.0 * q - up * un + c * lap) * iu
            u2[l, y, :] = new
            u0o[l, y, :] = q
            slow = 2.0 / vel
            w[l, y, :] = slow * (un - 2.0 * q + new)
            gp[l, y, :] = slow * a[l, y, :] * (u1[l, y, :] - 2.0 * un + q)
        return carry

    lax.fori_loop(0, CZ, layer, 0)

    def add_source_1(i, carry):
        lz, ly, x = source_cell(i)

        @pl.when((lz >= 0) & (lz < CZ) & (ly >= 0) & (ly < CY))
        def _():
            at, hit = cell_at(place, lz, ly, x)
            vel = v[at]
            c = vel * RATIO
            added = jnp.where(hit, (c * c) * (amp[1, i] * coef[2, z0 + lz + 2]), 0.0)
            u2[at] = u2[at] + added
            w[at] = w[at] + (2.0 / vel) * added

        return carry

    lax.fori_loop(0, src.shape[1], add_source_1, 0)


def adjoint_step(meta, coef, a, v, uf, u0f, a0p, w, gp, found, table, a2, a0o, grad, a0f):
    z0, yh, xl = meta[0], meta[2], meta[4]
    for k in range(8):
        a0f[k] = a0p[k]
    place = cell_place()
    turn = 1 - 2 * yh

    def observed(step, r):
        x = (r >> 5) & 3
        sender = (x + turn * ((x ^ xl) & 1)) & 3
        return table[(r >> 7) * 2 + (sender >> 1), ((x & 1) * 2 + ((r >> 4) & 1)) * 32 + step * 16 + (r & 15)]

    def add_receiver_0(n, carry):
        code = found[0, n + 1]
        r, x, y, z = code & 4095, (code >> 12) & 511, (code >> 21) & 63, code >> 27
        at, hit = cell_at(place, z, y + (O - 2), x)
        residual = (uf[at] - observed(0, r)) * coef[3, z0 + z]
        a0f[at] = a0f[at] + jnp.where(hit, residual, 0.0)
        return carry

    count = found[0, 0]
    lax.fori_loop(0, count, add_receiver_0, 0)

    def layer(l, carry):
        i = z0 + l + 2
        dn, ia = coef[1, i], coef[3, i]
        for s in range(O, O + CY, 8):
            y = slice(s - O, s - O + 8)
            c = v[l, y, :] * RATIO
            c = c * c
            q, lap = laplace(a0f, l + 2, s)
            a2[l, y, :] = (2.0 * q - dn * a[l, y, :] + c * lap) * ia
            a0o[l, y, :] = q
            grad[l, y, :] = gp[l, y, :] + w[l, y, :] * q
        return carry

    lax.fori_loop(0, CZ, layer, 0)

    def add_receiver_1(n, carry):
        code = found[0, n + 1]
        r, x, y, z = code & 4095, (code >> 12) & 511, ((code >> 21) & 63) - 2, (code >> 27) - 2

        @pl.when((z >= 0) & (z < CZ) & (y >= 0) & (y < CY))
        def _():
            at, hit = cell_at(place, z, y, x)
            before, _ = cell_at(place, z + 2, y + O, x)
            residual = (u0f[before] - observed(1, r)) * coef[3, z0 + z + 2]
            a2[at] = a2[at] + jnp.where(hit, residual, 0.0)

        return carry

    lax.fori_loop(0, count, add_receiver_1, 0)


def f32(*shape):
    return jax.ShapeDtypeStruct(shape, jnp.float32)


def call(kernel, out_shape, in_specs, scratch_shapes=()):
    many = isinstance(out_shape, tuple)
    return pl.pallas_call(
        kernel,
        out_shape=out_shape,
        in_specs=in_specs,
        out_specs=(vmem(),) * len(out_shape) if many else smem(),
        scratch_shapes=scratch_shapes,
        compiler_params=pltpu.CompilerParams(vmem_limit_bytes=VMEM_LIMIT),
        name=kernel.__name__,
    )


def swap(value, axis, size, first):
    pairs = [(i, (first + ((i - first) % size ^ 1)) % size) for i in range(size)]
    return lax.ppermute(value, axis, pairs)


def swap_open(value, axis, size):
    pairs = [(i, i + 1) for i in range(1, size - 1, 2)]
    return lax.ppermute(value, axis, pairs + [(j, i) for i, j in pairs])


def shards(u, u1, a, a1, v, obs, rec, src, amp):
    assert u.shape == (CZ, CY, NX)
    gz, gy = lax.axis_index(GZ), lax.axis_index(GY)
    meta = [gz * CZ, gy * CY, lax.axis_index("yh"), lax.axis_index("c"), lax.axis_index("xl")]
    meta = jnp.stack(meta).astype(jnp.int32)
    coef = jnp.asarray(coefficient_table())
    block, edge = f32(CZ, CY, NX), f32(CZ, 8, NX)
    frame, zpack = f32(8, FR, NX), f32(2, ZROWS, NX)
    part = pltpu.VMEM((2, CZ, 8, NX), jnp.float32)
    full = pltpu.VMEM((8, FR, NX), jnp.float32)

    h, g, own = call(
        pack_y,
        (f32(CZ, 16, NX), f32(CZ, 16, NX), f32(1, 128)),
        [smem()] + [pl.BlockSpec(memory_space=pltpu.HBM)] * 6,
        [pltpu.VMEM((5, CZ, 8, NX), jnp.float32)] * 2
        + [pltpu.VMEM((2, 16), jnp.float32), pltpu.VMEM((1, 128), jnp.float32), pltpu.SemaphoreType.DMA((11,))],
    )(meta, u, a, u1, a1, v, obs)
    rh = swap(h, GY, NY_DEV, 0)
    g = lax.dynamic_update_slice(g, rh[0:1, 14:15, :], (0, 15, 0))
    rg = swap(g, GY, NY_DEV, 1)

    u0p, a0p = call(own_step, (block, block), [smem()] * 2 + [vmem()] * 5)(meta, coef, u, a, u1, a1, v)

    found = call(
        list_receivers,
        jax.ShapeDtypeStruct((1, rec.shape[1] + 128), jnp.int32),
        [smem(), vmem(), smem()],
        [
            pltpu.VMEM((32, 128), jnp.int32),
            pltpu.VMEM((1, 128), jnp.int32),
            pltpu.SMEM((1, 128), jnp.int32),
            pltpu.SemaphoreType.DMA,
        ],
    )(meta, rec, rec)

    ulo, uhi, alo, ahi, zc, zb, traces = call(
        edge_step,
        (edge,) * 4 + (zpack, zpack, f32(64, 128)),
        [smem()] * 2 + [vmem()] * 10,
        [part] * 5,
    )(meta, coef, u, a, u1, a1, v, rh, rg, own, u0p, a0p)

    rc = swap(zc, GZ, NZ_DEV, 0)
    rb = swap_open(zb, GZ, NZ_DEV)
    table = lax.all_to_all(traces, ("yl", "z", "c", "xh"), 0, 0, tiled=True)

    u2, u0, w, gp, uf, u0f, a0f = call(
        wave_step,
        (block,) * 4 + (frame,) * 3,
        [smem()] * 2 + [vmem()] * 14 + [smem()] * 2,
        [full] * 2,
    )(meta, coef, u, a, u1, v, rh, rg, u0p, a0p, ulo, uhi, alo, ahi, rc, rb, src, amp)

    a2, a0, grad = call(
        adjoint_step,
        (block,) * 3,
        [smem()] * 2 + [vmem()] * 7 + [smem()] * 2,
        [full],
    )(meta, coef, a, v, uf, u0f, a0f, w, gp, found, table)
    return u2, u0, a2, a0, grad


def solution(mesh):
    fine = Mesh(mesh.devices.reshape(2, 8, 2, 2, 2, 2), ("yl", "z", "c", "xh", "xl", "yh"))
    field = P(GZ, GY, None)
    return jax.shard_map(
        shards,
        mesh=fine,
        in_specs=(field,) * 5 + (P(None, GZ + GY), P(), P(), P()),
        out_specs=(field,) * 5,
        check_vma=False,
    )
```

```python
import jax
import jax.numpy as jnp
import numpy as np
from jax import lax
from jax.experimental import pallas as pl
from jax.experimental.pallas import tpu as pltpu
from jax.sharding import Mesh
from jax.sharding import PartitionSpec as P

CENTRE = -7.5
NEAR = 4.0 / 3.0
FAR = -1.0 / 12.0
RATIO = 0.1
DAMP = 0.3

GZ = ("yl", "z", "c")
GY = ("x", "yh")
O = 8
NZ_DEV, NY_DEV = 32, 8
CZ, CY, NX = 4, 32, 512
NZ, NY = NZ_DEV * CZ, NY_DEV * CY
FR = CY + 2 * O
VMEM_LIMIT = 8 * 1024 * 1024
ZROWS = 5 * CY + 8
GROUP = 4


def coefficient_table():
    z = np.clip(np.arange(-2, NZ + 2), 0, NZ - 1).astype(np.float32)
    low = np.maximum(np.float32(CZ) - z, np.float32(0)) / np.float32(CZ)
    high = np.maximum(z - np.float32(NZ - 1 - CZ), np.float32(0)) / np.float32(CZ)
    a = np.float32(DAMP) * (low * low + high * high)
    one = np.float32(1)
    return np.stack([one + a, one - a, one / (one - a), one / (one + a)]).astype(np.float32)


def smem():
    return pl.BlockSpec(memory_space=pltpu.SMEM)


def vmem():
    return pl.BlockSpec()


def x_terms(u):
    lane = lax.broadcasted_iota(jnp.int32, u.shape, 1)
    a = jnp.where(lane >= 1, pltpu.roll(u, 1, 1), 0.0)
    b = jnp.where(lane < NX - 1, pltpu.roll(u, NX - 1, 1), 0.0)
    c = jnp.where(lane >= 2, pltpu.roll(u, 2, 1), 0.0)
    d = jnp.where(lane < NX - 2, pltpu.roll(u, NX - 2, 1), 0.0)
    return a + b, c + d


def laplace(f, k, s):
    rows = lambda layer, shift: f[layer, s + shift : s + shift + 8, :]
    u = rows(k, 0)
    near, far = x_terms(u)
    near = near + ((rows(k, -1) + rows(k, 1)) + (rows(k - 1, 0) + rows(k + 1, 0)))
    far = far + ((rows(k, -2) + rows(k, 2)) + (rows(k - 2, 0) + rows(k + 2, 0)))
    return u, CENTRE * u + NEAR * near + FAR * far


def depth_factors(l):
    near_up = jnp.where(l >= 1, jnp.float32(NEAR), jnp.float32(0.0))
    near_dn = jnp.where(l < CZ - 1, jnp.float32(NEAR), jnp.float32(0.0))
    far_up = jnp.where(l >= 2, jnp.float32(FAR), jnp.float32(0.0))
    far_dn = jnp.where(l < CZ - 2, jnp.float32(FAR), jnp.float32(0.0))
    layers = jnp.maximum(l - 1, 0), jnp.minimum(l + 1, CZ - 1), jnp.maximum(l - 2, 0), jnp.minimum(l + 2, CZ - 1)
    return tuple(zip(layers, (near_up, near_dn, far_up, far_dn)))


def partial_laplace(f, l, s, size, factors):
    u = f[l, s : s + 8, :]

    def shifted(shift):
        if 0 <= s + shift and s + shift + 8 <= size:
            return f[l, s + shift : s + shift + 8, :]
        return pltpu.roll(u, (-shift) % 8, 0)

    near, far = x_terms(u)
    lap = CENTRE * u + NEAR * (near + (shifted(-1) + shifted(1))) + FAR * (far + (shifted(-2) + shifted(2)))
    for layer, factor in factors:
        lap = lap + factor * f[layer, s : s + 8, :]
    return u, lap


def pack_y(meta, u, a, u1, a1, v, obs, h, g, own, first, last, obs_v, row, sem):
    copies = []
    for i, ref in enumerate((u, a, u1, a1, v)):
        copies.append(pltpu.make_async_copy(ref.at[:, 0:8, :], first.at[i], sem.at[2 * i]))
        copies.append(pltpu.make_async_copy(ref.at[:, CY - 8 : CY, :], last.at[i], sem.at[2 * i + 1]))
    copies.append(pltpu.make_async_copy(obs, obs_v, sem.at[10]))
    for copy in copies:
        copy.start()
    for copy in copies:
        copy.wait()
    for k in range(4):
        for t in range(2):
            row[0:1, 32 * k + 16 * t : 32 * k + 16 * t + 16] = obs_v[t : t + 1, :]
    lane = lax.broadcasted_iota(jnp.int32, (1, 128), 1)
    mine = jnp.where((lane >> 5) == meta[2], row[0:1, :], 0.0)
    own[...] = mine

    def pack(dst, high):
        rows = last if high else first
        four = slice(4, 8) if high else slice(0, 4)
        two = slice(6, 8) if high else slice(0, 2)
        dst[:, 0:4, :] = rows[0, :, four, :]
        dst[:, 4:8, :] = rows[1, :, four, :]
        dst[:, 8:10, :] = rows[2, :, two, :]
        dst[:, 10:12, :] = rows[3, :, two, :]
        dst[:, 12:14, :] = rows[4, :, two, :]
        dst[:, 14:16, :] = jnp.zeros((CZ, 2, NX), jnp.float32)
        dst[0, 14:15, 0:128] = mine

    @pl.when(meta[2] == 0)
    def _():
        pack(h, True)
        pack(g, False)

    @pl.when(meta[2] != 0)
    def _():
        pack(h, False)
        pack(g, True)


def pick_y(meta, rh, rg, low, high):
    @pl.when(meta[2] == 0)
    def _():
        high(rh)
        low(rg)

    @pl.when(meta[2] != 0)
    def _():
        low(rh)
        high(rg)


def own_step(meta, coef, u, a, u1, a1, v, u0p, a0p):
    z0 = meta[0]

    def layer(l, carry):
        i = z0 + l + 2
        up, dn, iu, ia = coef[0, i], coef[1, i], coef[2, i], coef[3, i]
        factors = depth_factors(l)
        for s in range(0, CY, 8):
            y = slice(s, s + 8)
            c = v[l, y, :] * RATIO
            c = c * c
            p, lap = partial_laplace(u, l, s, CY, factors)
            u0p[l, y, :] = (2.0 * p - up * u1[l, y, :] + c * lap) * iu
            q, lap = partial_laplace(a, l, s, CY, factors)
            a0p[l, y, :] = (2.0 * q - dn * a1[l, y, :] + c * lap) * ia
        return carry

    lax.fori_loop(0, CZ, layer, 0)


def edge_step(
    meta, coef, u, a, u1, a1, v, rh, rg, own, u0p, a0p, ut, at, zc, zb, traces,
    pu, pa, pu1, pa1, pv,
):
    z0 = meta[0]
    pu[0, :, 4:8, :] = u[:, 0:4, :]
    pu[1, :, 0:4, :] = u[:, CY - 4 : CY, :]
    pa[0, :, 4:8, :] = a[:, 0:4, :]
    pa[1, :, 0:4, :] = a[:, CY - 4 : CY, :]
    for part, block in ((pu1, u1), (pa1, a1), (pv, v)):
        part[0, :, 4:6, :] = block[:, 0:2, :]
        part[1, :, 2:4, :] = block[:, CY - 2 : CY, :]

    def low(r):
        pu[0, :, 0:4, :] = r[:, 0:4, :]
        pa[0, :, 0:4, :] = r[:, 4:8, :]
        pu1[0, :, 2:4, :] = r[:, 8:10, :]
        pa1[0, :, 2:4, :] = r[:, 10:12, :]
        pv[0, :, 2:4, :] = r[:, 12:14, :]

    def high(r):
        pu[1, :, 4:8, :] = r[:, 0:4, :]
        pa[1, :, 4:8, :] = r[:, 4:8, :]
        pu1[1, :, 4:6, :] = r[:, 8:10, :]
        pa1[1, :, 4:6, :] = r[:, 10:12, :]
        pv[1, :, 4:6, :] = r[:, 12:14, :]

    pick_y(meta, rh, rg, low, high)

    def layer(l, carry):
        i = z0 + l + 2
        up, dn, iu, ia = coef[0, i], coef[1, i], coef[2, i], coef[3, i]
        factors = depth_factors(l)
        for side in range(2):
            c = pv[side, l] * RATIO
            c = c * c
            p, lap = partial_laplace(pu.at[side], l, 0, 8, factors)
            ut[side, l] = (2.0 * p - up * pu1[side, l] + c * lap) * iu
            q, lap = partial_laplace(pa.at[side], l, 0, 8, factors)
            at[side, l] = (2.0 * q - dn * pa1[side, l] + c * lap) * ia
        return carry

    lax.fori_loop(0, CZ, layer, 0)
    ut[0, :, 0:2, :] = pu[0, :, 2:4, :]
    ut[0, :, 6:8, :] = pv[0, :, 2:4, :]
    ut[1, :, 6:8, :] = pu[1, :, 4:6, :]
    ut[1, :, 0:2, :] = pv[1, :, 4:6, :]

    def pack(dst, l):
        m = slice(l, l + 2)
        dst[:, 0:CY, :] = u[m]
        dst[:, CY : 2 * CY, :] = a[m]
        dst[:, 4 * CY : 5 * CY, :] = v[m]
        for b, p, t in ((2 * CY, u0p, ut), (3 * CY, a0p, at)):
            dst[:, b : b + CY, :] = p[m]
            dst[:, b : b + 2, :] = t[0, m, 4:6, :]
            dst[:, b + CY - 2 : b + CY, :] = t[1, m, 2:4, :]
        b = 5 * CY
        dst[:, b : b + 2, :] = pu[0, m, 2:4, :]
        dst[:, b + 2 : b + 4, :] = pu[1, m, 4:6, :]
        dst[:, b + 4 : b + 6, :] = pa[0, m, 2:4, :]
        dst[:, b + 6 : b + 8, :] = pa[1, m, 4:6, :]

    @pl.when(meta[3] == 0)
    def _():
        pack(zc, 2)
        pack(zb, 0)

    @pl.when(meta[3] != 0)
    def _():
        pack(zc, 0)
        pack(zb, 2)

    mine = rh[0, 14:15, 0:128] + own[...]
    traces[...] = jnp.broadcast_to(mine, traces.shape)


def list_receivers(meta, rec, out, bits, words_v, codes_v, words, codes, sem):
    z0, y0 = meta[0], meta[1]
    lz = rec[0:1, :] - z0
    ly = ((rec[1:2, :] - y0 + 16) & (NY - 1)) - 16
    own_z = (lz >= 0) & (lz < CZ)
    own_y = (ly >= 0) & (ly < CY)
    near = (lz >= -2) & (lz < CZ + 2) & (ly >= -2) & (ly < CY + 2) & (own_z | own_y)
    own = jnp.where(own_z & own_y, 1 << 30, 0)
    number = lax.broadcasted_iota(jnp.int32, lz.shape, 1)
    codes_v[...] = number | (rec[2:3, :] << 12) | ((ly + 2) << 21) | ((lz + 2) << 27) | own
    m = near.astype(jnp.int32)
    for i in range(32):
        bits[i : i + 1, :] = m[:, 128 * i : 128 * i + 128] << i
    words_v[...] = jnp.sum(bits[...], axis=0, keepdims=True)
    copies = [pltpu.make_async_copy(codes_v, codes, sem.at[0]), pltpu.make_async_copy(words_v, words, sem.at[1])]
    for copy in copies:
        copy.start()
    for copy in copies:
        copy.wait()

    def word_step(w, count):
        def bit_step(carry):
            word, count = carry
            low = word & (-word)
            out[0, count + 1] = codes[0, (31 - lax.clz(low)) * 128 + w]
            return word ^ low, count + 1

        return lax.while_loop(lambda carry: carry[0] != 0, bit_step, (words[0, w], count))[1]

    count = lax.fori_loop(0, 128, word_step, 0)
    out[0, 0] = count
    for k in range(GROUP - 1):
        out[0, count + 1 + k] = (2 << 21) | (2 << 27)


def cell_place():
    return lax.broadcasted_iota(jnp.int32, (8, 128), 0) * 128 + lax.broadcasted_iota(jnp.int32, (8, 128), 1)


def cell_at(place, layer, row, x):
    rows = pl.ds(pl.multiple_of((row >> 3) << 3, 8), 8)
    cols = pl.ds(pl.multiple_of((x >> 7) << 7, 128), 128)
    return (layer, rows, cols), place == ((row & 7) * 128 + (x & 127))


def wave_step(
    meta, coef, u, a, u1, v, u0p, a0p, ut, at, rc, rb, src, amp, found,
    u2, u0o, w, gp, ep, a0f,
    uf, u0f, af, vf,
):
    e = O + CY
    z0, y0 = meta[0], meta[1]
    uf[2:6, O:e, :] = u[...]
    vf[2:6, O:e, :] = v[...]
    u0f[2:6, O:e, :] = u0p[...]
    a0f[2:6, O:e, :] = a0p[...]
    for f0, t in ((u0f, ut), (a0f, at)):
        f0[2:6, O - 2 : O + 2, :] = t[0, :, 2:6, :]
        f0[2:6, e - 2 : e + 2, :] = t[1, :, 2:6, :]
    uf[2:6, O - 2 : O, :] = ut[0, :, 0:2, :]
    uf[2:6, e : e + 2, :] = ut[1, :, 6:8, :]
    vf[2:6, O - 2 : O, :] = ut[0, :, 6:8, :]
    vf[2:6, e : e + 2, :] = ut[1, :, 0:2, :]

    def fill_z(r, k):
        b = 5 * CY
        m = slice(k, k + 2)
        uf[m, O:e, :] = r[:, 0:CY, :]
        af[m, O:e, :] = r[:, CY : 2 * CY, :]
        u0f[m, O:e, :] = r[:, 2 * CY : 3 * CY, :]
        a0f[m, O:e, :] = r[:, 3 * CY : 4 * CY, :]
        vf[m, O:e, :] = r[:, 4 * CY : 5 * CY, :]
        uf[m, O - 2 : O, :] = r[:, b : b + 2, :]
        uf[m, e : e + 2, :] = r[:, b + 2 : b + 4, :]
        af[m, O - 2 : O, :] = r[:, b + 4 : b + 6, :]
        af[m, e : e + 2, :] = r[:, b + 6 : b + 8, :]

    @pl.when(meta[3] == 0)
    def _():
        fill_z(rb, 0)
        fill_z(rc, 6)

    @pl.when(meta[3] != 0)
    def _():
        fill_z(rc, 0)
        fill_z(rb, 6)

    lacks = ((0, None, 2), (1, 2, 3), (2, 1, 0), (3, None, 1), (4, None, 6), (5, 6, 7), (6, 5, 4), (7, None, 5))
    for k, near, far in lacks:
        edge = 2 <= k < 6
        iu, ia = coef[2, z0 + k], coef[3, z0 + k]

        def rows(t, carry):
            s = pl.multiple_of(t * 8, 8)
            c = vf[k, pl.ds(s, 8), :] * RATIO
            c = c * c
            for f, own, f0, scale in ((uf, u, u0f, iu), (af, a, a0f, ia)):
                term = lambda j: own[j - 2, pl.ds(s - O, 8), :] if 2 <= j < 6 else f[j, pl.ds(s, 8), :]
                lap = FAR * term(far)
                if near is not None:
                    lap = lap + NEAR * term(near)
                f0[k, pl.ds(s, 8), :] = f0[k, pl.ds(s, 8), :] + (c * scale) * lap
            return carry

        first = O // 8
        lax.fori_loop(first - edge, first + CY // 8 + edge, rows, 0)

    place = cell_place()

    def source_cell(i):
        return src[0, i] - z0, ((src[1, i] - y0 + 16) & (NY - 1)) - 16, src[2, i]

    def add_source_0(i, carry):
        lz, ly, x = source_cell(i)
        own_z = (lz >= 0) & (lz < CZ)
        own_y = (ly >= 0) & (ly < CY)
        near = (lz >= -2) & (lz < CZ + 2) & (ly >= -2) & (ly < CY + 2) & (own_z | own_y)

        @pl.when(near)
        def _():
            at, hit = cell_at(place, lz + 2, ly + O, x)
            c = vf[at] * RATIO
            u0f[at] = u0f[at] + jnp.where(hit, (c * c) * (amp[0, i] * coef[2, z0 + lz + 2]), 0.0)

        return carry

    lax.fori_loop(0, src.shape[1], add_source_0, 0)

    def layer(l, carry):
        i = z0 + l + 2
        up, dn, iu = coef[0, i], coef[1, i], coef[2, i]
        for s in range(O, O + CY, 8):
            y = slice(s - O, s - O + 8)
            vel = v[l, y, :]
            c = vel * RATIO
            c = c * c
            un = u[l, y, :]
            q, lap = laplace(u0f, l + 2, s)
            new = (2.0 * q - up * un + c * lap) * iu
            u2[l, y, :] = new
            u0o[l, y, :] = q
            slow = 2.0 / vel
            w[l, y, :] = slow * (un - 2.0 * q + new)
            an = a[l, y, :]
            gp[l, y, :] = slow * an * (u1[l, y, :] - 2.0 * un + q)
            ep[l, y, :] = -dn * an
        return carry

    lax.fori_loop(0, CZ, layer, 0)

    def add_source_1(i, carry):
        lz, ly, x = source_cell(i)

        @pl.when((lz >= 0) & (lz < CZ) & (ly >= 0) & (ly < CY))
        def _():
            at, hit = cell_at(place, lz, ly, x)
            vel = v[at]
            c = vel * RATIO
            added = jnp.where(hit, (c * c) * (amp[1, i] * coef[2, z0 + lz + 2]), 0.0)
            u2[at] = u2[at] + added
            w[at] = w[at] + (2.0 / vel) * added

        return carry

    lax.fori_loop(0, src.shape[1], add_source_1, 0)

    def sample(code, valid, own):
        _, framed, inner, hit, z = receiver(code, place)
        a0f[framed] = a0f[framed] + jnp.where(hit, uf[framed] * (coef[3, z0 + z] * valid), 0.0)
        ep[inner] = ep[inner] + jnp.where(hit, u0f[framed] * own, 0.0)

    each_receiver(found, place, sample)


def receiver(code, place):
    r, x, y, z = code & 4095, (code >> 12) & 511, (code >> 21) & 63, (code >> 27) & 7
    framed, hit = cell_at(place, z, y + (O - 2), x)
    own, _ = cell_at(place, jnp.clip(z - 2, 0, CZ - 1), jnp.clip(y - 2, 0, CY - 1), x)
    return r, framed, own, hit, z


def each_receiver(found, place, one):
    count = found[0, 0]

    def group(b, carry):
        for k in range(GROUP):
            n = b * GROUP + k
            code = found[0, n + 1]
            valid = jnp.where(n < count, jnp.float32(1.0), jnp.float32(0.0))
            one(code, valid, jnp.where(code >= 1 << 30, valid, jnp.float32(0.0)))
        return carry

    lax.fori_loop(0, (count + GROUP - 1) // GROUP, group, 0)


def adjoint_step(meta, coef, v, a0p, w, gp, ep, found, table, a2, a0o, grad, a0f, ef):
    z0 = meta[0]
    for k in range(8):
        a0f[k] = a0p[k]
    for l in range(CZ):
        ef[l] = ep[l]
    place = cell_place()

    def subtract(code, valid, own):
        r, framed, inner, hit, z = receiver(code, place)
        col = ((r >> 4) & 1) * 32 + (r & 15)
        first = table[r >> 5, col] * (coef[3, z0 + z] * valid)
        second = table[r >> 5, col + 16] * own
        a0f[framed] = a0f[framed] - jnp.where(hit, first, 0.0)
        ef[inner] = ef[inner] - jnp.where(hit, second, 0.0)

    each_receiver(found, place, subtract)

    def layer(l, carry):
        i = z0 + l + 2
        ia = coef[3, i]
        for s in range(O, O + CY, 8):
            y = slice(s - O, s - O + 8)
            c = v[l, y, :] * RATIO
            c = c * c
            q, lap = laplace(a0f, l + 2, s)
            a2[l, y, :] = (2.0 * q + ef[l, y, :] + c * lap) * ia
            a0o[l, y, :] = q
            grad[l, y, :] = gp[l, y, :] + w[l, y, :] * q
        return carry

    lax.fori_loop(0, CZ, layer, 0)


def f32(*shape):
    return jax.ShapeDtypeStruct(shape, jnp.float32)


def call(kernel, out_shape, in_specs, scratch_shapes=()):
    many = isinstance(out_shape, tuple)
    made = pl.pallas_call(
        kernel,
        out_shape=out_shape,
        in_specs=in_specs,
        out_specs=(vmem(),) * len(out_shape) if many else smem(),
        scratch_shapes=scratch_shapes,
        compiler_params=pltpu.CompilerParams(vmem_limit_bytes=VMEM_LIMIT),
        name=kernel.__name__,
    )

    def run(*args):
        if kernel is pack_y:
            args = args[:1] + tuple(pltpu.with_memory_space_constraint(x, pltpu.HBM) for x in args[1:])
        return made(*args)

    return run


def swap(value, axis, size, first):
    pairs = [(i, (first + ((i - first) % size ^ 1)) % size) for i in range(size)]
    return lax.ppermute(value, axis, pairs)


def swap_open(value, axis, size):
    pairs = [(i, i + 1) for i in range(1, size - 1, 2)]
    return lax.ppermute(value, axis, pairs + [(j, i) for i, j in pairs])


def shards(u, u1, a, a1, v, obs, rec, src, amp):
    assert u.shape == (CZ, CY, NX)
    gz, gy = lax.axis_index(GZ), lax.axis_index(GY)
    meta = [gz * CZ, gy * CY, lax.axis_index("yh"), lax.axis_index("c")]
    meta = jnp.stack(meta).astype(jnp.int32)
    coef = jnp.asarray(coefficient_table())
    block, edge = f32(CZ, CY, NX), f32(2, CZ, 8, NX)
    frame, zpack = f32(8, FR, NX), f32(2, ZROWS, NX)
    part = pltpu.VMEM((2, CZ, 8, NX), jnp.float32)
    full = pltpu.VMEM((8, FR, NX), jnp.float32)

    h, g, own = call(
        pack_y,
        (f32(CZ, 16, NX), f32(CZ, 16, NX), f32(1, 128)),
        [smem()] + [pl.BlockSpec(memory_space=pltpu.HBM)] * 6,
        [pltpu.VMEM((5, CZ, 8, NX), jnp.float32)] * 2
        + [pltpu.VMEM((2, 16), jnp.float32), pltpu.VMEM((1, 128), jnp.float32), pltpu.SemaphoreType.DMA((11,))],
    )(meta, u, a, u1, a1, v, obs)
    rh = swap(h, GY, NY_DEV, 0)
    rg = swap(g, GY, NY_DEV, 1)

    u0p, a0p = call(own_step, (block, block), [smem()] * 2 + [vmem()] * 5)(meta, coef, u, a, u1, a1, v)

    found = call(
        list_receivers,
        jax.ShapeDtypeStruct((1, rec.shape[1] + 128), jnp.int32),
        [smem(), vmem()],
        [
            pltpu.VMEM((32, 128), jnp.int32),
            pltpu.VMEM((1, 128), jnp.int32),
            pltpu.VMEM(rec[:1].shape, jnp.int32),
            pltpu.SMEM((1, 128), jnp.int32),
            pltpu.SMEM(rec[:1].shape, jnp.int32),
            pltpu.SemaphoreType.DMA((2,)),
        ],
    )(meta, rec)

    ut, at, zc, zb, traces = call(
        edge_step,
        (edge,) * 2 + (zpack, zpack, f32(128, 128)),
        [smem()] * 2 + [vmem()] * 10,
        [part] * 5,
    )(meta, coef, u, a, u1, a1, v, rh, rg, own, u0p, a0p)

    rc = swap(zc, GZ, NZ_DEV, 0)
    rb = swap_open(zb, GZ, NZ_DEV)
    table = lax.all_to_all(traces, GZ + ("x",), 0, 0, tiled=True)

    u2, u0, w, gp, ep, a0f = call(
        wave_step,
        (block,) * 5 + (frame,),
        [smem()] * 2 + [vmem()] * 10 + [smem()] * 3,
        [full] * 4,
    )(meta, coef, u, a, u1, v, u0p, a0p, ut, at, rc, rb, src, amp, found)

    a2, a0, grad = call(
        adjoint_step,
        (block,) * 3,
        [smem()] * 2 + [vmem()] * 5 + [smem()] * 2,
        [full, pltpu.VMEM((CZ, CY, NX), jnp.float32)],
    )(meta, coef, v, a0f, w, gp, ep, found, table)
    return u2, u0, a2, a0, grad


def solution(mesh):
    fine = Mesh(mesh.devices.reshape(2, 8, 2, 4, 2), ("yl", "z", "c", "x", "yh"))
    field = P(GZ, GY, None)
    return jax.shard_map(
        shards,
        mesh=fine,
        in_specs=(field,) * 5 + (P(None, GZ + GY), P(), P(), P()),
        out_specs=(field,) * 5,
        check_vma=False,
    )
```

```python
import jax
import jax.numpy as jnp
import numpy as np
from jax import lax
from jax.experimental import pallas as pl
from jax.experimental.pallas import tpu as pltpu
from jax.sharding import Mesh
from jax.sharding import PartitionSpec as P

CENTRE = -7.5
NEAR = 4.0 / 3.0
FAR = -1.0 / 12.0
RATIO = 0.1
DAMP = 0.3

GZ = ("yl", "z", "c")
GY = ("x", "yh")
O = 8
NZ_DEV, NY_DEV = 32, 8
CZ, CY, NX = 4, 32, 512
NZ, NY = NZ_DEV * CZ, NY_DEV * CY
FR = CY + 2 * O
VMEM_LIMIT = 8 * 1024 * 1024
ZROWS = 5 * CY + 8
GROUP = 4


def coefficient_table():
    z = np.clip(np.arange(-2, NZ + 2), 0, NZ - 1).astype(np.float32)
    low = np.maximum(np.float32(CZ) - z, np.float32(0)) / np.float32(CZ)
    high = np.maximum(z - np.float32(NZ - 1 - CZ), np.float32(0)) / np.float32(CZ)
    a = np.float32(DAMP) * (low * low + high * high)
    one = np.float32(1)
    return np.stack([one + a, one - a, one / (one - a), one / (one + a)]).astype(np.float32)


def smem():
    return pl.BlockSpec(memory_space=pltpu.SMEM)


def vmem():
    return pl.BlockSpec()


def x_terms(u):
    lane = lax.broadcasted_iota(jnp.int32, u.shape, 1)
    a = jnp.where(lane >= 1, pltpu.roll(u, 1, 1), 0.0)
    b = jnp.where(lane < NX - 1, pltpu.roll(u, NX - 1, 1), 0.0)
    c = jnp.where(lane >= 2, pltpu.roll(u, 2, 1), 0.0)
    d = jnp.where(lane < NX - 2, pltpu.roll(u, NX - 2, 1), 0.0)
    return a + b, c + d


def laplace(f, k, s):
    rows = lambda layer, shift: f[layer, s + shift : s + shift + 8, :]
    u = rows(k, 0)
    near, far = x_terms(u)
    near = near + ((rows(k, -1) + rows(k, 1)) + (rows(k - 1, 0) + rows(k + 1, 0)))
    far = far + ((rows(k, -2) + rows(k, 2)) + (rows(k - 2, 0) + rows(k + 2, 0)))
    return u, CENTRE * u + NEAR * near + FAR * far


def depth_factors(l):
    near_up = jnp.where(l >= 1, jnp.float32(NEAR), jnp.float32(0.0))
    near_dn = jnp.where(l < CZ - 1, jnp.float32(NEAR), jnp.float32(0.0))
    far_up = jnp.where(l >= 2, jnp.float32(FAR), jnp.float32(0.0))
    far_dn = jnp.where(l < CZ - 2, jnp.float32(FAR), jnp.float32(0.0))
    layers = jnp.maximum(l - 1, 0), jnp.minimum(l + 1, CZ - 1), jnp.maximum(l - 2, 0), jnp.minimum(l + 2, CZ - 1)
    return tuple(zip(layers, (near_up, near_dn, far_up, far_dn)))


def partial_laplace(f, l, s, size, factors):
    u = f[l, s : s + 8, :]

    def shifted(shift):
        if 0 <= s + shift and s + shift + 8 <= size:
            return f[l, s + shift : s + shift + 8, :]
        return pltpu.roll(u, (-shift) % 8, 0)

    near, far = x_terms(u)
    lap = CENTRE * u + NEAR * (near + (shifted(-1) + shifted(1))) + FAR * (far + (shifted(-2) + shifted(2)))
    for layer, factor in factors:
        lap = lap + factor * f[layer, s : s + 8, :]
    return u, lap


def pack_y(meta, u, a, u1, a1, v, obs, h, g, own, first, last, obs_v, row, sem):
    copies = []
    for i, ref in enumerate((u, a, u1, a1, v)):
        copies.append(pltpu.make_async_copy(ref.at[:, 0:8, :], first.at[i], sem.at[2 * i]))
        copies.append(pltpu.make_async_copy(ref.at[:, CY - 8 : CY, :], last.at[i], sem.at[2 * i + 1]))
    copies.append(pltpu.make_async_copy(obs, obs_v, sem.at[10]))
    for copy in copies:
        copy.start()
    for copy in copies:
        copy.wait()
    for k in range(4):
        for t in range(2):
            row[0:1, 32 * k + 16 * t : 32 * k + 16 * t + 16] = obs_v[t : t + 1, :]
    lane = lax.broadcasted_iota(jnp.int32, (1, 128), 1)
    mine = jnp.where((lane >> 5) == meta[2], row[0:1, :], 0.0)
    own[...] = mine

    def pack(dst, high):
        rows = last if high else first
        four = slice(4, 8) if high else slice(0, 4)
        two = slice(6, 8) if high else slice(0, 2)
        dst[:, 0:4, :] = rows[0, :, four, :]
        dst[:, 4:8, :] = rows[1, :, four, :]
        dst[:, 8:10, :] = rows[2, :, two, :]
        dst[:, 10:12, :] = rows[3, :, two, :]
        dst[:, 12:14, :] = rows[4, :, two, :]
        dst[:, 14:16, :] = jnp.zeros((CZ, 2, NX), jnp.float32)
        dst[0, 14:15, 0:128] = mine

    @pl.when(meta[2] == 0)
    def _():
        pack(h, True)
        pack(g, False)

    @pl.when(meta[2] != 0)
    def _():
        pack(h, False)
        pack(g, True)


def pick_y(meta, rh, rg, low, high):
    @pl.when(meta[2] == 0)
    def _():
        high(rh)
        low(rg)

    @pl.when(meta[2] != 0)
    def _():
        low(rh)
        high(rg)


def own_step(meta, coef, u, a, u1, a1, v, u0p, a0p):
    z0 = meta[0]

    def layer(l, carry):
        i = z0 + l + 2
        up, dn, iu, ia = coef[0, i], coef[1, i], coef[2, i], coef[3, i]
        factors = depth_factors(l)
        for s in range(0, CY, 8):
            y = slice(s, s + 8)
            c = v[l, y, :] * RATIO
            c = c * c
            p, lap = partial_laplace(u, l, s, CY, factors)
            u0p[l, y, :] = (2.0 * p - up * u1[l, y, :] + c * lap) * iu
            q, lap = partial_laplace(a, l, s, CY, factors)
            a0p[l, y, :] = (2.0 * q - dn * a1[l, y, :] + c * lap) * ia
        return carry

    lax.fori_loop(0, CZ, layer, 0)


def edge_step(
    meta, coef, u, a, u1, a1, v, rh, rg, own, u0p, a0p, ut, at, zc, zb, traces,
    pu, pa, pu1, pa1, pv,
):
    z0 = meta[0]
    pu[0, :, 4:8, :] = u[:, 0:4, :]
    pu[1, :, 0:4, :] = u[:, CY - 4 : CY, :]
    pa[0, :, 4:8, :] = a[:, 0:4, :]
    pa[1, :, 0:4, :] = a[:, CY - 4 : CY, :]
    for part, block in ((pu1, u1), (pa1, a1), (pv, v)):
        part[0, :, 4:6, :] = block[:, 0:2, :]
        part[1, :, 2:4, :] = block[:, CY - 2 : CY, :]

    def low(r):
        pu[0, :, 0:4, :] = r[:, 0:4, :]
        pa[0, :, 0:4, :] = r[:, 4:8, :]
        pu1[0, :, 2:4, :] = r[:, 8:10, :]
        pa1[0, :, 2:4, :] = r[:, 10:12, :]
        pv[0, :, 2:4, :] = r[:, 12:14, :]

    def high(r):
        pu[1, :, 4:8, :] = r[:, 0:4, :]
        pa[1, :, 4:8, :] = r[:, 4:8, :]
        pu1[1, :, 4:6, :] = r[:, 8:10, :]
        pa1[1, :, 4:6, :] = r[:, 10:12, :]
        pv[1, :, 4:6, :] = r[:, 12:14, :]

    pick_y(meta, rh, rg, low, high)

    def layer(l, carry):
        i = z0 + l + 2
        up, dn, iu, ia = coef[0, i], coef[1, i], coef[2, i], coef[3, i]
        factors = depth_factors(l)
        for side in range(2):
            c = pv[side, l] * RATIO
            c = c * c
            p, lap = partial_laplace(pu.at[side], l, 0, 8, factors)
            ut[side, l] = (2.0 * p - up * pu1[side, l] + c * lap) * iu
            q, lap = partial_laplace(pa.at[side], l, 0, 8, factors)
            at[side, l] = (2.0 * q - dn * pa1[side, l] + c * lap) * ia
        return carry

    lax.fori_loop(0, CZ, layer, 0)
    ut[0, :, 0:2, :] = pu[0, :, 2:4, :]
    ut[0, :, 6:8, :] = pv[0, :, 2:4, :]
    ut[1, :, 6:8, :] = pu[1, :, 4:6, :]
    ut[1, :, 0:2, :] = pv[1, :, 4:6, :]

    def pack(dst, l):
        m = slice(l, l + 2)
        dst[:, 0:CY, :] = u[m]
        dst[:, CY : 2 * CY, :] = a[m]
        dst[:, 4 * CY : 5 * CY, :] = v[m]
        for b, p, t in ((2 * CY, u0p, ut), (3 * CY, a0p, at)):
            dst[:, b : b + CY, :] = p[m]
            dst[:, b : b + 2, :] = t[0, m, 4:6, :]
            dst[:, b + CY - 2 : b + CY, :] = t[1, m, 2:4, :]
        b = 5 * CY
        dst[:, b : b + 2, :] = pu[0, m, 2:4, :]
        dst[:, b + 2 : b + 4, :] = pu[1, m, 4:6, :]
        dst[:, b + 4 : b + 6, :] = pa[0, m, 2:4, :]
        dst[:, b + 6 : b + 8, :] = pa[1, m, 4:6, :]

    @pl.when(meta[3] == 0)
    def _():
        pack(zc, 2)
        pack(zb, 0)

    @pl.when(meta[3] != 0)
    def _():
        pack(zc, 0)
        pack(zb, 2)

    mine = rh[0, 14:15, 0:128] + own[...]
    traces[...] = jnp.broadcast_to(mine, traces.shape)


def list_receivers(meta, rec, out, bits, words_v, codes_v, words, codes, sem):
    z0, y0 = meta[0], meta[1]
    lz = rec[0:1, :] - z0
    ly = ((rec[1:2, :] - y0 + 16) & (NY - 1)) - 16
    own_z = (lz >= 0) & (lz < CZ)
    own_y = (ly >= 0) & (ly < CY)
    near = (lz >= -2) & (lz < CZ + 2) & (ly >= -2) & (ly < CY + 2) & (own_z | own_y)
    own = jnp.where(own_z & own_y, 1 << 30, 0)
    number = lax.broadcasted_iota(jnp.int32, lz.shape, 1)
    codes_v[...] = number | (rec[2:3, :] << 12) | ((ly + 2) << 21) | ((lz + 2) << 27) | own
    m = near.astype(jnp.int32)
    for i in range(32):
        bits[i : i + 1, :] = m[:, 128 * i : 128 * i + 128] << i
    words_v[...] = jnp.sum(bits[...], axis=0, keepdims=True)
    copies = [pltpu.make_async_copy(codes_v, codes, sem.at[0]), pltpu.make_async_copy(words_v, words, sem.at[1])]
    for copy in copies:
        copy.start()
    for copy in copies:
        copy.wait()

    def word_step(w, count):
        def bit_step(carry):
            word, count = carry
            low = word & (-word)
            out[0, count + 1] = codes[0, (31 - lax.clz(low)) * 128 + w]
            return word ^ low, count + 1

        return lax.while_loop(lambda carry: carry[0] != 0, bit_step, (words[0, w], count))[1]

    count = lax.fori_loop(0, 128, word_step, 0)
    out[0, 0] = count
    for k in range(GROUP - 1):
        out[0, count + 1 + k] = (2 << 21) | (2 << 27)


def cell_place():
    return lax.broadcasted_iota(jnp.int32, (8, 128), 0) * 128 + lax.broadcasted_iota(jnp.int32, (8, 128), 1)


def cell_at(place, layer, row, x):
    rows = pl.ds(pl.multiple_of((row >> 3) << 3, 8), 8)
    cols = pl.ds(pl.multiple_of((x >> 7) << 7, 128), 128)
    return (layer, rows, cols), place == ((row & 7) * 128 + (x & 127))


def wave_step(
    meta, coef, u, a, u1, v, u0p, a0p, ut, at, rc, rb, src, amp, found,
    u2, u0o, w, gp, ep, a0f,
    uf, u0f, af, vf,
):
    e = O + CY
    z0, y0 = meta[0], meta[1]
    uf[2:6, O:e, :] = u[...]
    vf[2:6, O:e, :] = v[...]
    u0f[2:6, O:e, :] = u0p[...]
    a0f[2:6, O:e, :] = a0p[...]
    for f0, t in ((u0f, ut), (a0f, at)):
        f0[2:6, O - 2 : O + 2, :] = t[0, :, 2:6, :]
        f0[2:6, e - 2 : e + 2, :] = t[1, :, 2:6, :]
    uf[2:6, O - 2 : O, :] = ut[0, :, 0:2, :]
    uf[2:6, e : e + 2, :] = ut[1, :, 6:8, :]
    vf[2:6, O - 2 : O, :] = ut[0, :, 6:8, :]
    vf[2:6, e : e + 2, :] = ut[1, :, 0:2, :]

    def fill_z(r, k):
        b = 5 * CY
        m = slice(k, k + 2)
        uf[m, O:e, :] = r[:, 0:CY, :]
        af[m, O:e, :] = r[:, CY : 2 * CY, :]
        u0f[m, O:e, :] = r[:, 2 * CY : 3 * CY, :]
        a0f[m, O:e, :] = r[:, 3 * CY : 4 * CY, :]
        vf[m, O:e, :] = r[:, 4 * CY : 5 * CY, :]
        uf[m, O - 2 : O, :] = r[:, b : b + 2, :]
        uf[m, e : e + 2, :] = r[:, b + 2 : b + 4, :]
        af[m, O - 2 : O, :] = r[:, b + 4 : b + 6, :]
        af[m, e : e + 2, :] = r[:, b + 6 : b + 8, :]

    @pl.when(meta[3] == 0)
    def _():
        fill_z(rb, 0)
        fill_z(rc, 6)

    @pl.when(meta[3] != 0)
    def _():
        fill_z(rc, 0)
        fill_z(rb, 6)

    lacks = ((0, None, 2), (1, 2, 3), (2, 1, 0), (3, None, 1), (4, None, 6), (5, 6, 7), (6, 5, 4), (7, None, 5))
    for k, near, far in lacks:
        edge = 2 <= k < 6
        iu, ia = coef[2, z0 + k], coef[3, z0 + k]

        def rows(t, carry):
            s = pl.multiple_of(t * 8, 8)
            c = vf[k, pl.ds(s, 8), :] * RATIO
            c = c * c
            for f, own, f0, scale in ((uf, u, u0f, iu), (af, a, a0f, ia)):
                term = lambda j: own[j - 2, pl.ds(s - O, 8), :] if 2 <= j < 6 else f[j, pl.ds(s, 8), :]
                lap = FAR * term(far)
                if near is not None:
                    lap = lap + NEAR * term(near)
                f0[k, pl.ds(s, 8), :] = f0[k, pl.ds(s, 8), :] + (c * scale) * lap
            return carry

        first = O // 8
        lax.fori_loop(first - edge, first + CY // 8 + edge, rows, 0)

    place = cell_place()

    def source_cell(i):
        return src[0, i] - z0, ((src[1, i] - y0 + 16) & (NY - 1)) - 16, src[2, i]

    def add_source_0(i, carry):
        lz, ly, x = source_cell(i)
        own_z = (lz >= 0) & (lz < CZ)
        own_y = (ly >= 0) & (ly < CY)
        near = (lz >= -2) & (lz < CZ + 2) & (ly >= -2) & (ly < CY + 2) & (own_z | own_y)

        @pl.when(near)
        def _():
            at, hit = cell_at(place, lz + 2, ly + O, x)
            c = vf[at] * RATIO
            u0f[at] = u0f[at] + jnp.where(hit, (c * c) * (amp[0, i] * coef[2, z0 + lz + 2]), 0.0)

        return carry

    lax.fori_loop(0, src.shape[1], add_source_0, 0)

    def layer(l, carry):
        i = z0 + l + 2
        up, dn, iu = coef[0, i], coef[1, i], coef[2, i]
        for s in range(O, O + CY, 8):
            y = slice(s - O, s - O + 8)
            vel = v[l, y, :]
            c = vel * RATIO
            c = c * c
            un = u[l, y, :]
            q, lap = laplace(u0f, l + 2, s)
            new = (2.0 * q - up * un + c * lap) * iu
            u2[l, y, :] = new
            u0o[l, y, :] = q
            slow = 2.0 / vel
            w[l, y, :] = slow * (un - 2.0 * q + new)
            an = a[l, y, :]
            gp[l, y, :] = slow * an * (u1[l, y, :] - 2.0 * un + q)
            ep[l, y, :] = -dn * an
        return carry

    lax.fori_loop(0, CZ, layer, 0)

    def add_source_1(i, carry):
        lz, ly, x = source_cell(i)

        @pl.when((lz >= 0) & (lz < CZ) & (ly >= 0) & (ly < CY))
        def _():
            at, hit = cell_at(place, lz, ly, x)
            vel = v[at]
            c = vel * RATIO
            added = jnp.where(hit, (c * c) * (amp[1, i] * coef[2, z0 + lz + 2]), 0.0)
            u2[at] = u2[at] + added
            w[at] = w[at] + (2.0 / vel) * added

        return carry

    lax.fori_loop(0, src.shape[1], add_source_1, 0)

    def sample(code, valid, own):
        _, framed, inner, hit, z = receiver(code, place)
        a0f[framed] = a0f[framed] + jnp.where(hit, uf[framed] * (coef[3, z0 + z] * valid), 0.0)
        ep[inner] = ep[inner] + jnp.where(hit, u0f[framed] * own, 0.0)

    each_receiver(found, place, sample)


def receiver(code, place):
    r, x, y, z = code & 4095, (code >> 12) & 511, (code >> 21) & 63, (code >> 27) & 7
    framed, hit = cell_at(place, z, y + (O - 2), x)
    own, _ = cell_at(place, jnp.clip(z - 2, 0, CZ - 1), jnp.clip(y - 2, 0, CY - 1), x)
    return r, framed, own, hit, z


def each_receiver(found, place, one):
    count = found[0, 0]

    def group(b, carry):
        for k in range(GROUP):
            n = b * GROUP + k
            code = found[0, n + 1]
            valid = jnp.where(n < count, jnp.float32(1.0), jnp.float32(0.0))
            one(code, valid, jnp.where(code >= 1 << 30, valid, jnp.float32(0.0)))
        return carry

    lax.fori_loop(0, (count + GROUP - 1) // GROUP, group, 0)


def adjoint_step(meta, coef, v, a0p, w, gp, ep, found, table, a2, a0o, grad, a0f, ef):
    z0 = meta[0]
    for k in range(8):
        a0f[k] = a0p[k]
    for l in range(CZ):
        ef[l] = ep[l]
    place = cell_place()

    def subtract(code, valid, own):
        r, framed, inner, hit, z = receiver(code, place)
        col = ((r >> 4) & 1) * 32 + (r & 15)
        first = table[r >> 5, col] * (coef[3, z0 + z] * valid)
        second = table[r >> 5, col + 16] * own
        a0f[framed] = a0f[framed] - jnp.where(hit, first, 0.0)
        ef[inner] = ef[inner] - jnp.where(hit, second, 0.0)

    each_receiver(found, place, subtract)

    def layer(l, carry):
        i = z0 + l + 2
        ia = coef[3, i]
        for s in range(O, O + CY, 8):
            y = slice(s - O, s - O + 8)
            c = v[l, y, :] * RATIO
            c = c * c
            q, lap = laplace(a0f, l + 2, s)
            a2[l, y, :] = (2.0 * q + ef[l, y, :] + c * lap) * ia
            a0o[l, y, :] = q
            grad[l, y, :] = gp[l, y, :] + w[l, y, :] * q
        return carry

    lax.fori_loop(0, CZ, layer, 0)


def f32(*shape):
    return jax.ShapeDtypeStruct(shape, jnp.float32)


def hbm(*args):
    return tuple(pltpu.with_memory_space_constraint(x, pltpu.HBM) for x in args)


def call(kernel, out_shape, in_specs, scratch_shapes=()):
    many = isinstance(out_shape, tuple)
    return pl.pallas_call(
        kernel,
        out_shape=out_shape,
        in_specs=in_specs,
        out_specs=(vmem(),) * len(out_shape) if many else smem(),
        scratch_shapes=scratch_shapes,
        compiler_params=pltpu.CompilerParams(vmem_limit_bytes=VMEM_LIMIT),
        name=kernel.__name__,
    )


def swap(value, axis, size, first):
    pairs = [(i, (first + ((i - first) % size ^ 1)) % size) for i in range(size)]
    return lax.ppermute(value, axis, pairs)


def swap_open(value, axis, size):
    pairs = [(i, i + 1) for i in range(1, size - 1, 2)]
    return lax.ppermute(value, axis, pairs + [(j, i) for i, j in pairs])


def shards(u, u1, a, a1, v, obs, rec, src, amp):
    assert u.shape == (CZ, CY, NX)
    gz, gy = lax.axis_index(GZ), lax.axis_index(GY)
    meta = [gz * CZ, gy * CY, lax.axis_index("yh"), lax.axis_index("c")]
    meta = jnp.stack(meta).astype(jnp.int32)
    coef = jnp.asarray(coefficient_table())
    block, edge = f32(CZ, CY, NX), f32(2, CZ, 8, NX)
    frame, zpack = f32(8, FR, NX), f32(2, ZROWS, NX)
    part = pltpu.VMEM((2, CZ, 8, NX), jnp.float32)
    full = pltpu.VMEM((8, FR, NX), jnp.float32)

    h, g, own = call(
        pack_y,
        (f32(CZ, 16, NX), f32(CZ, 16, NX), f32(1, 128)),
        [smem()] + [pl.BlockSpec(memory_space=pltpu.HBM)] * 6,
        [pltpu.VMEM((5, CZ, 8, NX), jnp.float32)] * 2
        + [pltpu.VMEM((2, 16), jnp.float32), pltpu.VMEM((1, 128), jnp.float32), pltpu.SemaphoreType.DMA((11,))],
    )(meta, *hbm(u, a, u1, a1, v, obs))
    rh = swap(h, GY, NY_DEV, 0)
    rg = swap(g, GY, NY_DEV, 1)

    u0p, a0p = call(own_step, (block, block), [smem()] * 2 + [vmem()] * 5)(meta, coef, u, a, u1, a1, v)

    found = call(
        list_receivers,
        jax.ShapeDtypeStruct((1, rec.shape[1] + 128), jnp.int32),
        [smem(), vmem()],
        [
            pltpu.VMEM((32, 128), jnp.int32),
            pltpu.VMEM((1, 128), jnp.int32),
            pltpu.VMEM(rec[:1].shape, jnp.int32),
            pltpu.SMEM((1, 128), jnp.int32),
            pltpu.SMEM(rec[:1].shape, jnp.int32),
            pltpu.SemaphoreType.DMA((2,)),
        ],
    )(meta, rec)

    rg, found = lax.optimization_barrier((rg, found))
    ut, at, zc, zb, traces = call(
        edge_step,
        (edge,) * 2 + (zpack, zpack, f32(128, 128)),
        [smem()] * 2 + [vmem()] * 10,
        [part] * 5,
    )(meta, coef, u, a, u1, a1, v, rh, rg, own, u0p, a0p)

    rc = swap(zc, GZ, NZ_DEV, 0)
    rb = swap_open(zb, GZ, NZ_DEV)
    table = lax.all_to_all(traces, GZ + ("x",), 0, 0, tiled=True)

    u2, u0, w, gp, ep, a0f = call(
        wave_step,
        (block,) * 2 + (pltpu.HBM(block.shape, block.dtype),) * 3 + (frame,),
        [smem()] * 2 + [vmem()] * 10 + [smem()] * 3,
        [full] * 4,
    )(meta, coef, *hbm(u, a, u1, v), u0p, a0p, ut, at, rc, rb, src, amp, found)

    a2, a0, grad = call(
        adjoint_step,
        (block,) * 3,
        [smem()] * 2 + [vmem()] * 5 + [smem()] * 2,
        [full, pltpu.VMEM((CZ, CY, NX), jnp.float32)],
    )(meta, coef, *hbm(v), a0f, *hbm(w, gp, ep), found, table)
    return u2, u0, a2, a0, grad


def solution(mesh):
    fine = Mesh(mesh.devices.reshape(2, 8, 2, 4, 2), ("yl", "z", "c", "x", "yh"))
    field = P(GZ, GY, None)
    return jax.shard_map(
        shards,
        mesh=fine,
        in_specs=(field,) * 5 + (P(None, GZ + GY), P(), P(), P()),
        out_specs=(field,) * 5,
        check_vma=False,
    )
```

```python
import jax
import jax.numpy as jnp
import numpy as np
from jax import lax
from jax.experimental import pallas as pl
from jax.experimental.pallas import tpu as pltpu
from jax.sharding import Mesh
from jax.sharding import PartitionSpec as P

CENTRE = -7.5
NEAR = 4.0 / 3.0
FAR = -1.0 / 12.0
RATIO = 0.1
DAMP = 0.3

GZ = ("yl", "z", "c")
GY = ("xh", "xl", "yh")
O = 8
NZ_DEV, NY_DEV = 32, 8
CZ, CY, NX = 4, 32, 512
NZ, NY = NZ_DEV * CZ, NY_DEV * CY
FR = CY + 2 * O
VMEM_LIMIT = 8 * 1024 * 1024
ZROWS = 5 * CY + 8
GROUP = 4


def sponge_table():
    depth = np.arange(CZ + 1, dtype=np.float32) / np.float32(CZ)
    a = np.float32(DAMP) * (depth * depth)
    one = np.float32(1)
    return np.stack([one + a, one - a, one / (one - a), one / (one + a)]).astype(np.float32)


def sponge(z, which):
    into = jnp.minimum(jnp.maximum(jnp.maximum(CZ - z, z - (NZ - 1 - CZ)), 0), CZ)
    values = []
    for row in which:
        table = sponge_table()[row]
        value = jnp.float32(table[0])
        for k in range(1, CZ + 1):
            value = jnp.where(into == k, jnp.float32(table[k]), value)
        values.append(value)
    return values


def place_in_mesh():
    gz, gy = lax.axis_index(GZ), lax.axis_index(GY)
    return gz * CZ, gy * CY, lax.axis_index("yh"), lax.axis_index("c")


def smem():
    return pl.BlockSpec(memory_space=pltpu.SMEM)


def anywhere():
    return pl.BlockSpec(memory_space=pl.ANY)


def vmem():
    return pl.BlockSpec()


def x_terms(u):
    lane = lax.broadcasted_iota(jnp.int32, u.shape, 1)
    a = jnp.where(lane >= 1, pltpu.roll(u, 1, 1), 0.0)
    b = jnp.where(lane < NX - 1, pltpu.roll(u, NX - 1, 1), 0.0)
    c = jnp.where(lane >= 2, pltpu.roll(u, 2, 1), 0.0)
    d = jnp.where(lane < NX - 2, pltpu.roll(u, NX - 2, 1), 0.0)
    return a + b, c + d


def laplace(f, k, s):
    rows = lambda layer, shift: f[layer, s + shift : s + shift + 8, :]
    u = rows(k, 0)
    near, far = x_terms(u)
    near = near + ((rows(k, -1) + rows(k, 1)) + (rows(k - 1, 0) + rows(k + 1, 0)))
    far = far + ((rows(k, -2) + rows(k, 2)) + (rows(k - 2, 0) + rows(k + 2, 0)))
    return u, CENTRE * u + NEAR * near + FAR * far


def depth_factors(l):
    near_up = jnp.where(l >= 1, jnp.float32(NEAR), jnp.float32(0.0))
    near_dn = jnp.where(l < CZ - 1, jnp.float32(NEAR), jnp.float32(0.0))
    far_up = jnp.where(l >= 2, jnp.float32(FAR), jnp.float32(0.0))
    far_dn = jnp.where(l < CZ - 2, jnp.float32(FAR), jnp.float32(0.0))
    layers = jnp.maximum(l - 1, 0), jnp.minimum(l + 1, CZ - 1), jnp.maximum(l - 2, 0), jnp.minimum(l + 2, CZ - 1)
    return tuple(zip(layers, (near_up, near_dn, far_up, far_dn)))


def partial_laplace(f, l, s, size, factors):
    u = f[l, s : s + 8, :]

    def shifted(shift):
        if 0 <= s + shift and s + shift + 8 <= size:
            return f[l, s + shift : s + shift + 8, :]
        return pltpu.roll(u, (-shift) % 8, 0)

    near, far = x_terms(u)
    lap = CENTRE * u + NEAR * (near + (shifted(-1) + shifted(1))) + FAR * (far + (shifted(-2) + shifted(2)))
    for layer, factor in factors:
        lap = lap + factor * f[layer, s : s + 8, :]
    return u, lap


def pack_y(u, a, u1, a1, v, obs, h, g, own, first, last, obs_v, row, sem):
    _, y0, yh, _ = place_in_mesh()
    copies = []
    for i, ref in enumerate((u, a, u1, a1, v)):
        copies.append(pltpu.make_async_copy(ref.at[:, 0:8, :], first.at[i], sem.at[2 * i]))
        copies.append(pltpu.make_async_copy(ref.at[:, CY - 8 : CY, :], last.at[i], sem.at[2 * i + 1]))
    copies.append(pltpu.make_async_copy(obs, obs_v, sem.at[10]))
    for copy in copies:
        copy.start()
    for copy in copies:
        copy.wait()
    for k in range(4):
        for t in range(2):
            row[0:1, 32 * k + 16 * t : 32 * k + 16 * t + 16] = obs_v[t : t + 1, :]
    slot = lax.broadcasted_iota(jnp.int32, (1, 128), 1) >> 5
    mine = jnp.where(slot == ((y0 // CY) & 3), row[0:1, :], 0.0)
    own[...] = mine

    def pack(dst, high):
        rows = last if high else first
        four = slice(4, 8) if high else slice(0, 4)
        two = slice(6, 8) if high else slice(0, 2)
        dst[:, 0:4, :] = rows[0, :, four, :]
        dst[:, 4:8, :] = rows[1, :, four, :]
        dst[:, 8:10, :] = rows[2, :, two, :]
        dst[:, 10:12, :] = rows[3, :, two, :]
        dst[:, 12:14, :] = rows[4, :, two, :]
        dst[:, 14:16, :] = jnp.zeros((CZ, 2, NX), jnp.float32)
        dst[0, 14:15, 0:128] = mine

    @pl.when(yh == 0)
    def _():
        pack(h, True)
        pack(g, False)

    @pl.when(yh != 0)
    def _():
        pack(h, False)
        pack(g, True)


def pick_y(yh, rh, rg, low, high):
    @pl.when(yh == 0)
    def _():
        high(rh)
        low(rg)

    @pl.when(yh != 0)
    def _():
        low(rh)
        high(rg)


def own_step(u, a, u1, a1, v, u0p, a0p):
    z0, _, yh, core = place_in_mesh()

    def layer(l, carry):
        up, dn, iu, ia = sponge(z0 + l, range(4))
        factors = depth_factors(l)
        for s in range(0, CY, 8):
            y = slice(s, s + 8)
            c = v[l, y, :] * RATIO
            c = c * c
            p, lap = partial_laplace(u, l, s, CY, factors)
            u0p[l, y, :] = (2.0 * p - up * u1[l, y, :] + c * lap) * iu
            q, lap = partial_laplace(a, l, s, CY, factors)
            a0p[l, y, :] = (2.0 * q - dn * a1[l, y, :] + c * lap) * ia
        return carry

    lax.fori_loop(0, CZ, layer, 0)


def edge_step(
    u, a, u1, a1, v, rh, rg, u0p, a0p, ut, at, zc, zb,
    pu, pa, pu1, pa1, pv,
):
    z0, _, yh, core = place_in_mesh()
    pu[0, :, 4:8, :] = u[:, 0:4, :]
    pu[1, :, 0:4, :] = u[:, CY - 4 : CY, :]
    pa[0, :, 4:8, :] = a[:, 0:4, :]
    pa[1, :, 0:4, :] = a[:, CY - 4 : CY, :]
    for part, block in ((pu1, u1), (pa1, a1), (pv, v)):
        part[0, :, 4:6, :] = block[:, 0:2, :]
        part[1, :, 2:4, :] = block[:, CY - 2 : CY, :]

    def low(r):
        pu[0, :, 0:4, :] = r[:, 0:4, :]
        pa[0, :, 0:4, :] = r[:, 4:8, :]
        pu1[0, :, 2:4, :] = r[:, 8:10, :]
        pa1[0, :, 2:4, :] = r[:, 10:12, :]
        pv[0, :, 2:4, :] = r[:, 12:14, :]

    def high(r):
        pu[1, :, 4:8, :] = r[:, 0:4, :]
        pa[1, :, 4:8, :] = r[:, 4:8, :]
        pu1[1, :, 4:6, :] = r[:, 8:10, :]
        pa1[1, :, 4:6, :] = r[:, 10:12, :]
        pv[1, :, 4:6, :] = r[:, 12:14, :]

    pick_y(yh, rh, rg, low, high)

    def layer(l, carry):
        up, dn, iu, ia = sponge(z0 + l, range(4))
        factors = depth_factors(l)
        for side in range(2):
            c = pv[side, l] * RATIO
            c = c * c
            p, lap = partial_laplace(pu.at[side], l, 0, 8, factors)
            ut[side, l] = (2.0 * p - up * pu1[side, l] + c * lap) * iu
            q, lap = partial_laplace(pa.at[side], l, 0, 8, factors)
            at[side, l] = (2.0 * q - dn * pa1[side, l] + c * lap) * ia
        return carry

    lax.fori_loop(0, CZ, layer, 0)
    ut[0, :, 0:2, :] = pu[0, :, 2:4, :]
    ut[0, :, 6:8, :] = pv[0, :, 2:4, :]
    ut[1, :, 6:8, :] = pu[1, :, 4:6, :]
    ut[1, :, 0:2, :] = pv[1, :, 4:6, :]

    def pack(dst, l):
        m = slice(l, l + 2)
        dst[:, 0:CY, :] = u[m]
        dst[:, CY : 2 * CY, :] = a[m]
        dst[:, 4 * CY : 5 * CY, :] = v[m]
        for b, p, t in ((2 * CY, u0p, ut), (3 * CY, a0p, at)):
            dst[:, b : b + CY, :] = p[m]
            dst[:, b : b + 2, :] = t[0, m, 4:6, :]
            dst[:, b + CY - 2 : b + CY, :] = t[1, m, 2:4, :]
        b = 5 * CY
        dst[:, b : b + 2, :] = pu[0, m, 2:4, :]
        dst[:, b + 2 : b + 4, :] = pu[1, m, 4:6, :]
        dst[:, b + 4 : b + 6, :] = pa[0, m, 2:4, :]
        dst[:, b + 6 : b + 8, :] = pa[1, m, 4:6, :]

    @pl.when(core == 0)
    def _():
        pack(zc, 2)
        pack(zb, 0)

    @pl.when(core != 0)
    def _():
        pack(zc, 0)
        pack(zb, 2)


def list_receivers(rec, short, long, bits, words_v, codes_v, words, codes, found, sem):
    z0, y0, _, _ = place_in_mesh()
    lz = rec[0:1, :] - z0
    ly = ((rec[1:2, :] - y0 + 16) & (NY - 1)) - 16
    x = rec[2:3, :]
    own_z = (lz >= 0) & (lz < CZ)
    own_y = (ly >= 0) & (ly < CY)
    near = (lz >= -2) & (lz < CZ + 2) & (ly >= -2) & (ly < CY + 2) & (own_z | own_y)
    row = ly + O
    number = lax.broadcasted_iota(jnp.int32, lz.shape, 1)
    codes_v[...] = (
        ((row & 7) * 128 + (x & 127)) | ((x >> 7) << 10) | ((row >> 3) << 12) | ((lz + 2) << 15) | (number << 18)
    )
    m = near.astype(jnp.int32)
    for i in range(32):
        bits[i : i + 1, :] = m[:, 128 * i : 128 * i + 128] << i
    words_v[...] = jnp.sum(bits[...], axis=0, keepdims=True)
    copies = [pltpu.make_async_copy(codes_v, codes, sem.at[0]), pltpu.make_async_copy(words_v, words, sem.at[1])]
    for copy in copies:
        copy.start()
    for copy in copies:
        copy.wait()

    def word_step(w, count):
        def bit_step(carry):
            word, count = carry
            low = word & (-word)
            found[0, count + 1] = codes[0, (31 - lax.clz(low)) * 128 + w]
            return word ^ low, count + 1

        return lax.while_loop(lambda carry: carry[0] != 0, bit_step, (words[0, w], count))[1]

    count = lax.fori_loop(0, 128, word_step, 0)
    found[0, 0] = count
    for k in range(GROUP - 1):
        found[0, count + 1 + k] = 0
    copy = pltpu.make_async_copy(found.at[:, 0:128], short, sem.at[0])
    copy.start()
    copy.wait()

    @pl.when(count > 128 - GROUP)
    def _():
        copy = pltpu.make_async_copy(found, long, sem.at[1])
        copy.start()
        copy.wait()


def fetch_list(short, long, found, sem):
    copy = pltpu.make_async_copy(short, found.at[:, 0:128], sem)
    copy.start()

    def finish():
        copy.wait()

        @pl.when(found[0, 0] > 128 - GROUP)
        def _():
            rest = pltpu.make_async_copy(long, found, sem)
            rest.start()
            rest.wait()

    return finish


def cell_place():
    return lax.broadcasted_iota(jnp.int32, (8, 128), 0) * 128 + lax.broadcasted_iota(jnp.int32, (8, 128), 1)


def cell_at(place, layer, row, x):
    rows = pl.ds(pl.multiple_of((row >> 3) << 3, 8), 8)
    cols = pl.ds(pl.multiple_of((x >> 7) << 7, 128), 128)
    return (layer, rows, cols), place == ((row & 7) * 128 + (x & 127))


def wave_step(
    u, a, u1, v, u0p, a0p, ut, at, rc, rb, src, amp, short, long,
    u2, u0o, w, gp, ep, a0f,
    uf, u0f, af, vf, ef, sf, u1s, corners, u2s, ws, gs, found, sem, store_sem,
):
    e = O + CY
    z0, y0, yh, core = place_in_mesh()
    own = (slice(2, 6), slice(O, e), slice(None))
    into = [(u1, u1s), (u0p, u0f.at[own]), (a0p, a0f.at[own]), (u, uf.at[own]), (a, af.at[own]), (v, vf.at[own])]
    for j, r in enumerate((rc, rb)):
        k = 6 * (1 - core) if j == 0 else 6 * core
        for i, f in enumerate((uf, af, u0f, a0f, vf)):
            into.append((r.at[:, i * CY : (i + 1) * CY, :], f.at[pl.ds(k, 2), O:e, :]))
        into.append((r.at[:, 5 * CY : ZROWS, :], corners.at[j]))
    fetches = [pltpu.make_async_copy(part, whole, sem.at[i]) for i, (part, whole) in enumerate(into)]
    for fetch in fetches:
        fetch.start()
    finish = fetch_list(short, long, found, sem.at[len(into)])
    for l in range(CZ):
        sf[l] = jnp.zeros((CY, NX), jnp.float32)
    for fetch in fetches:
        fetch.wait()
    for f0, t in ((u0f, ut), (a0f, at)):
        f0[2:6, O - 2 : O + 2, :] = t[0, :, 2:6, :]
        f0[2:6, e - 2 : e + 2, :] = t[1, :, 2:6, :]
    uf[2:6, O - 2 : O, :] = ut[0, :, 0:2, :]
    uf[2:6, e : e + 2, :] = ut[1, :, 6:8, :]
    vf[2:6, O - 2 : O, :] = ut[0, :, 6:8, :]
    vf[2:6, e : e + 2, :] = ut[1, :, 0:2, :]

    def fill_corners(j, k):
        m = slice(k, k + 2)
        for i, f in enumerate((uf, af)):
            f[m, O - 2 : O, :] = corners[j, :, 4 * i : 4 * i + 2, :]
            f[m, e : e + 2, :] = corners[j, :, 4 * i + 2 : 4 * i + 4, :]

    @pl.when(core == 0)
    def _():
        fill_corners(1, 0)
        fill_corners(0, 6)

    @pl.when(core != 0)
    def _():
        fill_corners(0, 0)
        fill_corners(1, 6)

    lacks = ((0, None, 2), (1, 2, 3), (2, 1, 0), (3, None, 1), (4, None, 6), (5, 6, 7), (6, 5, 4), (7, None, 5))
    for k, near, far in lacks:
        edge = 2 <= k < 6
        iu, ia = sponge(z0 + k - 2, (2, 3))

        def rows(t, carry):
            s = pl.multiple_of(t * 8, 8)
            c = vf[k, pl.ds(s, 8), :] * RATIO
            c = c * c
            for f, f0, scale in ((uf, u0f, iu), (af, a0f, ia)):
                lap = FAR * f[far, pl.ds(s, 8), :]
                if near is not None:
                    lap = lap + NEAR * f[near, pl.ds(s, 8), :]
                f0[k, pl.ds(s, 8), :] = f0[k, pl.ds(s, 8), :] + (c * scale) * lap
            return carry

        first = O // 8
        lax.fori_loop(first - edge, first + CY // 8 + edge, rows, 0)

    place = cell_place()

    def add_source(i, carry):
        lz = src[0, i] - z0
        ly = ((src[1, i] - y0 + 16) & (NY - 1)) - 16
        own_z = (lz >= 0) & (lz < CZ)
        own_y = (ly >= 0) & (ly < CY)
        near = (lz >= -2) & (lz < CZ + 2) & (ly >= -2) & (ly < CY + 2) & (own_z | own_y)

        @pl.when(near)
        def _():
            at, hit = cell_at(place, lz + 2, ly + O, src[2, i])
            c = vf[at] * RATIO
            u0f[at] = u0f[at] + jnp.where(hit, (c * c) * (amp[0, i] * sponge(z0 + lz, (2,))[0]), 0.0)

        @pl.when(own_z & own_y)
        def _():
            at, hit = cell_at(place, lz, ly, src[2, i])
            sf[at] = sf[at] + jnp.where(hit, amp[1, i], 0.0)

        return carry

    lax.fori_loop(0, src.shape[1], add_source, 0)
    for l in range(CZ):
        ef[l + 2, O:e, :] = -sponge(z0 + l, (1,))[0] * af[l + 2, O:e, :]

    def sample(r, at, z, hit):
        a0f[at] = a0f[at] + jnp.where(hit, uf[at] * sponge(z0 + z - 2, (3,))[0], 0.0)
        ef[at] = ef[at] + jnp.where(hit, u0f[at], 0.0)

    finish()
    each_receiver(found, place, sample)

    stores = []
    for l in range(CZ):
        up, iu = sponge(z0 + l, (0, 2))
        for s in range(O, e, 8):
            y = slice(s - O, s - O + 8)
            vel = vf[l + 2, s : s + 8, :]
            c = vel * RATIO
            c = c * c
            un = uf[l + 2, s : s + 8, :]
            q, lap = laplace(u0f, l + 2, s)
            new = (2.0 * q - up * un + c * (lap + sf[l, y, :])) * iu
            u2s[l, y, :] = new
            slow = 2.0 / vel
            ws[l, y, :] = slow * (un - 2.0 * q + new)
            gs[l, y, :] = slow * af[l + 2, s : s + 8, :] * (u1s[l, y, :] - 2.0 * un + q)
        done = ((u2s.at[l], u2), (u0f.at[l + 2, O:e, :], u0o), (ws.at[l], w), (gs.at[l], gp), (ef.at[l + 2, O:e, :], ep))
        for i, (part, whole) in enumerate(done):
            stores.append(pltpu.make_async_copy(part, whole.at[l], store_sem.at[5 * l + i]))
            stores[-1].start()
    for store in stores:
        store.wait()


def each_receiver(found, place, one):
    count = found[0, 0]

    def group(b, carry):
        for k in range(GROUP):
            n = b * GROUP + k
            code = found[0, n + 1]
            z = (code >> 15) & 7
            rows = pl.ds(pl.multiple_of(((code >> 12) & 7) * 8, 8), 8)
            cols = pl.ds(pl.multiple_of(((code >> 10) & 3) * 128, 128), 128)
            one(code >> 18, (z, rows, cols), z, place == jnp.where(n < count, code & 1023, -1))
        return carry

    lax.fori_loop(0, (count + GROUP - 1) // GROUP, group, 0)


def adjoint_step(v, a0p, w, gp, ep, short, long, table, a2, a0o, grad, a0f, ef, vs, ws, gs, a2s, a0s, found, obs, sem):
    own = (slice(2, 6), slice(O, O + CY), slice(None))
    into = ((table, obs), (ep, ef.at[own]), (a0p, a0f), (v, vs), (w, ws), (gp, gs))
    fetches = [pltpu.make_async_copy(src, dst, sem.at[i]) for i, (src, dst) in enumerate(into)]
    finish = fetch_list(short, long, found, sem.at[6])
    for fetch in fetches:
        fetch.start()
    z0, _, _, _ = place_in_mesh()
    place = cell_place()
    finish()
    for fetch in fetches[:3]:
        fetch.wait()

    def subtract(r, at, z, hit):
        col = ((r >> 4) & 3) * 32 + (r & 15)
        first = obs[r >> 6, col] * sponge(z0 + z - 2, (3,))[0]
        second = obs[r >> 6, col + 16]
        a0f[at] = a0f[at] - jnp.where(hit, first, 0.0)
        ef[at] = ef[at] - jnp.where(hit, second, 0.0)

    each_receiver(found, place, subtract)
    for fetch in fetches[3:]:
        fetch.wait()

    stores = []
    for l in range(CZ):
        ia = sponge(z0 + l, (3,))[0]
        for s in range(O, O + CY, 8):
            y = slice(s - O, s - O + 8)
            c = vs[l, y, :] * RATIO
            c = c * c
            q, lap = laplace(a0f, l + 2, s)
            a2s[l, y, :] = (2.0 * q + ef[l + 2, s : s + 8, :] + c * lap) * ia
            a0s[l, y, :] = q
            gs[l, y, :] = gs[l, y, :] + ws[l, y, :] * q
        for i, (src, dst) in enumerate(((a2s, a2), (a0s, a0o), (gs, grad))):
            stores.append(pltpu.make_async_copy(src.at[l], dst.at[l], sem.at[7 + 3 * l + i]))
            stores[-1].start()
    for store in stores:
        store.wait()


def f32(*shape):
    return jax.ShapeDtypeStruct(shape, jnp.float32)


def hbm(*args):
    return tuple(pltpu.with_memory_space_constraint(x, pltpu.HBM) for x in args)


def call(kernel, out_shape, in_specs, scratch_shapes=(), out_specs=None):
    return pl.pallas_call(
        kernel,
        out_shape=out_shape,
        in_specs=in_specs,
        out_specs=tuple(out_specs) if out_specs else (vmem(),) * len(out_shape),
        scratch_shapes=scratch_shapes,
        compiler_params=pltpu.CompilerParams(vmem_limit_bytes=VMEM_LIMIT),
        name=kernel.__name__,
    )


def swap(value, axis, size, first):
    pairs = [(i, (first + ((i - first) % size ^ 1)) % size) for i in range(size)]
    return lax.ppermute(value, axis, pairs)


def swap_open(value, axis, size):
    pairs = [(i, i + 1) for i in range(1, size - 1, 2)]
    return lax.ppermute(value, axis, pairs + [(j, i) for i, j in pairs])


def shards(u, u1, a, a1, v, obs, rec, src, amp):
    assert u.shape == (CZ, CY, NX)
    block, edge = f32(CZ, CY, NX), f32(2, CZ, 8, NX)
    block_hbm = pltpu.HBM(block.shape, block.dtype)
    frame, zpack = f32(8, FR, NX), f32(2, ZROWS, NX)
    part = pltpu.VMEM((2, CZ, 8, NX), jnp.float32)
    full = pltpu.VMEM((8, FR, NX), jnp.float32)
    whole = pltpu.VMEM((CZ, CY, NX), jnp.float32)
    entries = rec.shape[1] + 128
    found_smem = pltpu.SMEM((1, entries), jnp.int32)
    dmas = lambda n: pltpu.SemaphoreType.DMA((n,))

    h, g, own = call(
        pack_y,
        (f32(CZ, 16, NX), f32(CZ, 16, NX), f32(1, 128)),
        [anywhere()] * 6,
        [pltpu.VMEM((5, CZ, 8, NX), jnp.float32)] * 2
        + [pltpu.VMEM((2, 16), jnp.float32), pltpu.VMEM((1, 128), jnp.float32), dmas(11)],
    )(*hbm(u, a, u1, a1, v, obs))
    rh = swap(h, GY, NY_DEV, 0)
    rg = swap(g, GY, NY_DEV, 1)
    two = own + rh[0, 14:15, 0:128]

    u0p, a0p = call(own_step, (block, block), [vmem()] * 5)(u, a, u1, a1, v)

    short, long = call(
        list_receivers,
        (jax.ShapeDtypeStruct((1, 128), jnp.int32), jax.ShapeDtypeStruct((1, entries), jnp.int32)),
        [vmem()],
        [
            pltpu.VMEM((32, 128), jnp.int32),
            pltpu.VMEM((1, 128), jnp.int32),
            pltpu.VMEM(rec[:1].shape, jnp.int32),
            pltpu.SMEM((1, 128), jnp.int32),
            pltpu.SMEM(rec[:1].shape, jnp.int32),
            found_smem,
            dmas(2),
        ],
        [anywhere()] * 2,
    )(rec)

    two, short, long = lax.optimization_barrier((two, short, long))
    four = two + swap(two, "xl", 2, 0)
    ut, at, zc, zb = call(
        edge_step,
        (edge,) * 2 + (pltpu.VMEM(zpack.shape, zpack.dtype),) * 2,
        [vmem()] * 9,
        [part] * 5,
    )(u, a, u1, a1, v, rh, rg, u0p, a0p)

    zc, zb, four = lax.optimization_barrier((zc, zb, four))
    rc = swap(zc, GZ, NZ_DEV, 0)
    rb = swap_open(zb, GZ, NZ_DEV)
    table = lax.all_to_all(jnp.broadcast_to(four, (64, 128)), GZ + ("xh",), 0, 0, tiled=True)

    u2, u0, w, gp, ep, a0f = call(
        wave_step,
        (block,) * 2 + (block_hbm,) * 3 + (frame,),
        [anywhere()] * 6 + [vmem()] * 2 + [anywhere()] * 2 + [smem()] * 2 + [anywhere()] * 2,
        [full] * 5
        + [whole] * 2
        + [pltpu.VMEM((2, 2, 8, NX), jnp.float32)]
        + [whole] * 3
        + [found_smem, dmas(19), dmas(20)],
        [anywhere()] * 5 + [vmem()],
    )(*hbm(u, a, u1, v), u0p, a0p, ut, at, *hbm(rc, rb, src, amp), short, long)

    a2, a0, grad = call(
        adjoint_step,
        (block,) * 3,
        [anywhere()] * 8,
        [full] * 2 + [whole] * 5 + [found_smem, pltpu.SMEM((64, 128), jnp.float32), dmas(19)],
        [anywhere()] * 3,
    )(*hbm(v), a0f, *hbm(w, gp, ep), short, long, table)
    return u2, u0, a2, a0, grad


def solution(mesh):
    fine = Mesh(mesh.devices.reshape(2, 8, 2, 2, 2, 2), ("yl", "z", "c", "xh", "xl", "yh"))
    field = P(GZ, GY, None)
    return jax.shard_map(
        shards,
        mesh=fine,
        in_specs=(field,) * 5 + (P(None, GZ + GY), P(), P(), P()),
        out_specs=(field,) * 5,
        check_vma=False,
    )
```

```python
import jax
import jax.numpy as jnp
import numpy as np
from jax import lax
from jax.experimental import pallas as pl
from jax.experimental.pallas import tpu as pltpu
from jax.sharding import Mesh
from jax.sharding import PartitionSpec as P

CENTRE = -7.5
NEAR = 4.0 / 3.0
FAR = -1.0 / 12.0
RATIO = 0.1
DAMP = 0.3

GZ = ("yl", "z", "c")
GY = ("xh", "xl", "yh")
O = 8
NZ_DEV, NY_DEV = 32, 8
CZ, CY, NX = 4, 32, 512
NZ, NY = NZ_DEV * CZ, NY_DEV * CY
FR = CY + 2 * O
VMEM_LIMIT = 8 * 1024 * 1024
ZROWS = 5 * CY + 8
GROUP = 4


def sponge_table():
    depth = np.arange(CZ + 1, dtype=np.float32) / np.float32(CZ)
    a = np.float32(DAMP) * (depth * depth)
    one = np.float32(1)
    return np.stack([one + a, one - a, one / (one - a), one / (one + a)]).astype(np.float32)


def sponge(z, which):
    into = jnp.minimum(jnp.maximum(jnp.maximum(CZ - z, z - (NZ - 1 - CZ)), 0), CZ)
    values = []
    for row in which:
        table = sponge_table()[row]
        value = jnp.float32(table[0])
        for k in range(1, CZ + 1):
            value = jnp.where(into == k, jnp.float32(table[k]), value)
        values.append(value)
    return values


def place_in_mesh():
    gz, gy = lax.axis_index(GZ), lax.axis_index(GY)
    return gz * CZ, gy * CY, lax.axis_index("yh"), lax.axis_index("c")


def smem():
    return pl.BlockSpec(memory_space=pltpu.SMEM)


def anywhere():
    return pl.BlockSpec(memory_space=pl.ANY)


def vmem():
    return pl.BlockSpec()


def x_terms(u):
    lane = lax.broadcasted_iota(jnp.int32, u.shape, 1)
    a = jnp.where(lane >= 1, pltpu.roll(u, 1, 1), 0.0)
    b = jnp.where(lane < NX - 1, pltpu.roll(u, NX - 1, 1), 0.0)
    c = jnp.where(lane >= 2, pltpu.roll(u, 2, 1), 0.0)
    d = jnp.where(lane < NX - 2, pltpu.roll(u, NX - 2, 1), 0.0)
    return a + b, c + d


def laplace(f, k, s):
    rows = lambda layer, shift: f[layer, s + shift : s + shift + 8, :]
    u = rows(k, 0)
    near, far = x_terms(u)
    near = near + ((rows(k, -1) + rows(k, 1)) + (rows(k - 1, 0) + rows(k + 1, 0)))
    far = far + ((rows(k, -2) + rows(k, 2)) + (rows(k - 2, 0) + rows(k + 2, 0)))
    return u, CENTRE * u + NEAR * near + FAR * far


def depth_factors(l):
    near_up = jnp.where(l >= 1, jnp.float32(NEAR), jnp.float32(0.0))
    near_dn = jnp.where(l < CZ - 1, jnp.float32(NEAR), jnp.float32(0.0))
    far_up = jnp.where(l >= 2, jnp.float32(FAR), jnp.float32(0.0))
    far_dn = jnp.where(l < CZ - 2, jnp.float32(FAR), jnp.float32(0.0))
    layers = jnp.maximum(l - 1, 0), jnp.minimum(l + 1, CZ - 1), jnp.maximum(l - 2, 0), jnp.minimum(l + 2, CZ - 1)
    return tuple(zip(layers, (near_up, near_dn, far_up, far_dn)))


def partial_laplace(f, l, s, factors):
    u = f[l, s : s + 8, :]
    row = lax.broadcasted_iota(jnp.int32, u.shape, 0) + s

    def shifted(shift):
        if 0 <= s + shift and s + shift + 8 <= CY:
            return f[l, s + shift : s + shift + 8, :]
        inside = (row + shift >= 0) & (row + shift < CY)
        return jnp.where(inside, pltpu.roll(u, (-shift) % 8, 0), 0.0)

    near, far = x_terms(u)
    lap = CENTRE * u + NEAR * (near + (shifted(-1) + shifted(1))) + FAR * (far + (shifted(-2) + shifted(2)))
    for layer, factor in factors:
        lap = lap + factor * f[layer, s : s + 8, :]
    return u, lap


def own_step(u_hbm, a_hbm, u1_hbm, a1_hbm, v_hbm, obs, u0p, a0p, h, g, own, u, a, u1, a1, v, obs_v, row, sem):
    z0, y0, yh, _ = place_in_mesh()
    into = ((u_hbm, u), (a_hbm, a), (u1_hbm, u1), (a1_hbm, a1), (v_hbm, v), (obs, obs_v))
    fetches = [pltpu.make_async_copy(src, dst, sem.at[i]) for i, (src, dst) in enumerate(into)]
    for fetch in fetches:
        fetch.start()
    for fetch in fetches:
        fetch.wait()
    for k in range(4):
        for t in range(2):
            row[0:1, 32 * k + 16 * t : 32 * k + 16 * t + 16] = obs_v[t : t + 1, :]
    slot = lax.broadcasted_iota(jnp.int32, (1, 128), 1) >> 5
    mine = jnp.where(slot == ((y0 // CY) & 3), row[0:1, :], 0.0)
    own[...] = mine

    def layer(l, carry):
        up, dn, iu, ia = sponge(z0 + l, range(4))
        factors = depth_factors(l)
        for s in range(0, CY, 8):
            y = slice(s, s + 8)
            c = v[l, y, :] * RATIO
            c = c * c
            p, lap = partial_laplace(u, l, s, factors)
            u0p[l, y, :] = (2.0 * p - up * u1[l, y, :] + c * lap) * iu
            q, lap = partial_laplace(a, l, s, factors)
            a0p[l, y, :] = (2.0 * q - dn * a1[l, y, :] + c * lap) * ia
        return carry

    lax.fori_loop(0, CZ, layer, 0)

    def pack(dst, high):
        two = slice(CY - 2, CY) if high else slice(0, 2)
        for i, f in enumerate((u, a, u0p, a0p)):
            dst[:, 2 * i : 2 * i + 2, 0:NX] = f[:, two, :]
        for i in range(4):
            dst[:, 2 * i : 2 * i + 2, NX : NX + 128] = v[:, two, 128 * i : 128 * i + 128]

    @pl.when(yh == 0)
    def _():
        pack(h, True)
        pack(g, False)

    @pl.when(yh != 0)
    def _():
        pack(h, False)
        pack(g, True)

    h[:, :, NX + 128 : NX + 256] = jnp.zeros((CZ, 8, 128), jnp.float32)
    h[0, 0:1, NX + 128 : NX + 256] = mine


def pick_y(yh, rh, rg, low, high):
    @pl.when(yh == 0)
    def _():
        high(rh)
        low(rg)

    @pl.when(yh != 0)
    def _():
        low(rh)
        high(rg)


def beyond(u):
    row = lax.broadcasted_iota(jnp.int32, u.shape, 0)
    near = jnp.where(row == 3, pltpu.roll(u, 7, 0), 0.0) + jnp.where(row == 4, pltpu.roll(u, 1, 0), 0.0)
    far = jnp.where(row < 4, pltpu.roll(u, 6, 0), pltpu.roll(u, 2, 0))
    return NEAR * near + FAR * far


def edge_step(u, a, v, rh, rg, u0p, a0p, ut, at, zc, zb, pu, pa, pv, pu0, pa0):
    z0, _, yh, core = place_in_mesh()
    parts = (pu, pa, pu0, pa0)
    for part, block in zip(parts + (pv,), (u, a, u0p, a0p, v)):
        part[0, :, 4:6, :] = block[:, 0:2, :]
        part[1, :, 2:4, :] = block[:, CY - 2 : CY, :]

    def received(r, side, first):
        rows = slice(first, first + 2)
        for i, part in enumerate(parts):
            part[side, :, rows, :] = r[:, 2 * i : 2 * i + 2, 0:NX]
        for i in range(4):
            pv[side, :, rows, 128 * i : 128 * i + 128] = r[:, 2 * i : 2 * i + 2, NX : NX + 128]

    pick_y(yh, rh, rg, lambda r: received(r, 0, 2), lambda r: received(r, 1, 4))

    def layer(l, carry):
        iu, ia = sponge(z0 + l, (2, 3))
        for side in range(2):
            c = pv[side, l] * RATIO
            c = c * c
            ut[side, l] = pu0[side, l] + (c * iu) * beyond(pu[side, l])
            at[side, l] = pa0[side, l] + (c * ia) * beyond(pa[side, l])
        return carry

    lax.fori_loop(0, CZ, layer, 0)
    ut[0, :, 0:2, :] = pu[0, :, 2:4, :]
    ut[0, :, 6:8, :] = pv[0, :, 2:4, :]
    ut[1, :, 6:8, :] = pu[1, :, 4:6, :]
    ut[1, :, 0:2, :] = pv[1, :, 4:6, :]

    def pack(dst, l):
        m = slice(l, l + 2)
        dst[:, 0:CY, :] = u[m]
        dst[:, CY : 2 * CY, :] = a[m]
        dst[:, 4 * CY : 5 * CY, :] = v[m]
        for b, p, t in ((2 * CY, u0p, ut), (3 * CY, a0p, at)):
            dst[:, b : b + CY, :] = p[m]
            dst[:, b : b + 2, :] = t[0, m, 4:6, :]
            dst[:, b + CY - 2 : b + CY, :] = t[1, m, 2:4, :]
        b = 5 * CY
        dst[:, b : b + 2, :] = pu[0, m, 2:4, :]
        dst[:, b + 2 : b + 4, :] = pu[1, m, 4:6, :]
        dst[:, b + 4 : b + 6, :] = pa[0, m, 2:4, :]
        dst[:, b + 6 : b + 8, :] = pa[1, m, 4:6, :]

    @pl.when(core == 0)
    def _():
        pack(zc, 2)
        pack(zb, 0)

    @pl.when(core != 0)
    def _():
        pack(zc, 0)
        pack(zb, 2)


def list_receivers(rec, short, long, bits, words_v, codes_v, words, codes, found, sem):
    z0, y0, _, _ = place_in_mesh()
    lz = rec[0:1, :] - z0
    ly = ((rec[1:2, :] - y0 + 16) & (NY - 1)) - 16
    x = rec[2:3, :]
    own_z = (lz >= 0) & (lz < CZ)
    own_y = (ly >= 0) & (ly < CY)
    near = (lz >= -2) & (lz < CZ + 2) & (ly >= -2) & (ly < CY + 2) & (own_z | own_y)
    row = ly + O
    number = lax.broadcasted_iota(jnp.int32, lz.shape, 1)
    codes_v[...] = (
        ((row & 7) * 128 + (x & 127)) | ((x >> 7) << 10) | ((row >> 3) << 12) | ((lz + 2) << 15) | (number << 18)
    )
    m = near.astype(jnp.int32)
    for i in range(32):
        bits[i : i + 1, :] = m[:, 128 * i : 128 * i + 128] << i
    words_v[...] = jnp.sum(bits[...], axis=0, keepdims=True)
    copies = [pltpu.make_async_copy(codes_v, codes, sem.at[0]), pltpu.make_async_copy(words_v, words, sem.at[1])]
    for copy in copies:
        copy.start()
    for copy in copies:
        copy.wait()

    def word_step(w, count):
        def bit_step(carry):
            word, count = carry
            low = word & (-word)
            found[0, count + 1] = codes[0, (31 - lax.clz(low)) * 128 + w]
            return word ^ low, count + 1

        return lax.while_loop(lambda carry: carry[0] != 0, bit_step, (words[0, w], count))[1]

    count = lax.fori_loop(0, 128, word_step, 0)
    found[0, 0] = count
    for k in range(GROUP - 1):
        found[0, count + 1 + k] = 0
    copy = pltpu.make_async_copy(found.at[:, 0:128], short, sem.at[0])
    copy.start()
    copy.wait()

    @pl.when(count > 128 - GROUP)
    def _():
        copy = pltpu.make_async_copy(found, long, sem.at[1])
        copy.start()
        copy.wait()


def fetch_list(short, long, found, sem):
    copy = pltpu.make_async_copy(short, found.at[:, 0:128], sem)
    copy.start()

    def finish():
        copy.wait()

        @pl.when(found[0, 0] > 128 - GROUP)
        def _():
            rest = pltpu.make_async_copy(long, found, sem)
            rest.start()
            rest.wait()

    return finish


def cell_place():
    return lax.broadcasted_iota(jnp.int32, (8, 128), 0) * 128 + lax.broadcasted_iota(jnp.int32, (8, 128), 1)


def cell_at(place, layer, row, x):
    rows = pl.ds(pl.multiple_of((row >> 3) << 3, 8), 8)
    cols = pl.ds(pl.multiple_of((x >> 7) << 7, 128), 128)
    return (layer, rows, cols), place == ((row & 7) * 128 + (x & 127))


def wave_step(
    u, a, u1, v, u0p, a0p, ut, at, rc, rb, src, amp, short, long,
    u2, u0o, w, gp, ep, a0f,
    uf, u0f, af, vf, ef, sf, u1s, corners, u2s, ws, gs, found, sem, store_sem,
):
    e = O + CY
    z0, y0, yh, core = place_in_mesh()
    own = (slice(2, 6), slice(O, e), slice(None))
    into = [(u1, u1s), (u0p, u0f.at[own]), (a0p, a0f.at[own]), (u, uf.at[own]), (a, af.at[own]), (v, vf.at[own])]
    for j, r in enumerate((rc, rb)):
        k = 6 * (1 - core) if j == 0 else 6 * core
        for i, f in enumerate((uf, af, u0f, a0f, vf)):
            into.append((r.at[:, i * CY : (i + 1) * CY, :], f.at[pl.ds(k, 2), O:e, :]))
        into.append((r.at[:, 5 * CY : ZROWS, :], corners.at[j]))
    fetches = [pltpu.make_async_copy(part, whole, sem.at[i]) for i, (part, whole) in enumerate(into)]
    for fetch in fetches:
        fetch.start()
    finish = fetch_list(short, long, found, sem.at[len(into)])
    for l in range(CZ):
        sf[l] = jnp.zeros((CY, NX), jnp.float32)
    for fetch in fetches:
        fetch.wait()
    for f0, t in ((u0f, ut), (a0f, at)):
        f0[2:6, O - 2 : O + 2, :] = t[0, :, 2:6, :]
        f0[2:6, e - 2 : e + 2, :] = t[1, :, 2:6, :]
    uf[2:6, O - 2 : O, :] = ut[0, :, 0:2, :]
    uf[2:6, e : e + 2, :] = ut[1, :, 6:8, :]
    vf[2:6, O - 2 : O, :] = ut[0, :, 6:8, :]
    vf[2:6, e : e + 2, :] = ut[1, :, 0:2, :]

    def fill_corners(j, k):
        m = slice(k, k + 2)
        for i, f in enumerate((uf, af)):
            f[m, O - 2 : O, :] = corners[j, :, 4 * i : 4 * i + 2, :]
            f[m, e : e + 2, :] = corners[j, :, 4 * i + 2 : 4 * i + 4, :]

    @pl.when(core == 0)
    def _():
        fill_corners(1, 0)
        fill_corners(0, 6)

    @pl.when(core != 0)
    def _():
        fill_corners(0, 0)
        fill_corners(1, 6)

    lacks = ((0, None, 2), (1, 2, 3), (2, 1, 0), (3, None, 1), (4, None, 6), (5, 6, 7), (6, 5, 4), (7, None, 5))
    for k, near, far in lacks:
        edge = 2 <= k < 6
        iu, ia = sponge(z0 + k - 2, (2, 3))

        def rows(t, carry):
            s = pl.multiple_of(t * 8, 8)
            c = vf[k, pl.ds(s, 8), :] * RATIO
            c = c * c
            for f, f0, scale in ((uf, u0f, iu), (af, a0f, ia)):
                lap = FAR * f[far, pl.ds(s, 8), :]
                if near is not None:
                    lap = lap + NEAR * f[near, pl.ds(s, 8), :]
                f0[k, pl.ds(s, 8), :] = f0[k, pl.ds(s, 8), :] + (c * scale) * lap
            return carry

        first = O // 8
        lax.fori_loop(first - edge, first + CY // 8 + edge, rows, 0)

    place = cell_place()

    def add_source(i, carry):
        lz = src[0, i] - z0
        ly = ((src[1, i] - y0 + 16) & (NY - 1)) - 16
        own_z = (lz >= 0) & (lz < CZ)
        own_y = (ly >= 0) & (ly < CY)
        near = (lz >= -2) & (lz < CZ + 2) & (ly >= -2) & (ly < CY + 2) & (own_z | own_y)

        @pl.when(near)
        def _():
            at, hit = cell_at(place, lz + 2, ly + O, src[2, i])
            c = vf[at] * RATIO
            u0f[at] = u0f[at] + jnp.where(hit, (c * c) * (amp[0, i] * sponge(z0 + lz, (2,))[0]), 0.0)

        @pl.when(own_z & own_y)
        def _():
            at, hit = cell_at(place, lz, ly, src[2, i])
            sf[at] = sf[at] + jnp.where(hit, amp[1, i], 0.0)

        return carry

    lax.fori_loop(0, src.shape[1], add_source, 0)
    for l in range(CZ):
        ef[l + 2, O:e, :] = -sponge(z0 + l, (1,))[0] * af[l + 2, O:e, :]

    def sample(r, at, z, hit):
        a0f[at] = a0f[at] + jnp.where(hit, uf[at] * sponge(z0 + z - 2, (3,))[0], 0.0)
        ef[at] = ef[at] + jnp.where(hit, u0f[at], 0.0)

    finish()
    each_receiver(found, place, sample)

    stores = []
    for l in range(CZ):
        up, iu = sponge(z0 + l, (0, 2))
        for s in range(O, e, 8):
            y = slice(s - O, s - O + 8)
            vel = vf[l + 2, s : s + 8, :]
            c = vel * RATIO
            c = c * c
            un = uf[l + 2, s : s + 8, :]
            q, lap = laplace(u0f, l + 2, s)
            new = (2.0 * q - up * un + c * (lap + sf[l, y, :])) * iu
            u2s[l, y, :] = new
            slow = 2.0 / vel
            ws[l, y, :] = slow * (un - 2.0 * q + new)
            gs[l, y, :] = slow * af[l + 2, s : s + 8, :] * (u1s[l, y, :] - 2.0 * un + q)
        done = ((u2s.at[l], u2), (u0f.at[l + 2, O:e, :], u0o), (ws.at[l], w), (gs.at[l], gp), (ef.at[l + 2, O:e, :], ep))
        for i, (part, whole) in enumerate(done):
            stores.append(pltpu.make_async_copy(part, whole.at[l], store_sem.at[5 * l + i]))
            stores[-1].start()
    for store in stores:
        store.wait()


def each_receiver(found, place, one):
    count = found[0, 0]

    def group(b, carry):
        for k in range(GROUP):
            n = b * GROUP + k
            code = found[0, n + 1]
            z = (code >> 15) & 7
            rows = pl.ds(pl.multiple_of(((code >> 12) & 7) * 8, 8), 8)
            cols = pl.ds(pl.multiple_of(((code >> 10) & 3) * 128, 128), 128)
            one(code >> 18, (z, rows, cols), z, place == jnp.where(n < count, code & 1023, -1))
        return carry

    lax.fori_loop(0, (count + GROUP - 1) // GROUP, group, 0)


def adjoint_step(v, a0p, w, gp, ep, short, long, table, a2, a0o, grad, a0f, ef, vs, ws, gs, a2s, a0s, found, obs, sem):
    own = (slice(2, 6), slice(O, O + CY), slice(None))
    into = ((table, obs), (ep, ef.at[own]), (a0p, a0f), (v, vs), (w, ws), (gp, gs))
    fetches = [pltpu.make_async_copy(src, dst, sem.at[i]) for i, (src, dst) in enumerate(into)]
    finish = fetch_list(short, long, found, sem.at[6])
    for fetch in fetches:
        fetch.start()
    z0, _, _, _ = place_in_mesh()
    place = cell_place()
    finish()
    for fetch in fetches[:3]:
        fetch.wait()

    def subtract(r, at, z, hit):
        col = ((r >> 4) & 3) * 32 + (r & 15)
        first = obs[r >> 6, col] * sponge(z0 + z - 2, (3,))[0]
        second = obs[r >> 6, col + 16]
        a0f[at] = a0f[at] - jnp.where(hit, first, 0.0)
        ef[at] = ef[at] - jnp.where(hit, second, 0.0)

    each_receiver(found, place, subtract)
    for fetch in fetches[3:]:
        fetch.wait()

    stores = []
    for l in range(CZ):
        ia = sponge(z0 + l, (3,))[0]
        for s in range(O, O + CY, 8):
            y = slice(s - O, s - O + 8)
            c = vs[l, y, :] * RATIO
            c = c * c
            q, lap = laplace(a0f, l + 2, s)
            a2s[l, y, :] = (2.0 * q + ef[l + 2, s : s + 8, :] + c * lap) * ia
            a0s[l, y, :] = q
            gs[l, y, :] = gs[l, y, :] + ws[l, y, :] * q
        for i, (src, dst) in enumerate(((a2s, a2), (a0s, a0o), (gs, grad))):
            stores.append(pltpu.make_async_copy(src.at[l], dst.at[l], sem.at[7 + 3 * l + i]))
            stores[-1].start()
    for store in stores:
        store.wait()


def f32(*shape):
    return jax.ShapeDtypeStruct(shape, jnp.float32)


def hbm(*args):
    return tuple(pltpu.with_memory_space_constraint(x, pltpu.HBM) for x in args)


def call(kernel, out_shape, in_specs, scratch_shapes=(), out_specs=None):
    return pl.pallas_call(
        kernel,
        out_shape=out_shape,
        in_specs=in_specs,
        out_specs=tuple(out_specs) if out_specs else (vmem(),) * len(out_shape),
        scratch_shapes=scratch_shapes,
        compiler_params=pltpu.CompilerParams(vmem_limit_bytes=VMEM_LIMIT),
        name=kernel.__name__,
    )


def swap(value, axis, size, first):
    pairs = [(i, (first + ((i - first) % size ^ 1)) % size) for i in range(size)]
    return lax.ppermute(value, axis, pairs)


def swap_open(value, axis, size):
    pairs = [(i, i + 1) for i in range(1, size - 1, 2)]
    return lax.ppermute(value, axis, pairs + [(j, i) for i, j in pairs])


def shards(u, u1, a, a1, v, obs, rec, src, amp):
    assert u.shape == (CZ, CY, NX)
    block, edge = f32(CZ, CY, NX), f32(2, CZ, 8, NX)
    block_hbm = pltpu.HBM(block.shape, block.dtype)
    frame, zpack = f32(8, FR, NX), f32(2, ZROWS, NX)
    part = pltpu.VMEM((2, CZ, 8, NX), jnp.float32)
    full = pltpu.VMEM((8, FR, NX), jnp.float32)
    whole = pltpu.VMEM((CZ, CY, NX), jnp.float32)
    entries = rec.shape[1] + 128
    found_smem = pltpu.SMEM((1, entries), jnp.int32)
    dmas = lambda n: pltpu.SemaphoreType.DMA((n,))

    u0p, a0p, h, g, own = call(
        own_step,
        (block, block, f32(CZ, 8, NX + 256), f32(CZ, 8, NX + 128), f32(1, 128)),
        [anywhere()] * 6,
        [whole] * 5 + [pltpu.VMEM((2, 16), jnp.float32), pltpu.VMEM((1, 128), jnp.float32), dmas(6)],
    )(*hbm(u, a, u1, a1, v, obs))
    rh = swap(h, GY, NY_DEV, 0)
    rg = swap(g, GY, NY_DEV, 1)
    two = own + rh[0, 0:1, NX + 128 : NX + 256]

    short, long = call(
        list_receivers,
        (jax.ShapeDtypeStruct((1, 128), jnp.int32), jax.ShapeDtypeStruct((1, entries), jnp.int32)),
        [vmem()],
        [
            pltpu.VMEM((32, 128), jnp.int32),
            pltpu.VMEM((1, 128), jnp.int32),
            pltpu.VMEM(rec[:1].shape, jnp.int32),
            pltpu.SMEM((1, 128), jnp.int32),
            pltpu.SMEM(rec[:1].shape, jnp.int32),
            found_smem,
            dmas(2),
        ],
        [anywhere()] * 2,
    )(rec)

    four = two + swap(two, "xl", 2, 0)
    ut, at, zc, zb = call(
        edge_step,
        (edge,) * 2 + (pltpu.VMEM(zpack.shape, zpack.dtype),) * 2,
        [vmem()] * 7,
        [part] * 5,
    )(u, a, v, rh, rg, u0p, a0p)

    zc, zb, four = lax.optimization_barrier((zc, zb, four))
    rc = swap(zc, GZ, NZ_DEV, 0)
    rb = swap_open(zb, GZ, NZ_DEV)
    table = lax.all_to_all(jnp.broadcast_to(four, (64, 128)), GZ + ("xh",), 0, 0, tiled=True)

    u2, u0, w, gp, ep, a0f = call(
        wave_step,
        (block,) * 2 + (block_hbm,) * 3 + (frame,),
        [anywhere()] * 6 + [vmem()] * 2 + [anywhere()] * 2 + [smem()] * 2 + [anywhere()] * 2,
        [full] * 5
        + [whole] * 2
        + [pltpu.VMEM((2, 2, 8, NX), jnp.float32)]
        + [whole] * 3
        + [found_smem, dmas(19), dmas(20)],
        [anywhere()] * 5 + [vmem()],
    )(*hbm(u, a, u1, v), u0p, a0p, ut, at, *hbm(rc, rb, src, amp), short, long)

    a2, a0, grad = call(
        adjoint_step,
        (block,) * 3,
        [anywhere()] * 8,
        [full] * 2 + [whole] * 5 + [found_smem, pltpu.SMEM((64, 128), jnp.float32), dmas(19)],
        [anywhere()] * 3,
    )(*hbm(v), a0f, *hbm(w, gp, ep), short, long, table)
    return u2, u0, a2, a0, grad


def solution(mesh):
    fine = Mesh(mesh.devices.reshape(2, 8, 2, 2, 2, 2), ("yl", "z", "c", "xh", "xl", "yh"))
    field = P(GZ, GY, None)
    return jax.shard_map(
        shards,
        mesh=fine,
        in_specs=(field,) * 5 + (P(None, GZ + GY), P(), P(), P()),
        out_specs=(field,) * 5,
        check_vma=False,
    )
```

```python
import jax
import jax.numpy as jnp
import numpy as np
from jax import lax
from jax.experimental import pallas as pl
from jax.experimental.pallas import tpu as pltpu
from jax.sharding import Mesh
from jax.sharding import PartitionSpec as P

CENTRE = -7.5
NEAR = 4.0 / 3.0
FAR = -1.0 / 12.0
RATIO = 0.1
DAMP = 0.3

GZ = ("yl", "z", "c")
GY = ("xh", "xl", "yh")
O = 8
NZ_DEV, NY_DEV = 32, 8
CZ, CY, NX = 4, 32, 512
NZ, NY = NZ_DEV * CZ, NY_DEV * CY
FR = CY + 2 * O
VMEM_LIMIT = 8 * 1024 * 1024
ZROWS = 5 * CY + 8
GROUP = 4


def sponge_table():
    depth = np.arange(CZ + 1, dtype=np.float32) / np.float32(CZ)
    a = np.float32(DAMP) * (depth * depth)
    one = np.float32(1)
    return np.stack([one + a, one - a, one / (one - a), one / (one + a)]).astype(np.float32)


def sponge(z, which):
    into = jnp.minimum(jnp.maximum(jnp.maximum(CZ - z, z - (NZ - 1 - CZ)), 0), CZ)
    values = []
    for row in which:
        table = sponge_table()[row]
        value = jnp.float32(table[0])
        for k in range(1, CZ + 1):
            value = jnp.where(into == k, jnp.float32(table[k]), value)
        values.append(value)
    return values


def place_in_mesh():
    gz, gy = lax.axis_index(GZ), lax.axis_index(GY)
    return gz * CZ, gy * CY, lax.axis_index("yh"), lax.axis_index("c")


def smem():
    return pl.BlockSpec(memory_space=pltpu.SMEM)


def anywhere():
    return pl.BlockSpec(memory_space=pl.ANY)


def vmem():
    return pl.BlockSpec()


def x_terms(u):
    lane = lax.broadcasted_iota(jnp.int32, u.shape, 1)
    a = jnp.where(lane >= 1, pltpu.roll(u, 1, 1), 0.0)
    b = jnp.where(lane < NX - 1, pltpu.roll(u, NX - 1, 1), 0.0)
    c = jnp.where(lane >= 2, pltpu.roll(u, 2, 1), 0.0)
    d = jnp.where(lane < NX - 2, pltpu.roll(u, NX - 2, 1), 0.0)
    return a + b, c + d


def laplace(f, k, s):
    rows = lambda layer, shift: f[layer, s + shift : s + shift + 8, :]
    u = rows(k, 0)
    near, far = x_terms(u)
    near = near + ((rows(k, -1) + rows(k, 1)) + (rows(k - 1, 0) + rows(k + 1, 0)))
    far = far + ((rows(k, -2) + rows(k, 2)) + (rows(k - 2, 0) + rows(k + 2, 0)))
    return u, CENTRE * u + NEAR * near + FAR * far


def depth_factors(l):
    near_up = jnp.where(l >= 1, jnp.float32(NEAR), jnp.float32(0.0))
    near_dn = jnp.where(l < CZ - 1, jnp.float32(NEAR), jnp.float32(0.0))
    far_up = jnp.where(l >= 2, jnp.float32(FAR), jnp.float32(0.0))
    far_dn = jnp.where(l < CZ - 2, jnp.float32(FAR), jnp.float32(0.0))
    layers = jnp.maximum(l - 1, 0), jnp.minimum(l + 1, CZ - 1), jnp.maximum(l - 2, 0), jnp.minimum(l + 2, CZ - 1)
    return tuple(zip(layers, (near_up, near_dn, far_up, far_dn)))


def partial_laplace(f, l, s, factors):
    u = f[l, s : s + 8, :]
    row = lax.broadcasted_iota(jnp.int32, u.shape, 0) + s

    def shifted(shift):
        if 0 <= s + shift and s + shift + 8 <= CY:
            return f[l, s + shift : s + shift + 8, :]
        inside = (row + shift >= 0) & (row + shift < CY)
        return jnp.where(inside, pltpu.roll(u, (-shift) % 8, 0), 0.0)

    near, far = x_terms(u)
    lap = CENTRE * u + NEAR * (near + (shifted(-1) + shifted(1))) + FAR * (far + (shifted(-2) + shifted(2)))
    for layer, factor in factors:
        lap = lap + factor * f[layer, s : s + 8, :]
    return u, lap


def outer_laplace(f, l, factors):
    u = f[l]
    row = lax.broadcasted_iota(jnp.int32, u.shape, 0)

    def shifted(shift):
        return jnp.where((row + shift >= 0) & (row + shift < 8), pltpu.roll(u, (-shift) % 8, 0), 0.0)

    near, far = x_terms(u)
    lap = CENTRE * u + NEAR * (near + (shifted(-1) + shifted(1))) + FAR * (far + (shifted(-2) + shifted(2)))
    for layer, factor in factors:
        lap = lap + factor * f[layer]
    return u, lap


def pack_y(u_hbm, a_hbm, u1_hbm, a1_hbm, v_hbm, obs, h, g, own, outer, both, first_step, obs_v, row, sem):
    z0, y0, yh, _ = place_in_mesh()
    fetches = [pltpu.make_async_copy(obs, obs_v, sem.at[10])]
    for i, f in enumerate((u_hbm, a_hbm, u1_hbm, a1_hbm, v_hbm)):
        fetches.append(pltpu.make_async_copy(f.at[:, 0:8, :], outer.at[0, i], sem.at[2 * i]))
        fetches.append(pltpu.make_async_copy(f.at[:, CY - 8 : CY, :], outer.at[1, i], sem.at[2 * i + 1]))
    for fetch in fetches:
        fetch.start()
    for fetch in fetches:
        fetch.wait()
    for k in range(4):
        for t in range(2):
            row[0:1, 32 * k + 16 * t : 32 * k + 16 * t + 16] = obs_v[t : t + 1, :]
    slot = lax.broadcasted_iota(jnp.int32, (1, 128), 1) >> 5
    mine = jnp.where(slot == ((y0 // CY) & 3), row[0:1, :], 0.0)
    own[...] = mine
    both[:, :, 0:4, :] = outer[0, :, :, 0:4, :]
    both[:, :, 4:8, :] = outer[1, :, :, 4:8, :]

    def layer(l, carry):
        up, dn, iu, ia = sponge(z0 + l, range(4))
        factors = depth_factors(l)
        c = both[4, l] * RATIO
        c = c * c
        p, lap = outer_laplace(both.at[0], l, factors)
        first_step[0, l] = (2.0 * p - up * both[2, l] + c * lap) * iu
        q, lap = outer_laplace(both.at[1], l, factors)
        first_step[1, l] = (2.0 * q - dn * both[3, l] + c * lap) * ia
        return carry

    lax.fori_loop(0, CZ, layer, 0)

    def pack(dst, side):
        two = slice(6, 8) if side else slice(0, 2)
        for i in range(2):
            dst[:, 2 * i : 2 * i + 2, 0:NX] = both[i, :, two, :]
            dst[:, 4 + 2 * i : 6 + 2 * i, 0:NX] = first_step[i, :, two, :]
        for i in range(4):
            dst[:, 2 * i : 2 * i + 2, NX : NX + 128] = both[4, :, two, 128 * i : 128 * i + 128]

    @pl.when(yh == 0)
    def _():
        pack(h, 1)
        pack(g, 0)

    @pl.when(yh != 0)
    def _():
        pack(h, 0)
        pack(g, 1)

    h[:, :, NX + 128 : NX + 256] = jnp.zeros((CZ, 8, 128), jnp.float32)
    h[0, 0:1, NX + 128 : NX + 256] = mine


def own_step(u, a, u1, a1, v, u0p, a0p):
    z0, _, _, _ = place_in_mesh()

    def layer(l, carry):
        up, dn, iu, ia = sponge(z0 + l, range(4))
        factors = depth_factors(l)
        for s in range(0, CY, 8):
            y = slice(s, s + 8)
            c = v[l, y, :] * RATIO
            c = c * c
            p, lap = partial_laplace(u, l, s, factors)
            u0p[l, y, :] = (2.0 * p - up * u1[l, y, :] + c * lap) * iu
            q, lap = partial_laplace(a, l, s, factors)
            a0p[l, y, :] = (2.0 * q - dn * a1[l, y, :] + c * lap) * ia
        return carry

    lax.fori_loop(0, CZ, layer, 0)


def pick_y(yh, rh, rg, low, high):
    @pl.when(yh == 0)
    def _():
        high(rh)
        low(rg)

    @pl.when(yh != 0)
    def _():
        low(rh)
        high(rg)


def beyond(u):
    row = lax.broadcasted_iota(jnp.int32, u.shape, 0)
    near = jnp.where(row == 3, pltpu.roll(u, 7, 0), 0.0) + jnp.where(row == 4, pltpu.roll(u, 1, 0), 0.0)
    far = jnp.where(row < 4, pltpu.roll(u, 6, 0), pltpu.roll(u, 2, 0))
    return NEAR * near + FAR * far


def edge_step(u, a, v, rh, rg, u0p, a0p, ut, at, zc, zb, pu, pa, pv, pu0, pa0):
    z0, _, yh, core = place_in_mesh()
    parts = (pu, pa, pu0, pa0)
    for part, block in zip(parts + (pv,), (u, a, u0p, a0p, v)):
        part[0, :, 4:6, :] = block[:, 0:2, :]
        part[1, :, 2:4, :] = block[:, CY - 2 : CY, :]

    def received(r, side, first):
        rows = slice(first, first + 2)
        for i, part in enumerate(parts):
            part[side, :, rows, :] = r[:, 2 * i : 2 * i + 2, 0:NX]
        for i in range(4):
            pv[side, :, rows, 128 * i : 128 * i + 128] = r[:, 2 * i : 2 * i + 2, NX : NX + 128]

    pick_y(yh, rh, rg, lambda r: received(r, 0, 2), lambda r: received(r, 1, 4))

    def layer(l, carry):
        iu, ia = sponge(z0 + l, (2, 3))
        for side in range(2):
            c = pv[side, l] * RATIO
            c = c * c
            ut[side, l] = pu0[side, l] + (c * iu) * beyond(pu[side, l])
            at[side, l] = pa0[side, l] + (c * ia) * beyond(pa[side, l])
        return carry

    lax.fori_loop(0, CZ, layer, 0)
    ut[0, :, 0:2, :] = pu[0, :, 2:4, :]
    ut[0, :, 6:8, :] = pv[0, :, 2:4, :]
    ut[1, :, 6:8, :] = pu[1, :, 4:6, :]
    ut[1, :, 0:2, :] = pv[1, :, 4:6, :]

    def pack(dst, l):
        m = slice(l, l + 2)
        dst[:, 0:CY, :] = u[m]
        dst[:, CY : 2 * CY, :] = a[m]
        dst[:, 4 * CY : 5 * CY, :] = v[m]
        for b, p, t in ((2 * CY, u0p, ut), (3 * CY, a0p, at)):
            dst[:, b : b + CY, :] = p[m]
            dst[:, b : b + 2, :] = t[0, m, 4:6, :]
            dst[:, b + CY - 2 : b + CY, :] = t[1, m, 2:4, :]
        b = 5 * CY
        dst[:, b : b + 2, :] = pu[0, m, 2:4, :]
        dst[:, b + 2 : b + 4, :] = pu[1, m, 4:6, :]
        dst[:, b + 4 : b + 6, :] = pa[0, m, 2:4, :]
        dst[:, b + 6 : b + 8, :] = pa[1, m, 4:6, :]

    @pl.when(core == 0)
    def _():
        pack(zc, 2)
        pack(zb, 0)

    @pl.when(core != 0)
    def _():
        pack(zc, 0)
        pack(zb, 2)


def list_receivers(rec, short, long, bits, words_v, codes_v, words, codes, found, sem):
    z0, y0, _, _ = place_in_mesh()
    lz = rec[0:1, :] - z0
    ly = ((rec[1:2, :] - y0 + 16) & (NY - 1)) - 16
    x = rec[2:3, :]
    own_z = (lz >= 0) & (lz < CZ)
    own_y = (ly >= 0) & (ly < CY)
    near = (lz >= -2) & (lz < CZ + 2) & (ly >= -2) & (ly < CY + 2) & (own_z | own_y)
    row = ly + O
    number = lax.broadcasted_iota(jnp.int32, lz.shape, 1)
    codes_v[...] = (
        ((row & 7) * 128 + (x & 127)) | ((x >> 7) << 10) | ((row >> 3) << 12) | ((lz + 2) << 15) | (number << 18)
    )
    m = near.astype(jnp.int32)
    for i in range(32):
        bits[i : i + 1, :] = m[:, 128 * i : 128 * i + 128] << i
    words_v[...] = jnp.sum(bits[...], axis=0, keepdims=True)
    copies = [pltpu.make_async_copy(codes_v, codes, sem.at[0]), pltpu.make_async_copy(words_v, words, sem.at[1])]
    for copy in copies:
        copy.start()
    for copy in copies:
        copy.wait()

    def word_step(w, count):
        def bit_step(carry):
            word, count = carry
            low = word & (-word)
            found[0, count + 1] = codes[0, (31 - lax.clz(low)) * 128 + w]
            return word ^ low, count + 1

        return lax.while_loop(lambda carry: carry[0] != 0, bit_step, (words[0, w], count))[1]

    count = lax.fori_loop(0, 128, word_step, 0)
    found[0, 0] = count
    for k in range(GROUP - 1):
        found[0, count + 1 + k] = 0
    copy = pltpu.make_async_copy(found.at[:, 0:128], short, sem.at[0])
    copy.start()
    copy.wait()

    @pl.when(count > 128 - GROUP)
    def _():
        copy = pltpu.make_async_copy(found, long, sem.at[1])
        copy.start()
        copy.wait()


def fetch_list(short, long, found, sem):
    copy = pltpu.make_async_copy(short, found.at[:, 0:128], sem)
    copy.start()

    def finish():
        copy.wait()

        @pl.when(found[0, 0] > 128 - GROUP)
        def _():
            rest = pltpu.make_async_copy(long, found, sem)
            rest.start()
            rest.wait()

    return finish


def cell_place():
    return lax.broadcasted_iota(jnp.int32, (8, 128), 0) * 128 + lax.broadcasted_iota(jnp.int32, (8, 128), 1)


def cell_at(place, layer, row, x):
    rows = pl.ds(pl.multiple_of((row >> 3) << 3, 8), 8)
    cols = pl.ds(pl.multiple_of((x >> 7) << 7, 128), 128)
    return (layer, rows, cols), place == ((row & 7) * 128 + (x & 127))


def wave_step(
    u, a, u1, v, u0p, a0p, ut, at, rc, rb, src, amp, short, long,
    u2, u0o, w, gp, ep, a0f,
    uf, u0f, af, vf, ef, sf, u1s, corners, u2s, ws, gs, found, scales, sem, store_sem,
):
    e = O + CY
    z0, y0, yh, core = place_in_mesh()
    own = (slice(2, 6), slice(O, e), slice(None))
    into = [(u1, u1s), (u0p, u0f.at[own]), (a0p, a0f.at[own]), (u, uf.at[own]), (a, af.at[own]), (v, vf.at[own])]
    for j, r in enumerate((rc, rb)):
        k = 6 * (1 - core) if j == 0 else 6 * core
        for i, f in enumerate((uf, af, u0f, a0f, vf)):
            into.append((r.at[:, i * CY : (i + 1) * CY, :], f.at[pl.ds(k, 2), O:e, :]))
        into.append((r.at[:, 5 * CY : ZROWS, :], corners.at[j]))
    fetches = [pltpu.make_async_copy(part, whole, sem.at[i]) for i, (part, whole) in enumerate(into)]
    for fetch in fetches:
        fetch.start()
    finish = fetch_list(short, long, found, sem.at[len(into)])
    for l in range(CZ):
        sf[l] = jnp.zeros((CY, NX), jnp.float32)
    for fetch in fetches:
        fetch.wait()
    for f0, t in ((u0f, ut), (a0f, at)):
        f0[2:6, O - 2 : O + 2, :] = t[0, :, 2:6, :]
        f0[2:6, e - 2 : e + 2, :] = t[1, :, 2:6, :]
    uf[2:6, O - 2 : O, :] = ut[0, :, 0:2, :]
    uf[2:6, e : e + 2, :] = ut[1, :, 6:8, :]
    vf[2:6, O - 2 : O, :] = ut[0, :, 6:8, :]
    vf[2:6, e : e + 2, :] = ut[1, :, 0:2, :]

    def fill_corners(j, k):
        m = slice(k, k + 2)
        for i, f in enumerate((uf, af)):
            f[m, O - 2 : O, :] = corners[j, :, 4 * i : 4 * i + 2, :]
            f[m, e : e + 2, :] = corners[j, :, 4 * i + 2 : 4 * i + 4, :]

    @pl.when(core == 0)
    def _():
        fill_corners(1, 0)
        fill_corners(0, 6)

    @pl.when(core != 0)
    def _():
        fill_corners(0, 0)
        fill_corners(1, 6)

    lacks = ((0, None, 2), (1, 2, 3), (2, 1, 0), (3, None, 1), (4, None, 6), (5, 6, 7), (6, 5, 4), (7, None, 5))
    for k, near, far in lacks:
        edge = 2 <= k < 6
        iu, ia = sponge(z0 + k - 2, (2, 3))

        def rows(t, carry):
            s = pl.multiple_of(t * 8, 8)
            c = vf[k, pl.ds(s, 8), :] * RATIO
            c = c * c
            for f, f0, scale in ((uf, u0f, iu), (af, a0f, ia)):
                lap = FAR * f[far, pl.ds(s, 8), :]
                if near is not None:
                    lap = lap + NEAR * f[near, pl.ds(s, 8), :]
                f0[k, pl.ds(s, 8), :] = f0[k, pl.ds(s, 8), :] + (c * scale) * lap
            return carry

        first = O // 8
        lax.fori_loop(first - edge, first + CY // 8 + edge, rows, 0)

    place = cell_place()

    def add_source(i, carry):
        lz = src[0, i] - z0
        ly = ((src[1, i] - y0 + 16) & (NY - 1)) - 16
        own_z = (lz >= 0) & (lz < CZ)
        own_y = (ly >= 0) & (ly < CY)
        near = (lz >= -2) & (lz < CZ + 2) & (ly >= -2) & (ly < CY + 2) & (own_z | own_y)

        @pl.when(near)
        def _():
            at, hit = cell_at(place, lz + 2, ly + O, src[2, i])
            c = vf[at] * RATIO
            u0f[at] = u0f[at] + jnp.where(hit, (c * c) * (amp[0, i] * sponge(z0 + lz, (2,))[0]), 0.0)

        @pl.when(own_z & own_y)
        def _():
            at, hit = cell_at(place, lz, ly, src[2, i])
            sf[at] = sf[at] + jnp.where(hit, amp[1, i], 0.0)

        return carry

    lax.fori_loop(0, src.shape[1], add_source, 0)
    for l in range(CZ):
        ef[l + 2, O:e, :] = -sponge(z0 + l, (1,))[0] * af[l + 2, O:e, :]

    def sample(r, at, z, hit):
        a0f[at] = a0f[at] + jnp.where(hit, uf[at] * scales[0, z], 0.0)
        ef[at] = ef[at] + jnp.where(hit, u0f[at], 0.0)

    for k in range(8):
        scales[0, k] = sponge(z0 + k - 2, (3,))[0]
    finish()
    each_receiver(found, place, sample)

    stores = []
    for l in range(CZ):
        up, iu = sponge(z0 + l, (0, 2))
        for s in range(O, e, 8):
            y = slice(s - O, s - O + 8)
            vel = vf[l + 2, s : s + 8, :]
            c = vel * RATIO
            c = c * c
            un = uf[l + 2, s : s + 8, :]
            q, lap = laplace(u0f, l + 2, s)
            new = (2.0 * q - up * un + c * (lap + sf[l, y, :])) * iu
            u2s[l, y, :] = new
            slow = 2.0 / vel
            ws[l, y, :] = slow * (un - 2.0 * q + new)
            gs[l, y, :] = slow * af[l + 2, s : s + 8, :] * (u1s[l, y, :] - 2.0 * un + q)
        done = ((u2s.at[l], u2), (u0f.at[l + 2, O:e, :], u0o), (ws.at[l], w), (gs.at[l], gp), (ef.at[l + 2, O:e, :], ep))
        for i, (part, whole) in enumerate(done):
            stores.append(pltpu.make_async_copy(part, whole.at[l], store_sem.at[5 * l + i]))
            stores[-1].start()
    for store in stores:
        store.wait()


def each_receiver(found, place, one):
    count = found[0, 0]

    def group(b, carry):
        for k in range(GROUP):
            n = b * GROUP + k
            code = found[0, n + 1]
            z = (code >> 15) & 7
            rows = pl.ds(pl.multiple_of(((code >> 12) & 7) * 8, 8), 8)
            cols = pl.ds(pl.multiple_of(((code >> 10) & 3) * 128, 128), 128)
            one(code >> 18, (z, rows, cols), z, place == jnp.where(n < count, code & 1023, -1))
        return carry

    lax.fori_loop(0, (count + GROUP - 1) // GROUP, group, 0)


def adjoint_step(v, a0p, w, gp, ep, short, long, table, a2, a0o, grad, a0f, ef, vs, ws, gs, a2s, a0s, found, obs, scales, sem):
    own = (slice(2, 6), slice(O, O + CY), slice(None))
    into = ((table, obs), (ep, ef.at[own]), (v, vs), (w, ws), (gp, gs))
    fetches = [pltpu.make_async_copy(src, dst, sem.at[i]) for i, (src, dst) in enumerate(into)]
    finish = fetch_list(short, long, found, sem.at[6])
    for fetch in fetches:
        fetch.start()
    z0, _, _, _ = place_in_mesh()
    place = cell_place()
    for k in range(8):
        scales[0, k] = sponge(z0 + k - 2, (3,))[0]
        a0f[k] = a0p[k]
    finish()
    for fetch in fetches[:2]:
        fetch.wait()

    def subtract(r, at, z, hit):
        col = ((r >> 4) & 3) * 32 + (r & 15)
        first = obs[r >> 6, col] * scales[0, z]
        second = obs[r >> 6, col + 16]
        a0f[at] = a0f[at] - jnp.where(hit, first, 0.0)
        ef[at] = ef[at] - jnp.where(hit, second, 0.0)

    each_receiver(found, place, subtract)
    for fetch in fetches[2:]:
        fetch.wait()

    stores = []
    for l in range(CZ):
        ia = sponge(z0 + l, (3,))[0]
        for s in range(O, O + CY, 8):
            y = slice(s - O, s - O + 8)
            c = vs[l, y, :] * RATIO
            c = c * c
            q, lap = laplace(a0f, l + 2, s)
            a2s[l, y, :] = (2.0 * q + ef[l + 2, s : s + 8, :] + c * lap) * ia
            a0s[l, y, :] = q
            gs[l, y, :] = gs[l, y, :] + ws[l, y, :] * q
        for i, (src, dst) in enumerate(((a2s, a2), (a0s, a0o), (gs, grad))):
            stores.append(pltpu.make_async_copy(src.at[l], dst.at[l], sem.at[7 + 3 * l + i]))
            stores[-1].start()
    for store in stores:
        store.wait()


def f32(*shape):
    return jax.ShapeDtypeStruct(shape, jnp.float32)


def hbm(*args):
    return tuple(pltpu.with_memory_space_constraint(x, pltpu.HBM) for x in args)


def call(kernel, out_shape, in_specs, scratch_shapes=(), out_specs=None):
    return pl.pallas_call(
        kernel,
        out_shape=out_shape,
        in_specs=in_specs,
        out_specs=tuple(out_specs) if out_specs else (vmem(),) * len(out_shape),
        scratch_shapes=scratch_shapes,
        compiler_params=pltpu.CompilerParams(vmem_limit_bytes=VMEM_LIMIT),
        name=kernel.__name__,
    )


def swap(value, axis, size, first):
    pairs = [(i, (first + ((i - first) % size ^ 1)) % size) for i in range(size)]
    return lax.ppermute(value, axis, pairs)


def swap_open(value, axis, size):
    pairs = [(i, i + 1) for i in range(1, size - 1, 2)]
    return lax.ppermute(value, axis, pairs + [(j, i) for i, j in pairs])


def shards(u, u1, a, a1, v, obs, rec, src, amp):
    assert u.shape == (CZ, CY, NX)
    block, edge = f32(CZ, CY, NX), f32(2, CZ, 8, NX)
    block_hbm = pltpu.HBM(block.shape, block.dtype)
    frame, zpack = f32(8, FR, NX), f32(2, ZROWS, NX)
    part = pltpu.VMEM((2, CZ, 8, NX), jnp.float32)
    full = pltpu.VMEM((8, FR, NX), jnp.float32)
    whole = pltpu.VMEM((CZ, CY, NX), jnp.float32)
    entries = rec.shape[1] + 128
    found_smem = pltpu.SMEM((1, entries), jnp.int32)
    eight_smem = pltpu.SMEM((1, 8), jnp.float32)
    dmas = lambda n: pltpu.SemaphoreType.DMA((n,))

    h, g, own = call(
        pack_y,
        (f32(CZ, 8, NX + 256), f32(CZ, 8, NX + 128), f32(1, 128)),
        [anywhere()] * 6,
        [pltpu.VMEM((2, 5, CZ, 8, NX), jnp.float32), pltpu.VMEM((5, CZ, 8, NX), jnp.float32), pltpu.VMEM((2, CZ, 8, NX), jnp.float32)]
        + [pltpu.VMEM((2, 16), jnp.float32), pltpu.VMEM((1, 128), jnp.float32), dmas(11)],
    )(*hbm(u, a, u1, a1, v, obs))
    rh = swap(h, GY, NY_DEV, 0)
    rg = swap(g, GY, NY_DEV, 1)
    two = own + rh[0, 0:1, NX + 128 : NX + 256]

    short, long = call(
        list_receivers,
        (jax.ShapeDtypeStruct((1, 128), jnp.int32), jax.ShapeDtypeStruct((1, entries), jnp.int32)),
        [vmem()],
        [
            pltpu.VMEM((32, 128), jnp.int32),
            pltpu.VMEM((1, 128), jnp.int32),
            pltpu.VMEM(rec[:1].shape, jnp.int32),
            pltpu.SMEM((1, 128), jnp.int32),
            pltpu.SMEM(rec[:1].shape, jnp.int32),
            found_smem,
            dmas(2),
        ],
        [anywhere()] * 2,
    )(rec)

    four = two + swap(two, "xl", 2, 0)
    u0p, a0p = call(own_step, (block, block), [vmem()] * 5)(u, a, u1, a1, v)
    ut, at, zc, zb = call(
        edge_step,
        (edge,) * 2 + (pltpu.VMEM(zpack.shape, zpack.dtype),) * 2,
        [vmem()] * 7,
        [part] * 5,
    )(u, a, v, rh, rg, u0p, a0p)

    zc, zb, four = lax.optimization_barrier((zc, zb, four))
    rc = swap(zc, GZ, NZ_DEV, 0)
    rb = swap_open(zb, GZ, NZ_DEV)
    table = lax.all_to_all(jnp.broadcast_to(four, (64, 128)), GZ + ("xh",), 0, 0, tiled=True)

    u2, u0, w, gp, ep, a0f = call(
        wave_step,
        (block,) * 2 + (block_hbm,) * 3 + (frame,),
        [anywhere()] * 6 + [vmem()] * 2 + [anywhere()] * 2 + [smem()] * 2 + [anywhere()] * 2,
        [full] * 5
        + [whole] * 2
        + [pltpu.VMEM((2, 2, 8, NX), jnp.float32)]
        + [whole] * 3
        + [found_smem, eight_smem, dmas(19), dmas(20)],
        [anywhere()] * 5 + [vmem()],
    )(*hbm(u, a, u1, v), u0p, a0p, ut, at, *hbm(rc, rb, src, amp), short, long)

    a2, a0, grad = call(
        adjoint_step,
        (block,) * 3,
        [anywhere(), vmem()] + [anywhere()] * 6,
        [full] * 2 + [whole] * 5 + [found_smem, pltpu.SMEM((64, 128), jnp.float32), eight_smem, dmas(19)],
        [anywhere()] * 3,
    )(*hbm(v), a0f, *hbm(w, gp, ep), short, long, table)
    return u2, u0, a2, a0, grad


def solution(mesh):
    fine = Mesh(mesh.devices.reshape(2, 8, 2, 2, 2, 2), ("yl", "z", "c", "xh", "xl", "yh"))
    field = P(GZ, GY, None)
    return jax.shard_map(
        shards,
        mesh=fine,
        in_specs=(field,) * 5 + (P(None, GZ + GY), P(), P(), P()),
        out_specs=(field,) * 5,
        check_vma=False,
    )
```

```python
import jax
import jax.numpy as jnp
import numpy as np
from jax import lax
from jax.experimental import pallas as pl
from jax.experimental.pallas import tpu as pltpu
from jax.sharding import Mesh
from jax.sharding import PartitionSpec as P

CENTRE = -7.5
NEAR = 4.0 / 3.0
FAR = -1.0 / 12.0
RATIO = 0.1
DAMP = 0.3

GZ = ("yl", "z", "c")
GY = ("x", "yh")
O = 8
NZ_DEV, NY_DEV = 32, 8
CZ, CY, NX = 4, 32, 512
NZ, NY = NZ_DEV * CZ, NY_DEV * CY
FR = CY + 2 * O
VMEM_LIMIT = 8 * 1024 * 1024
ZROWS = 5 * CY + 8
GROUP = 4


def sponge_table():
    depth = np.arange(CZ + 1, dtype=np.float32) / np.float32(CZ)
    a = np.float32(DAMP) * (depth * depth)
    one = np.float32(1)
    return np.stack([one + a, one - a, one / (one - a), one / (one + a)]).astype(np.float32)


def sponge(z, which):
    into = jnp.minimum(jnp.maximum(jnp.maximum(CZ - z, z - (NZ - 1 - CZ)), 0), CZ)
    values = []
    for row in which:
        table = sponge_table()[row]
        value = jnp.float32(table[0])
        for k in range(1, CZ + 1):
            value = jnp.where(into == k, jnp.float32(table[k]), value)
        values.append(value)
    return values


def place_in_mesh():
    gz, gy = lax.axis_index(GZ), lax.axis_index(GY)
    return gz * CZ, gy * CY, lax.axis_index("yh"), lax.axis_index("c")


def smem():
    return pl.BlockSpec(memory_space=pltpu.SMEM)


def anywhere():
    return pl.BlockSpec(memory_space=pl.ANY)


def vmem():
    return pl.BlockSpec()


def x_terms(u):
    lane = lax.broadcasted_iota(jnp.int32, u.shape, 1)
    a = jnp.where(lane >= 1, pltpu.roll(u, 1, 1), 0.0)
    b = jnp.where(lane < NX - 1, pltpu.roll(u, NX - 1, 1), 0.0)
    c = jnp.where(lane >= 2, pltpu.roll(u, 2, 1), 0.0)
    d = jnp.where(lane < NX - 2, pltpu.roll(u, NX - 2, 1), 0.0)
    return a + b, c + d


def laplace(f, k, s):
    rows = lambda layer, shift: f[layer, s + shift : s + shift + 8, :]
    u = rows(k, 0)
    near, far = x_terms(u)
    near = near + ((rows(k, -1) + rows(k, 1)) + (rows(k - 1, 0) + rows(k + 1, 0)))
    far = far + ((rows(k, -2) + rows(k, 2)) + (rows(k - 2, 0) + rows(k + 2, 0)))
    return u, CENTRE * u + NEAR * near + FAR * far


def depth_factors(l):
    near_up = jnp.where(l >= 1, jnp.float32(NEAR), jnp.float32(0.0))
    near_dn = jnp.where(l < CZ - 1, jnp.float32(NEAR), jnp.float32(0.0))
    far_up = jnp.where(l >= 2, jnp.float32(FAR), jnp.float32(0.0))
    far_dn = jnp.where(l < CZ - 2, jnp.float32(FAR), jnp.float32(0.0))
    layers = jnp.maximum(l - 1, 0), jnp.minimum(l + 1, CZ - 1), jnp.maximum(l - 2, 0), jnp.minimum(l + 2, CZ - 1)
    return tuple(zip(layers, (near_up, near_dn, far_up, far_dn)))


def partial_laplace(f, l, s, factors):
    u = f[l, s : s + 8, :]
    row = lax.broadcasted_iota(jnp.int32, u.shape, 0) + s

    def shifted(shift):
        if 0 <= s + shift and s + shift + 8 <= CY:
            return f[l, s + shift : s + shift + 8, :]
        inside = (row + shift >= 0) & (row + shift < CY)
        return jnp.where(inside, pltpu.roll(u, (-shift) % 8, 0), 0.0)

    near, far = x_terms(u)
    lap = CENTRE * u + NEAR * (near + (shifted(-1) + shifted(1))) + FAR * (far + (shifted(-2) + shifted(2)))
    for layer, factor in factors:
        lap = lap + factor * f[layer, s : s + 8, :]
    return u, lap


def outer_laplace(f, l, factors):
    u = f[l]
    row = lax.broadcasted_iota(jnp.int32, u.shape, 0)

    def shifted(shift):
        return jnp.where((row + shift >= 0) & (row + shift < 8), pltpu.roll(u, (-shift) % 8, 0), 0.0)

    near, far = x_terms(u)
    lap = CENTRE * u + NEAR * (near + (shifted(-1) + shifted(1))) + FAR * (far + (shifted(-2) + shifted(2)))
    for layer, factor in factors:
        lap = lap + factor * f[layer]
    return u, lap


def pack_y(u_hbm, a_hbm, u1_hbm, a1_hbm, v_hbm, obs, h, g, own, outer, both, first_step, obs_v, row, sem):
    z0, _, yh, core = place_in_mesh()
    fetches = [pltpu.make_async_copy(obs, obs_v, sem.at[10])]
    for i, f in enumerate((u_hbm, a_hbm, u1_hbm, a1_hbm, v_hbm)):
        fetches.append(pltpu.make_async_copy(f.at[:, 0:8, :], outer.at[0, i], sem.at[2 * i]))
        fetches.append(pltpu.make_async_copy(f.at[:, CY - 8 : CY, :], outer.at[1, i], sem.at[2 * i + 1]))
    for fetch in fetches:
        fetch.start()
    for fetch in fetches:
        fetch.wait()
    for k in range(4):
        for t in range(2):
            row[0:1, 32 * k + 16 * t : 32 * k + 16 * t + 16] = obs_v[t : t + 1, :]
    slot = lax.broadcasted_iota(jnp.int32, (1, 128), 1) >> 5
    mine = jnp.where(slot == core * 2 + yh, row[0:1, :], 0.0)
    own[...] = mine
    both[:, :, 0:4, :] = outer[0, :, :, 0:4, :]
    both[:, :, 4:8, :] = outer[1, :, :, 4:8, :]

    def layer(l, carry):
        up, dn, iu, ia = sponge(z0 + l, range(4))
        factors = depth_factors(l)
        c = both[4, l] * RATIO
        c = c * c
        p, lap = outer_laplace(both.at[0], l, factors)
        first_step[0, l] = (2.0 * p - up * both[2, l] + c * lap) * iu
        q, lap = outer_laplace(both.at[1], l, factors)
        first_step[1, l] = (2.0 * q - dn * both[3, l] + c * lap) * ia
        return carry

    lax.fori_loop(0, CZ, layer, 0)

    def pack(dst, side):
        two = slice(6, 8) if side else slice(0, 2)
        for i in range(2):
            dst[:, 2 * i : 2 * i + 2, 0:NX] = both[i, :, two, :]
            dst[:, 4 + 2 * i : 6 + 2 * i, 0:NX] = first_step[i, :, two, :]
        for i in range(4):
            dst[:, 2 * i : 2 * i + 2, NX : NX + 128] = both[4, :, two, 128 * i : 128 * i + 128]

    @pl.when(yh == 0)
    def _():
        pack(h, 1)
        pack(g, 0)

    @pl.when(yh != 0)
    def _():
        pack(h, 0)
        pack(g, 1)

    h[:, :, NX + 128 : NX + 256] = jnp.zeros((CZ, 8, 128), jnp.float32)
    h[0, 0:1, NX + 128 : NX + 256] = mine


def own_step(u, a, u1, a1, v, u0p, a0p):
    z0, _, _, _ = place_in_mesh()

    def layer(l, carry):
        up, dn, iu, ia = sponge(z0 + l, range(4))
        factors = depth_factors(l)
        for s in range(0, CY, 8):
            y = slice(s, s + 8)
            c = v[l, y, :] * RATIO
            c = c * c
            p, lap = partial_laplace(u, l, s, factors)
            u0p[l, y, :] = (2.0 * p - up * u1[l, y, :] + c * lap) * iu
            q, lap = partial_laplace(a, l, s, factors)
            a0p[l, y, :] = (2.0 * q - dn * a1[l, y, :] + c * lap) * ia
        return carry

    lax.fori_loop(0, CZ, layer, 0)


def pick_y(yh, rh, rg, low, high):
    @pl.when(yh == 0)
    def _():
        high(rh)
        low(rg)

    @pl.when(yh != 0)
    def _():
        low(rh)
        high(rg)


def beyond(u):
    row = lax.broadcasted_iota(jnp.int32, u.shape, 0)
    near = jnp.where(row == 3, pltpu.roll(u, 7, 0), 0.0) + jnp.where(row == 4, pltpu.roll(u, 1, 0), 0.0)
    far = jnp.where(row < 4, pltpu.roll(u, 6, 0), pltpu.roll(u, 2, 0))
    return NEAR * near + FAR * far


def edge_step(u, a, v, rh, rg, u0p, a0p, ut, at, zc, zb, pu, pa, pv, pu0, pa0):
    z0, _, yh, core = place_in_mesh()
    parts = (pu, pa, pu0, pa0)
    for part, block in zip(parts + (pv,), (u, a, u0p, a0p, v)):
        part[0, :, 4:6, :] = block[:, 0:2, :]
        part[1, :, 2:4, :] = block[:, CY - 2 : CY, :]

    def received(r, side, first):
        rows = slice(first, first + 2)
        for i, part in enumerate(parts):
            part[side, :, rows, :] = r[:, 2 * i : 2 * i + 2, 0:NX]
        for i in range(4):
            pv[side, :, rows, 128 * i : 128 * i + 128] = r[:, 2 * i : 2 * i + 2, NX : NX + 128]

    pick_y(yh, rh, rg, lambda r: received(r, 0, 2), lambda r: received(r, 1, 4))

    def layer(l, carry):
        iu, ia = sponge(z0 + l, (2, 3))
        for side in range(2):
            c = pv[side, l] * RATIO
            c = c * c
            ut[side, l] = pu0[side, l] + (c * iu) * beyond(pu[side, l])
            at[side, l] = pa0[side, l] + (c * ia) * beyond(pa[side, l])
        return carry

    lax.fori_loop(0, CZ, layer, 0)
    ut[0, :, 0:2, :] = pu[0, :, 2:4, :]
    ut[0, :, 6:8, :] = pv[0, :, 2:4, :]
    ut[1, :, 6:8, :] = pu[1, :, 4:6, :]
    ut[1, :, 0:2, :] = pv[1, :, 4:6, :]

    def pack(dst, l):
        m = slice(l, l + 2)
        dst[:, 0:CY, :] = u[m]
        dst[:, CY : 2 * CY, :] = a[m]
        dst[:, 4 * CY : 5 * CY, :] = v[m]
        for b, p, t in ((2 * CY, u0p, ut), (3 * CY, a0p, at)):
            dst[:, b : b + CY, :] = p[m]
            dst[:, b : b + 2, :] = t[0, m, 4:6, :]
            dst[:, b + CY - 2 : b + CY, :] = t[1, m, 2:4, :]
        b = 5 * CY
        dst[:, b : b + 2, :] = pu[0, m, 2:4, :]
        dst[:, b + 2 : b + 4, :] = pu[1, m, 4:6, :]
        dst[:, b + 4 : b + 6, :] = pa[0, m, 2:4, :]
        dst[:, b + 6 : b + 8, :] = pa[1, m, 4:6, :]

    @pl.when(core == 0)
    def _():
        pack(zc, 2)
        pack(zb, 0)

    @pl.when(core != 0)
    def _():
        pack(zc, 0)
        pack(zb, 2)


def list_receivers(rec, short, long, bits, words_v, codes_v, words, codes, found, sem):
    z0, y0, _, _ = place_in_mesh()
    lz = rec[0:1, :] - z0
    ly = ((rec[1:2, :] - y0 + 16) & (NY - 1)) - 16
    x = rec[2:3, :]
    own_z = (lz >= 0) & (lz < CZ)
    own_y = (ly >= 0) & (ly < CY)
    near = (lz >= -2) & (lz < CZ + 2) & (ly >= -2) & (ly < CY + 2) & (own_z | own_y)
    row = ly + O
    number = lax.broadcasted_iota(jnp.int32, lz.shape, 1)
    codes_v[...] = (
        ((row & 7) * 128 + (x & 127)) | ((x >> 7) << 10) | ((row >> 3) << 12) | ((lz + 2) << 15) | (number << 18)
    )
    m = near.astype(jnp.int32)
    for i in range(32):
        bits[i : i + 1, :] = m[:, 128 * i : 128 * i + 128] << i
    words_v[...] = jnp.sum(bits[...], axis=0, keepdims=True)
    copies = [pltpu.make_async_copy(codes_v, codes, sem.at[0]), pltpu.make_async_copy(words_v, words, sem.at[1])]
    for copy in copies:
        copy.start()
    for copy in copies:
        copy.wait()

    def word_step(w, count):
        def bit_step(carry):
            word, count = carry
            low = word & (-word)
            found[0, count + 1] = codes[0, (31 - lax.clz(low)) * 128 + w]
            return word ^ low, count + 1

        return lax.while_loop(lambda carry: carry[0] != 0, bit_step, (words[0, w], count))[1]

    count = lax.fori_loop(0, 128, word_step, 0, unroll=8)
    found[0, 0] = count
    for k in range(GROUP - 1):
        found[0, count + 1 + k] = 0
    copy = pltpu.make_async_copy(found.at[:, 0:128], short, sem.at[0])
    copy.start()
    copy.wait()

    @pl.when(count > 128 - GROUP)
    def _():
        copy = pltpu.make_async_copy(found, long, sem.at[1])
        copy.start()
        copy.wait()


def fetch_list(short, long, found, sem):
    copy = pltpu.make_async_copy(short, found.at[:, 0:128], sem)
    copy.start()

    def finish():
        copy.wait()

        @pl.when(found[0, 0] > 128 - GROUP)
        def _():
            rest = pltpu.make_async_copy(long, found, sem)
            rest.start()
            rest.wait()

    return finish


def cell_place():
    return lax.broadcasted_iota(jnp.int32, (8, 128), 0) * 128 + lax.broadcasted_iota(jnp.int32, (8, 128), 1)


def cell_at(place, layer, row, x):
    rows = pl.ds(pl.multiple_of((row >> 3) << 3, 8), 8)
    cols = pl.ds(pl.multiple_of((x >> 7) << 7, 128), 128)
    return (layer, rows, cols), place == ((row & 7) * 128 + (x & 127))


def wave_step(
    u, a, u1, v, u0p, a0p, ut, at, rc, rb, src, amp, short, long,
    u2, u0o, w, gp, ep, a0f,
    uf, u0f, af, vf, ef, sf, u1s, corners, u2s, ws, gs, found, scales, sem, store_sem,
):
    e = O + CY
    z0, y0, yh, core = place_in_mesh()
    own = (slice(2, 6), slice(O, e), slice(None))
    into = [(u1, u1s), (u0p, u0f.at[own]), (a0p, a0f.at[own]), (u, uf.at[own]), (a, af.at[own]), (v, vf.at[own])]
    for j, r in enumerate((rc, rb)):
        k = 6 * (1 - core) if j == 0 else 6 * core
        for i, f in enumerate((uf, af, u0f, a0f, vf)):
            into.append((r.at[:, i * CY : (i + 1) * CY, :], f.at[pl.ds(k, 2), O:e, :]))
        into.append((r.at[:, 5 * CY : ZROWS, :], corners.at[j]))
    fetches = [pltpu.make_async_copy(part, whole, sem.at[i]) for i, (part, whole) in enumerate(into)]
    for fetch in fetches:
        fetch.start()
    finish = fetch_list(short, long, found, sem.at[len(into)])
    for l in range(CZ):
        sf[l] = jnp.zeros((CY, NX), jnp.float32)
    for fetch in fetches:
        fetch.wait()
    for f0, t in ((u0f, ut), (a0f, at)):
        f0[2:6, O - 2 : O + 2, :] = t[0, :, 2:6, :]
        f0[2:6, e - 2 : e + 2, :] = t[1, :, 2:6, :]
    uf[2:6, O - 2 : O, :] = ut[0, :, 0:2, :]
    uf[2:6, e : e + 2, :] = ut[1, :, 6:8, :]
    vf[2:6, O - 2 : O, :] = ut[0, :, 6:8, :]
    vf[2:6, e : e + 2, :] = ut[1, :, 0:2, :]

    def fill_corners(j, k):
        m = slice(k, k + 2)
        for i, f in enumerate((uf, af)):
            f[m, O - 2 : O, :] = corners[j, :, 4 * i : 4 * i + 2, :]
            f[m, e : e + 2, :] = corners[j, :, 4 * i + 2 : 4 * i + 4, :]

    @pl.when(core == 0)
    def _():
        fill_corners(1, 0)
        fill_corners(0, 6)

    @pl.when(core != 0)
    def _():
        fill_corners(0, 0)
        fill_corners(1, 6)

    lacks = ((0, None, 2), (1, 2, 3), (2, 1, 0), (3, None, 1), (4, None, 6), (5, 6, 7), (6, 5, 4), (7, None, 5))
    for k, near, far in lacks:
        edge = 2 <= k < 6
        iu, ia = sponge(z0 + k - 2, (2, 3))

        def rows(t, carry):
            s = pl.multiple_of(t * 8, 8)
            c = vf[k, pl.ds(s, 8), :] * RATIO
            c = c * c
            for f, f0, scale in ((uf, u0f, iu), (af, a0f, ia)):
                lap = FAR * f[far, pl.ds(s, 8), :]
                if near is not None:
                    lap = lap + NEAR * f[near, pl.ds(s, 8), :]
                f0[k, pl.ds(s, 8), :] = f0[k, pl.ds(s, 8), :] + (c * scale) * lap
            return carry

        first = O // 8
        lax.fori_loop(first - edge, first + CY // 8 + edge, rows, 0)

    place = cell_place()

    def add_source(i, carry):
        lz = src[0, i] - z0
        ly = ((src[1, i] - y0 + 16) & (NY - 1)) - 16
        own_z = (lz >= 0) & (lz < CZ)
        own_y = (ly >= 0) & (ly < CY)
        near = (lz >= -2) & (lz < CZ + 2) & (ly >= -2) & (ly < CY + 2) & (own_z | own_y)

        @pl.when(near)
        def _():
            at, hit = cell_at(place, lz + 2, ly + O, src[2, i])
            c = vf[at] * RATIO
            u0f[at] = u0f[at] + jnp.where(hit, (c * c) * (amp[0, i] * sponge(z0 + lz, (2,))[0]), 0.0)

        @pl.when(own_z & own_y)
        def _():
            at, hit = cell_at(place, lz, ly, src[2, i])
            sf[at] = sf[at] + jnp.where(hit, amp[1, i], 0.0)

        return carry

    lax.fori_loop(0, src.shape[1], add_source, 0)
    for l in range(CZ):
        ef[l + 2, O:e, :] = -sponge(z0 + l, (1,))[0] * af[l + 2, O:e, :]

    def sample(r, at, z, hit):
        a0f[at] = a0f[at] + jnp.where(hit, uf[at] * scales[0, z], 0.0)
        ef[at] = ef[at] + jnp.where(hit, u0f[at], 0.0)

    for k in range(8):
        scales[0, k] = sponge(z0 + k - 2, (3,))[0]
    finish()
    each_receiver(found, place, sample)

    stores = []
    for l in range(CZ):
        up, iu = sponge(z0 + l, (0, 2))
        for s in range(O, e, 8):
            y = slice(s - O, s - O + 8)
            vel = vf[l + 2, s : s + 8, :]
            c = vel * RATIO
            c = c * c
            un = uf[l + 2, s : s + 8, :]
            q, lap = laplace(u0f, l + 2, s)
            new = (2.0 * q - up * un + c * (lap + sf[l, y, :])) * iu
            u2s[l, y, :] = new
            slow = 2.0 / vel
            ws[l, y, :] = slow * (un - 2.0 * q + new)
            gs[l, y, :] = slow * af[l + 2, s : s + 8, :] * (u1s[l, y, :] - 2.0 * un + q)
        done = ((u2s.at[l], u2), (u0f.at[l + 2, O:e, :], u0o), (ws.at[l], w), (gs.at[l], gp), (ef.at[l + 2, O:e, :], ep))
        for i, (part, whole) in enumerate(done):
            stores.append(pltpu.make_async_copy(part, whole.at[l], store_sem.at[5 * l + i]))
            stores[-1].start()
    for store in stores:
        store.wait()


def each_receiver(found, place, one):
    count = found[0, 0]

    def group(b, carry):
        for k in range(GROUP):
            n = b * GROUP + k
            code = found[0, n + 1]
            z = (code >> 15) & 7
            rows = pl.ds(pl.multiple_of(((code >> 12) & 7) * 8, 8), 8)
            cols = pl.ds(pl.multiple_of(((code >> 10) & 3) * 128, 128), 128)
            one(code >> 18, (z, rows, cols), z, place == jnp.where(n < count, code & 1023, -1))
        return carry

    lax.fori_loop(0, (count + GROUP - 1) // GROUP, group, 0)


def adjoint_step(v, a0p, w, gp, ep, short, long, table, a2, a0o, grad, a0f, ef, vs, ws, gs, a2s, a0s, found, obs, scales, sem):
    own = (slice(2, 6), slice(O, O + CY), slice(None))
    into = ((table, obs), (ep, ef.at[own]), (v, vs), (w, ws), (gp, gs))
    fetches = [pltpu.make_async_copy(src, dst, sem.at[i]) for i, (src, dst) in enumerate(into)]
    finish = fetch_list(short, long, found, sem.at[6])
    for fetch in fetches:
        fetch.start()
    z0, _, _, _ = place_in_mesh()
    place = cell_place()
    for k in range(8):
        scales[0, k] = sponge(z0 + k - 2, (3,))[0]
        a0f[k] = a0p[k]
    finish()
    for fetch in fetches[:2]:
        fetch.wait()

    def subtract(r, at, z, hit):
        slot = (r >> 8) * 4 + ((r >> 5) & 3)
        col = ((r >> 7) & 1) * 64 + ((r >> 4) & 1) * 32 + (r & 15)
        first = obs[slot, col] * scales[0, z]
        second = obs[slot, col + 16]
        a0f[at] = a0f[at] - jnp.where(hit, first, 0.0)
        ef[at] = ef[at] - jnp.where(hit, second, 0.0)

    each_receiver(found, place, subtract)
    for fetch in fetches[2:]:
        fetch.wait()

    stores = []
    for l in range(CZ):
        ia = sponge(z0 + l, (3,))[0]
        for s in range(O, O + CY, 8):
            y = slice(s - O, s - O + 8)
            c = vs[l, y, :] * RATIO
            c = c * c
            q, lap = laplace(a0f, l + 2, s)
            a2s[l, y, :] = (2.0 * q + ef[l + 2, s : s + 8, :] + c * lap) * ia
            a0s[l, y, :] = q
            gs[l, y, :] = gs[l, y, :] + ws[l, y, :] * q
        for i, (src, dst) in enumerate(((a2s, a2), (a0s, a0o), (gs, grad))):
            stores.append(pltpu.make_async_copy(src.at[l], dst.at[l], sem.at[7 + 3 * l + i]))
            stores[-1].start()
    for store in stores:
        store.wait()


def f32(*shape):
    return jax.ShapeDtypeStruct(shape, jnp.float32)


def hbm(*args):
    return tuple(pltpu.with_memory_space_constraint(x, pltpu.HBM) for x in args)


def call(kernel, out_shape, in_specs, scratch_shapes=(), out_specs=None):
    return pl.pallas_call(
        kernel,
        out_shape=out_shape,
        in_specs=in_specs,
        out_specs=tuple(out_specs) if out_specs else (vmem(),) * len(out_shape),
        scratch_shapes=scratch_shapes,
        compiler_params=pltpu.CompilerParams(vmem_limit_bytes=VMEM_LIMIT),
        name=kernel.__name__,
    )


def swap(value, axis, size, first):
    pairs = [(i, (first + ((i - first) % size ^ 1)) % size) for i in range(size)]
    return lax.ppermute(value, axis, pairs)


def swap_open(value, axis, size):
    pairs = [(i, i + 1) for i in range(1, size - 1, 2)]
    return lax.ppermute(value, axis, pairs + [(j, i) for i, j in pairs])


def shards(u, u1, a, a1, v, obs, rec, src, amp):
    assert u.shape == (CZ, CY, NX)
    block, edge = f32(CZ, CY, NX), f32(2, CZ, 8, NX)
    block_hbm = pltpu.HBM(block.shape, block.dtype)
    frame, zpack = f32(8, FR, NX), f32(2, ZROWS, NX)
    part = pltpu.VMEM((2, CZ, 8, NX), jnp.float32)
    full = pltpu.VMEM((8, FR, NX), jnp.float32)
    whole = pltpu.VMEM((CZ, CY, NX), jnp.float32)
    entries = rec.shape[1] + 128
    found_smem = pltpu.SMEM((1, entries), jnp.int32)
    eight_smem = pltpu.SMEM((1, 8), jnp.float32)
    dmas = lambda n: pltpu.SemaphoreType.DMA((n,))

    h, g, own = call(
        pack_y,
        (f32(CZ, 8, NX + 256), f32(CZ, 8, NX + 128), f32(1, 128)),
        [anywhere()] * 6,
        [pltpu.VMEM((2, 5, CZ, 8, NX), jnp.float32), pltpu.VMEM((5, CZ, 8, NX), jnp.float32), pltpu.VMEM((2, CZ, 8, NX), jnp.float32)]
        + [pltpu.VMEM((2, 16), jnp.float32), pltpu.VMEM((1, 128), jnp.float32), dmas(11)],
    )(*hbm(u, a, u1, a1, v, obs))
    rh = swap(h, GY, NY_DEV, 0)
    rg = swap(g, GY, NY_DEV, 1)
    two = own + rh[0, 0:1, NX + 128 : NX + 256]

    short, long = call(
        list_receivers,
        (jax.ShapeDtypeStruct((1, 128), jnp.int32), jax.ShapeDtypeStruct((1, entries), jnp.int32)),
        [vmem()],
        [
            pltpu.VMEM((32, 128), jnp.int32),
            pltpu.VMEM((1, 128), jnp.int32),
            pltpu.VMEM(rec[:1].shape, jnp.int32),
            pltpu.SMEM((1, 128), jnp.int32),
            pltpu.SMEM(rec[:1].shape, jnp.int32),
            found_smem,
            dmas(2),
        ],
        [anywhere()] * 2,
    )(rec)

    four = two + swap(two, "c", 2, 0)
    u0p, a0p = call(own_step, (block, block), [vmem()] * 5)(u, a, u1, a1, v)
    ut, at, zc, zb = call(
        edge_step,
        (edge,) * 2 + (pltpu.VMEM(zpack.shape, zpack.dtype),) * 2,
        [vmem()] * 7,
        [part] * 5,
    )(u, a, v, rh, rg, u0p, a0p)

    zc, zb, four = lax.optimization_barrier((zc, zb, four))
    rc = swap(zc, GZ, NZ_DEV, 0)
    rb = swap_open(zb, GZ, NZ_DEV)
    table = lax.all_to_all(jnp.broadcast_to(four, (64, 128)), ("yl", "z", "x"), 0, 0, tiled=True)

    u2, u0, w, gp, ep, a0f = call(
        wave_step,
        (block,) * 2 + (block_hbm,) * 3 + (frame,),
        [anywhere()] * 6 + [vmem()] * 2 + [anywhere()] * 2 + [smem()] * 2 + [anywhere()] * 2,
        [full] * 5
        + [whole] * 2
        + [pltpu.VMEM((2, 2, 8, NX), jnp.float32)]
        + [whole] * 3
        + [found_smem, eight_smem, dmas(19), dmas(20)],
        [anywhere()] * 5 + [vmem()],
    )(*hbm(u, a, u1, v), u0p, a0p, ut, at, *hbm(rc, rb, src, amp), short, long)

    a2, a0, grad = call(
        adjoint_step,
        (block,) * 3,
        [anywhere(), vmem()] + [anywhere()] * 6,
        [full] * 2 + [whole] * 5 + [found_smem, pltpu.SMEM((64, 128), jnp.float32), eight_smem, dmas(19)],
        [anywhere()] * 3,
    )(*hbm(v), a0f, *hbm(w, gp, ep), short, long, table)
    return u2, u0, a2, a0, grad


def solution(mesh):
    fine = Mesh(mesh.devices.reshape(2, 8, 2, 4, 2), ("yl", "z", "c", "x", "yh"))
    field = P(GZ, GY, None)
    return jax.shard_map(
        shards,
        mesh=fine,
        in_specs=(field,) * 5 + (P(None, GZ + GY), P(), P(), P()),
        out_specs=(field,) * 5,
        check_vma=False,
    )
```

```python
import jax
import jax.numpy as jnp
import numpy as np
from jax import lax
from jax.experimental import pallas as pl
from jax.experimental.pallas import tpu as pltpu
from jax.sharding import Mesh
from jax.sharding import PartitionSpec as P

CENTRE = -7.5
NEAR = 4.0 / 3.0
FAR = -1.0 / 12.0
RATIO = 0.1
DAMP = 0.3

GZ = ("yl", "z", "c")
GY = ("x", "yh")
O = 8
NZ_DEV, NY_DEV = 32, 8
CZ, CY, NX = 4, 32, 512
NZ, NY = NZ_DEV * CZ, NY_DEV * CY
FR = CY + 2 * O
VMEM_LIMIT = 8 * 1024 * 1024
ZROWS = 5 * CY + 8
YROWS = CZ * 5 * 8
GROUP = 4


def sponge_table():
    depth = np.arange(CZ + 1, dtype=np.float32) / np.float32(CZ)
    a = np.float32(DAMP) * (depth * depth)
    one = np.float32(1)
    return np.stack([one + a, one - a, one / (one - a), one / (one + a)]).astype(np.float32)


def sponge(z, which):
    into = jnp.minimum(jnp.maximum(jnp.maximum(CZ - z, z - (NZ - 1 - CZ)), 0), CZ)
    values = []
    for row in which:
        table = sponge_table()[row]
        value = jnp.float32(table[0])
        for k in range(1, CZ + 1):
            value = jnp.where(into == k, jnp.float32(table[k]), value)
        values.append(value)
    return values


def place_in_mesh():
    gz, gy = lax.axis_index(GZ), lax.axis_index(GY)
    return gz * CZ, gy * CY, lax.axis_index("yh"), lax.axis_index("c")


def smem():
    return pl.BlockSpec(memory_space=pltpu.SMEM)


def anywhere():
    return pl.BlockSpec(memory_space=pl.ANY)


def vmem():
    return pl.BlockSpec()


def x_terms(u):
    lane = lax.broadcasted_iota(jnp.int32, u.shape, 1)
    a = jnp.where(lane >= 1, pltpu.roll(u, 1, 1), 0.0)
    b = jnp.where(lane < NX - 1, pltpu.roll(u, NX - 1, 1), 0.0)
    c = jnp.where(lane >= 2, pltpu.roll(u, 2, 1), 0.0)
    d = jnp.where(lane < NX - 2, pltpu.roll(u, NX - 2, 1), 0.0)
    return a + b, c + d


def laplace(f, k, s):
    rows = lambda layer, shift: f[layer, s + shift : s + shift + 8, :]
    u = rows(k, 0)
    near, far = x_terms(u)
    near = near + ((rows(k, -1) + rows(k, 1)) + (rows(k - 1, 0) + rows(k + 1, 0)))
    far = far + ((rows(k, -2) + rows(k, 2)) + (rows(k - 2, 0) + rows(k + 2, 0)))
    return u, CENTRE * u + NEAR * near + FAR * far


def depth_factors(l):
    near_up = jnp.where(l >= 1, jnp.float32(NEAR), jnp.float32(0.0))
    near_dn = jnp.where(l < CZ - 1, jnp.float32(NEAR), jnp.float32(0.0))
    far_up = jnp.where(l >= 2, jnp.float32(FAR), jnp.float32(0.0))
    far_dn = jnp.where(l < CZ - 2, jnp.float32(FAR), jnp.float32(0.0))
    layers = jnp.maximum(l - 1, 0), jnp.minimum(l + 1, CZ - 1), jnp.maximum(l - 2, 0), jnp.minimum(l + 2, CZ - 1)
    return tuple(zip(layers, (near_up, near_dn, far_up, far_dn)))


def partial_laplace(f, l, s, factors):
    u = f[l, s : s + 8, :]
    row = lax.broadcasted_iota(jnp.int32, u.shape, 0) + s

    def shifted(shift):
        if 0 <= s + shift and s + shift + 8 <= CY:
            return f[l, s + shift : s + shift + 8, :]
        inside = (row + shift >= 0) & (row + shift < CY)
        return jnp.where(inside, pltpu.roll(u, (-shift) % 8, 0), 0.0)

    near, far = x_terms(u)
    lap = CENTRE * u + NEAR * (near + (shifted(-1) + shifted(1))) + FAR * (far + (shifted(-2) + shifted(2)))
    for layer, factor in factors:
        lap = lap + factor * f[layer, s : s + 8, :]
    return u, lap


def outer_laplace(f, l, factors):
    u = f[l]
    row = lax.broadcasted_iota(jnp.int32, u.shape, 0)

    def shifted(shift):
        return jnp.where((row + shift >= 0) & (row + shift < 8), pltpu.roll(u, (-shift) % 8, 0), 0.0)

    near, far = x_terms(u)
    lap = CENTRE * u + NEAR * (near + (shifted(-1) + shifted(1))) + FAR * (far + (shifted(-2) + shifted(2)))
    for layer, factor in factors:
        lap = lap + factor * f[layer]
    return u, lap


def pack_y(u_hbm, a_hbm, u1_hbm, a1_hbm, v_hbm, obs, h, g, own, outer, both, first_step, obs_v, row, sem):
    z0, _, yh, core = place_in_mesh()
    fetches = [pltpu.make_async_copy(obs, obs_v, sem.at[10])]
    for i, f in enumerate((u_hbm, a_hbm, u1_hbm, a1_hbm, v_hbm)):
        fetches.append(pltpu.make_async_copy(f.at[:, 0:8, :], outer.at[0, i], sem.at[2 * i]))
        fetches.append(pltpu.make_async_copy(f.at[:, CY - 8 : CY, :], outer.at[1, i], sem.at[2 * i + 1]))
    for fetch in fetches:
        fetch.start()
    for fetch in fetches:
        fetch.wait()
    for k in range(4):
        for t in range(2):
            row[0:1, 32 * k + 16 * t : 32 * k + 16 * t + 16] = obs_v[t : t + 1, :]
    slot = lax.broadcasted_iota(jnp.int32, (1, 128), 1) >> 5
    mine = jnp.where(slot == core * 2 + yh, row[0:1, :], 0.0)
    own[...] = mine
    both[:, :, 0:4, :] = outer[0, :, :, 0:4, :]
    both[:, :, 4:8, :] = outer[1, :, :, 4:8, :]

    def layer(l, carry):
        up, dn, iu, ia = sponge(z0 + l, range(4))
        factors = depth_factors(l)
        c = both[4, l] * RATIO
        c = c * c
        p, lap = outer_laplace(both.at[0], l, factors)
        first_step[0, l] = (2.0 * p - up * both[2, l] + c * lap) * iu
        q, lap = outer_laplace(both.at[1], l, factors)
        first_step[1, l] = (2.0 * q - dn * both[3, l] + c * lap) * ia
        return carry

    lax.fori_loop(0, CZ, layer, 0)

    def pack(dst, side):
        two = slice(6, 8) if side else slice(0, 2)
        for l in range(CZ):
            for t in range(5):
                b = 8 * (5 * l + t)
                for i in range(4):
                    if t == 4:
                        part = both[4, l, two, 128 * i : 128 * i + 128]
                    else:
                        f = both if i < 2 else first_step
                        part = f[i % 2, l, two, 128 * t : 128 * t + 128]
                    dst[b + 2 * i : b + 2 * i + 2, :] = part

    @pl.when(yh == 0)
    def _():
        pack(h, 1)
        pack(g, 0)

    @pl.when(yh != 0)
    def _():
        pack(h, 0)
        pack(g, 1)

    h[YROWS : YROWS + 8, :] = jnp.broadcast_to(mine, (8, 128))


def own_step(u, a, u1, a1, v, u0p, a0p):
    z0, _, _, _ = place_in_mesh()

    def layer(l, carry):
        up, dn, iu, ia = sponge(z0 + l, range(4))
        factors = depth_factors(l)
        for s in range(0, CY, 8):
            y = slice(s, s + 8)
            c = v[l, y, :] * RATIO
            c = c * c
            p, lap = partial_laplace(u, l, s, factors)
            u0p[l, y, :] = (2.0 * p - up * u1[l, y, :] + c * lap) * iu
            q, lap = partial_laplace(a, l, s, factors)
            a0p[l, y, :] = (2.0 * q - dn * a1[l, y, :] + c * lap) * ia
        return carry

    lax.fori_loop(0, CZ, layer, 0)


def pick_y(yh, rh, rg, low, high):
    @pl.when(yh == 0)
    def _():
        high(rh)
        low(rg)

    @pl.when(yh != 0)
    def _():
        low(rh)
        high(rg)


def beyond(u):
    row = lax.broadcasted_iota(jnp.int32, u.shape, 0)
    near = jnp.where(row == 3, pltpu.roll(u, 7, 0), 0.0) + jnp.where(row == 4, pltpu.roll(u, 1, 0), 0.0)
    far = jnp.where(row < 4, pltpu.roll(u, 6, 0), pltpu.roll(u, 2, 0))
    return NEAR * near + FAR * far


def edge_step(u, a, v, rh, rg, u0p, a0p, ut, at, zc, zb, pu, pa, pv, pu0, pa0):
    z0, _, yh, core = place_in_mesh()
    parts = (pu, pa, pu0, pa0)
    for part, block in zip(parts + (pv,), (u, a, u0p, a0p, v)):
        part[0, :, 4:6, :] = block[:, 0:2, :]
        part[1, :, 2:4, :] = block[:, CY - 2 : CY, :]

    def received(r, side, first):
        rows = slice(first, first + 2)
        for l in range(CZ):
            for t in range(5):
                b = 8 * (5 * l + t)
                for i in range(4):
                    part, k = (pv, i) if t == 4 else (parts[i], t)
                    part[side, l, rows, 128 * k : 128 * k + 128] = r[b + 2 * i : b + 2 * i + 2, :]

    pick_y(yh, rh, rg, lambda r: received(r, 0, 2), lambda r: received(r, 1, 4))

    def layer(l, carry):
        iu, ia = sponge(z0 + l, (2, 3))
        for side in range(2):
            c = pv[side, l] * RATIO
            c = c * c
            ut[side, l] = pu0[side, l] + (c * iu) * beyond(pu[side, l])
            at[side, l] = pa0[side, l] + (c * ia) * beyond(pa[side, l])
        return carry

    lax.fori_loop(0, CZ, layer, 0)
    ut[0, :, 0:2, :] = pu[0, :, 2:4, :]
    ut[0, :, 6:8, :] = pv[0, :, 2:4, :]
    ut[1, :, 6:8, :] = pu[1, :, 4:6, :]
    ut[1, :, 0:2, :] = pv[1, :, 4:6, :]

    def pack(dst, l):
        m = slice(l, l + 2)
        dst[:, 0:CY, :] = u[m]
        dst[:, CY : 2 * CY, :] = a[m]
        dst[:, 4 * CY : 5 * CY, :] = v[m]
        for b, p, t in ((2 * CY, u0p, ut), (3 * CY, a0p, at)):
            dst[:, b : b + CY, :] = p[m]
            dst[:, b : b + 2, :] = t[0, m, 4:6, :]
            dst[:, b + CY - 2 : b + CY, :] = t[1, m, 2:4, :]
        b = 5 * CY
        dst[:, b : b + 2, :] = pu[0, m, 2:4, :]
        dst[:, b + 2 : b + 4, :] = pu[1, m, 4:6, :]
        dst[:, b + 4 : b + 6, :] = pa[0, m, 2:4, :]
        dst[:, b + 6 : b + 8, :] = pa[1, m, 4:6, :]

    @pl.when(core == 0)
    def _():
        pack(zc, 2)
        pack(zb, 0)

    @pl.when(core != 0)
    def _():
        pack(zc, 0)
        pack(zb, 2)


def list_receivers(rec, short, long, bits, words_v, codes_v, words, codes, found, sem):
    z0, y0, _, _ = place_in_mesh()
    lz = rec[0:1, :] - z0
    ly = ((rec[1:2, :] - y0 + 16) & (NY - 1)) - 16
    x = rec[2:3, :]
    own_z = (lz >= 0) & (lz < CZ)
    own_y = (ly >= 0) & (ly < CY)
    near = (lz >= -2) & (lz < CZ + 2) & (ly >= -2) & (ly < CY + 2) & (own_z | own_y)
    row = ly + O
    number = lax.broadcasted_iota(jnp.int32, lz.shape, 1)
    codes_v[...] = (
        ((row & 7) * 128 + (x & 127)) | ((x >> 7) << 10) | ((row >> 3) << 12) | ((lz + 2) << 15) | (number << 18)
    )
    m = near.astype(jnp.int32)
    for i in range(32):
        bits[i : i + 1, :] = m[:, 128 * i : 128 * i + 128] << i
    words_v[...] = jnp.sum(bits[...], axis=0, keepdims=True)
    copies = [pltpu.make_async_copy(codes_v, codes, sem.at[0]), pltpu.make_async_copy(words_v, words, sem.at[1])]
    for copy in copies:
        copy.start()
    for copy in copies:
        copy.wait()

    def word_step(w, count):
        def bit_step(carry):
            word, count = carry
            low = word & (-word)
            found[0, count + 1] = codes[0, (31 - lax.clz(low)) * 128 + w]
            return word ^ low, count + 1

        return lax.while_loop(lambda carry: carry[0] != 0, bit_step, (words[0, w], count))[1]

    count = lax.fori_loop(0, 128, word_step, 0, unroll=8)
    found[0, 0] = count
    for k in range(GROUP - 1):
        found[0, count + 1 + k] = 0
    copy = pltpu.make_async_copy(found.at[:, 0:128], short, sem.at[0])
    copy.start()
    copy.wait()

    @pl.when(count > 128 - GROUP)
    def _():
        copy = pltpu.make_async_copy(found, long, sem.at[1])
        copy.start()
        copy.wait()


def fetch_list(short, long, found, sem):
    copy = pltpu.make_async_copy(short, found.at[:, 0:128], sem)
    copy.start()

    def finish():
        copy.wait()

        @pl.when(found[0, 0] > 128 - GROUP)
        def _():
            rest = pltpu.make_async_copy(long, found, sem)
            rest.start()
            rest.wait()

    return finish


def cell_place():
    return lax.broadcasted_iota(jnp.int32, (8, 128), 0) * 128 + lax.broadcasted_iota(jnp.int32, (8, 128), 1)


def cell_at(place, layer, row, x):
    rows = pl.ds(pl.multiple_of((row >> 3) << 3, 8), 8)
    cols = pl.ds(pl.multiple_of((x >> 7) << 7, 128), 128)
    return (layer, rows, cols), place == ((row & 7) * 128 + (x & 127))


def wave_step(
    u, a, u1, v, u0p, a0p, ut, at, rc, rb, src, amp, short, long,
    u2, u0o, w, gp, ep, a0f,
    uf, u0f, af, vf, ef, sf, u1s, corners, u2s, ws, gs, found, scales, sem, store_sem,
):
    e = O + CY
    z0, y0, yh, core = place_in_mesh()
    own = (slice(2, 6), slice(O, e), slice(None))
    into = [(u1, u1s), (u0p, u0f.at[own]), (a0p, a0f.at[own]), (u, uf.at[own]), (a, af.at[own]), (v, vf.at[own])]
    for j, r in enumerate((rc, rb)):
        k = 6 * (1 - core) if j == 0 else 6 * core
        for i, f in enumerate((uf, af, u0f, a0f, vf)):
            into.append((r.at[:, i * CY : (i + 1) * CY, :], f.at[pl.ds(k, 2), O:e, :]))
        into.append((r.at[:, 5 * CY : ZROWS, :], corners.at[j]))
    fetches = [pltpu.make_async_copy(part, whole, sem.at[i]) for i, (part, whole) in enumerate(into)]
    for fetch in fetches:
        fetch.start()
    finish = fetch_list(short, long, found, sem.at[len(into)])
    for l in range(CZ):
        sf[l] = jnp.zeros((CY, NX), jnp.float32)
    for fetch in fetches:
        fetch.wait()
    for f0, t in ((u0f, ut), (a0f, at)):
        f0[2:6, O - 2 : O + 2, :] = t[0, :, 2:6, :]
        f0[2:6, e - 2 : e + 2, :] = t[1, :, 2:6, :]
    uf[2:6, O - 2 : O, :] = ut[0, :, 0:2, :]
    uf[2:6, e : e + 2, :] = ut[1, :, 6:8, :]
    vf[2:6, O - 2 : O, :] = ut[0, :, 6:8, :]
    vf[2:6, e : e + 2, :] = ut[1, :, 0:2, :]

    def fill_corners(j, k):
        m = slice(k, k + 2)
        for i, f in enumerate((uf, af)):
            f[m, O - 2 : O, :] = corners[j, :, 4 * i : 4 * i + 2, :]
            f[m, e : e + 2, :] = corners[j, :, 4 * i + 2 : 4 * i + 4, :]

    @pl.when(core == 0)
    def _():
        fill_corners(1, 0)
        fill_corners(0, 6)

    @pl.when(core != 0)
    def _():
        fill_corners(0, 0)
        fill_corners(1, 6)

    lacks = ((0, None, 2), (1, 2, 3), (2, 1, 0), (3, None, 1), (4, None, 6), (5, 6, 7), (6, 5, 4), (7, None, 5))
    for k, near, far in lacks:
        edge = 2 <= k < 6
        iu, ia = sponge(z0 + k - 2, (2, 3))

        def rows(t, carry):
            s = pl.multiple_of(t * 8, 8)
            c = vf[k, pl.ds(s, 8), :] * RATIO
            c = c * c
            for f, f0, scale in ((uf, u0f, iu), (af, a0f, ia)):
                lap = FAR * f[far, pl.ds(s, 8), :]
                if near is not None:
                    lap = lap + NEAR * f[near, pl.ds(s, 8), :]
                f0[k, pl.ds(s, 8), :] = f0[k, pl.ds(s, 8), :] + (c * scale) * lap
            return carry

        first = O // 8
        lax.fori_loop(first - edge, first + CY // 8 + edge, rows, 0)

    place = cell_place()

    def add_source(i, carry):
        lz = src[0, i] - z0
        ly = ((src[1, i] - y0 + 16) & (NY - 1)) - 16
        own_z = (lz >= 0) & (lz < CZ)
        own_y = (ly >= 0) & (ly < CY)
        near = (lz >= -2) & (lz < CZ + 2) & (ly >= -2) & (ly < CY + 2) & (own_z | own_y)

        @pl.when(near)
        def _():
            at, hit = cell_at(place, lz + 2, ly + O, src[2, i])
            c = vf[at] * RATIO
            u0f[at] = u0f[at] + jnp.where(hit, (c * c) * (amp[0, i] * sponge(z0 + lz, (2,))[0]), 0.0)

        @pl.when(own_z & own_y)
        def _():
            at, hit = cell_at(place, lz, ly, src[2, i])
            sf[at] = sf[at] + jnp.where(hit, amp[1, i], 0.0)

        return carry

    lax.fori_loop(0, src.shape[1], add_source, 0)
    for l in range(CZ):
        ef[l + 2, O:e, :] = -sponge(z0 + l, (1,))[0] * af[l + 2, O:e, :]

    def sample(r, at, z, hit):
        a0f[at] = a0f[at] + jnp.where(hit, uf[at] * scales[0, z], 0.0)
        ef[at] = ef[at] + jnp.where(hit, u0f[at], 0.0)

    for k in range(8):
        scales[0, k] = sponge(z0 + k - 2, (3,))[0]
    finish()
    each_receiver(found, place, sample)

    stores = []
    for l in range(CZ):
        up, iu = sponge(z0 + l, (0, 2))
        for s in range(O, e, 8):
            y = slice(s - O, s - O + 8)
            vel = vf[l + 2, s : s + 8, :]
            c = vel * RATIO
            c = c * c
            un = uf[l + 2, s : s + 8, :]
            q, lap = laplace(u0f, l + 2, s)
            new = (2.0 * q - up * un + c * (lap + sf[l, y, :])) * iu
            u2s[l, y, :] = new
            slow = 2.0 / vel
            ws[l, y, :] = slow * (un - 2.0 * q + new)
            gs[l, y, :] = slow * af[l + 2, s : s + 8, :] * (u1s[l, y, :] - 2.0 * un + q)
        done = ((u2s.at[l], u2), (u0f.at[l + 2, O:e, :], u0o), (ws.at[l], w), (gs.at[l], gp), (ef.at[l + 2, O:e, :], ep))
        for i, (part, whole) in enumerate(done):
            stores.append(pltpu.make_async_copy(part, whole.at[l], store_sem.at[5 * l + i]))
            stores[-1].start()
    for store in stores:
        store.wait()


def each_receiver(found, place, one):
    count = found[0, 0]

    def group(b, carry):
        for k in range(GROUP):
            n = b * GROUP + k
            code = found[0, n + 1]
            z = (code >> 15) & 7
            rows = pl.ds(pl.multiple_of(((code >> 12) & 7) * 8, 8), 8)
            cols = pl.ds(pl.multiple_of(((code >> 10) & 3) * 128, 128), 128)
            one(code >> 18, (z, rows, cols), z, place == jnp.where(n < count, code & 1023, -1))
        return carry

    lax.fori_loop(0, (count + GROUP - 1) // GROUP, group, 0)


def adjoint_step(v, a0p, w, gp, ep, short, long, table, a2, a0o, grad, a0f, ef, vs, ws, gs, a2s, a0s, found, obs, scales, sem):
    own = (slice(2, 6), slice(O, O + CY), slice(None))
    into = ((table, obs), (ep, ef.at[own]), (v, vs), (w, ws), (gp, gs))
    fetches = [pltpu.make_async_copy(src, dst, sem.at[i]) for i, (src, dst) in enumerate(into)]
    finish = fetch_list(short, long, found, sem.at[6])
    for fetch in fetches:
        fetch.start()
    z0, _, _, _ = place_in_mesh()
    place = cell_place()
    for k in range(8):
        scales[0, k] = sponge(z0 + k - 2, (3,))[0]
        a0f[k] = a0p[k]
    finish()
    for fetch in fetches[:2]:
        fetch.wait()

    def subtract(r, at, z, hit):
        slot = (r >> 8) * 4 + ((r >> 5) & 3)
        col = ((r >> 7) & 1) * 64 + ((r >> 4) & 1) * 32 + (r & 15)
        first = obs[slot, col] * scales[0, z]
        second = obs[slot, col + 16]
        a0f[at] = a0f[at] - jnp.where(hit, first, 0.0)
        ef[at] = ef[at] - jnp.where(hit, second, 0.0)

    each_receiver(found, place, subtract)
    for fetch in fetches[2:]:
        fetch.wait()

    stores = []
    for l in range(CZ):
        ia = sponge(z0 + l, (3,))[0]
        for s in range(O, O + CY, 8):
            y = slice(s - O, s - O + 8)
            c = vs[l, y, :] * RATIO
            c = c * c
            q, lap = laplace(a0f, l + 2, s)
            a2s[l, y, :] = (2.0 * q + ef[l + 2, s : s + 8, :] + c * lap) * ia
            a0s[l, y, :] = q
            gs[l, y, :] = gs[l, y, :] + ws[l, y, :] * q
        for i, (src, dst) in enumerate(((a2s, a2), (a0s, a0o), (gs, grad))):
            stores.append(pltpu.make_async_copy(src.at[l], dst.at[l], sem.at[7 + 3 * l + i]))
            stores[-1].start()
    for store in stores:
        store.wait()


def f32(*shape):
    return jax.ShapeDtypeStruct(shape, jnp.float32)


def hbm(*args):
    return tuple(pltpu.with_memory_space_constraint(x, pltpu.HBM) for x in args)


def call(kernel, out_shape, in_specs, scratch_shapes=(), out_specs=None):
    return pl.pallas_call(
        kernel,
        out_shape=out_shape,
        in_specs=in_specs,
        out_specs=tuple(out_specs) if out_specs else (vmem(),) * len(out_shape),
        scratch_shapes=scratch_shapes,
        compiler_params=pltpu.CompilerParams(vmem_limit_bytes=VMEM_LIMIT),
        name=kernel.__name__,
    )


def swap(value, axis, size, first):
    pairs = [(i, (first + ((i - first) % size ^ 1)) % size) for i in range(size)]
    return lax.ppermute(value, axis, pairs)


def swap_open(value, axis, size):
    pairs = [(i, i + 1) for i in range(1, size - 1, 2)]
    return lax.ppermute(value, axis, pairs + [(j, i) for i, j in pairs])


def shards(u, u1, a, a1, v, obs, rec, src, amp):
    assert u.shape == (CZ, CY, NX)
    block, edge = f32(CZ, CY, NX), f32(2, CZ, 8, NX)
    block_hbm = pltpu.HBM(block.shape, block.dtype)
    frame, zpack = f32(8, FR, NX), f32(2, ZROWS, NX)
    part = pltpu.VMEM((2, CZ, 8, NX), jnp.float32)
    full = pltpu.VMEM((8, FR, NX), jnp.float32)
    whole = pltpu.VMEM((CZ, CY, NX), jnp.float32)
    entries = rec.shape[1] + 128
    found_smem = pltpu.SMEM((1, entries), jnp.int32)
    eight_smem = pltpu.SMEM((1, 8), jnp.float32)
    dmas = lambda n: pltpu.SemaphoreType.DMA((n,))

    h, g, own = call(
        pack_y,
        (f32(YROWS + 8, 128), f32(YROWS, 128), f32(1, 128)),
        [anywhere()] * 6,
        [pltpu.VMEM((2, 5, CZ, 8, NX), jnp.float32), pltpu.VMEM((5, CZ, 8, NX), jnp.float32), pltpu.VMEM((2, CZ, 8, NX), jnp.float32)]
        + [pltpu.VMEM((2, 16), jnp.float32), pltpu.VMEM((1, 128), jnp.float32), dmas(11)],
    )(*hbm(u, a, u1, a1, v, obs))
    rh = swap(h, GY, NY_DEV, 0)
    rg = swap(g, GY, NY_DEV, 1)
    two = own + rh[YROWS : YROWS + 1, :]

    short, long = call(
        list_receivers,
        (jax.ShapeDtypeStruct((1, 128), jnp.int32), jax.ShapeDtypeStruct((1, entries), jnp.int32)),
        [vmem()],
        [
            pltpu.VMEM((32, 128), jnp.int32),
            pltpu.VMEM((1, 128), jnp.int32),
            pltpu.VMEM(rec[:1].shape, jnp.int32),
            pltpu.SMEM((1, 128), jnp.int32),
            pltpu.SMEM(rec[:1].shape, jnp.int32),
            found_smem,
            dmas(2),
        ],
        [anywhere()] * 2,
    )(rec)

    u0p, a0p = call(own_step, (block, block), [vmem()] * 5)(u, a, u1, a1, v)
    two, u0p, a0p, short, long = lax.optimization_barrier((two, u0p, a0p, short, long))
    four = two + swap(two, "c", 2, 0)
    ut, at, zc, zb = call(
        edge_step,
        (edge,) * 2 + (pltpu.VMEM(zpack.shape, zpack.dtype),) * 2,
        [vmem()] * 7,
        [part] * 5,
    )(u, a, v, rh, rg, u0p, a0p)

    zc, zb, four = lax.optimization_barrier((zc, zb, four))
    rc = swap(zc, GZ, NZ_DEV, 0)
    rb = swap_open(zb, GZ, NZ_DEV)
    table = lax.all_to_all(jnp.broadcast_to(four, (64, 128)), ("yl", "z", "x"), 0, 0, tiled=True)

    u2, u0, w, gp, ep, a0f = call(
        wave_step,
        (block,) * 2 + (block_hbm,) * 3 + (frame,),
        [anywhere()] * 6 + [vmem()] * 2 + [anywhere()] * 2 + [smem()] * 2 + [anywhere()] * 2,
        [full] * 5
        + [whole] * 2
        + [pltpu.VMEM((2, 2, 8, NX), jnp.float32)]
        + [whole] * 3
        + [found_smem, eight_smem, dmas(19), dmas(20)],
        [anywhere()] * 5 + [vmem()],
    )(*hbm(u, a, u1, v), u0p, a0p, ut, at, *hbm(rc, rb, src, amp), short, long)

    a2, a0, grad = call(
        adjoint_step,
        (block,) * 3,
        [anywhere(), vmem()] + [anywhere()] * 6,
        [full] * 2 + [whole] * 5 + [found_smem, pltpu.SMEM((64, 128), jnp.float32), eight_smem, dmas(19)],
        [anywhere()] * 3,
    )(*hbm(v), a0f, *hbm(w, gp, ep), short, long, table)
    return u2, u0, a2, a0, grad


def solution(mesh):
    fine = Mesh(mesh.devices.reshape(2, 8, 2, 4, 2), ("yl", "z", "c", "x", "yh"))
    field = P(GZ, GY, None)
    return jax.shard_map(
        shards,
        mesh=fine,
        in_specs=(field,) * 5 + (P(None, GZ + GY), P(), P(), P()),
        out_specs=(field,) * 5,
        check_vma=False,
    )
```

```python
import jax
import jax.numpy as jnp
import numpy as np
from jax import lax
from jax.experimental import pallas as pl
from jax.experimental.pallas import tpu as pltpu
from jax.sharding import Mesh
from jax.sharding import PartitionSpec as P

CENTRE = -7.5
NEAR = 4.0 / 3.0
FAR = -1.0 / 12.0
RATIO = 0.1
DAMP = 0.3

GZ = ("yl", "z", "c")
GY = ("x", "yh")
O = 8
NZ_DEV, NY_DEV = 32, 8
CZ, CY, NX = 4, 32, 512
NZ, NY = NZ_DEV * CZ, NY_DEV * CY
FR = CY + 2 * O
VMEM_LIMIT = 8 * 1024 * 1024
ZROWS = 5 * CY + 8
YROWS = CZ * 5 * 8
GROUP = 8


def sponge_table():
    depth = np.arange(CZ + 1, dtype=np.float32) / np.float32(CZ)
    a = np.float32(DAMP) * (depth * depth)
    one = np.float32(1)
    return np.stack([one + a, one - a, one / (one - a), one / (one + a)]).astype(np.float32)


def sponge(z, which):
    into = jnp.minimum(jnp.maximum(jnp.maximum(CZ - z, z - (NZ - 1 - CZ)), 0), CZ)
    values = []
    for row in which:
        table = sponge_table()[row]
        value = jnp.float32(table[0])
        for k in range(1, CZ + 1):
            value = jnp.where(into == k, jnp.float32(table[k]), value)
        values.append(value)
    return values


def place_in_mesh():
    gz, gy = lax.axis_index(GZ), lax.axis_index(GY)
    return gz * CZ, gy * CY, lax.axis_index("yh"), lax.axis_index("c")


def smem():
    return pl.BlockSpec(memory_space=pltpu.SMEM)


def anywhere():
    return pl.BlockSpec(memory_space=pl.ANY)


def vmem():
    return pl.BlockSpec()


def x_terms(u):
    lane = lax.broadcasted_iota(jnp.int32, u.shape, 1)
    a = jnp.where(lane >= 1, pltpu.roll(u, 1, 1), 0.0)
    b = jnp.where(lane < NX - 1, pltpu.roll(u, NX - 1, 1), 0.0)
    c = jnp.where(lane >= 2, pltpu.roll(u, 2, 1), 0.0)
    d = jnp.where(lane < NX - 2, pltpu.roll(u, NX - 2, 1), 0.0)
    return a + b, c + d


def laplace(f, k, s):
    rows = lambda layer, shift: f[layer, s + shift : s + shift + 8, :]
    u = rows(k, 0)
    near, far = x_terms(u)
    near = near + ((rows(k, -1) + rows(k, 1)) + (rows(k - 1, 0) + rows(k + 1, 0)))
    far = far + ((rows(k, -2) + rows(k, 2)) + (rows(k - 2, 0) + rows(k + 2, 0)))
    return u, CENTRE * u + NEAR * near + FAR * far


def depth_factors(l):
    near_up = jnp.where(l >= 1, jnp.float32(NEAR), jnp.float32(0.0))
    near_dn = jnp.where(l < CZ - 1, jnp.float32(NEAR), jnp.float32(0.0))
    far_up = jnp.where(l >= 2, jnp.float32(FAR), jnp.float32(0.0))
    far_dn = jnp.where(l < CZ - 2, jnp.float32(FAR), jnp.float32(0.0))
    layers = jnp.maximum(l - 1, 0), jnp.minimum(l + 1, CZ - 1), jnp.maximum(l - 2, 0), jnp.minimum(l + 2, CZ - 1)
    return tuple(zip(layers, (near_up, near_dn, far_up, far_dn)))


def partial_laplace(f, l, s, factors):
    u = f[l, s : s + 8, :]
    row = lax.broadcasted_iota(jnp.int32, u.shape, 0) + s

    def shifted(shift):
        if 0 <= s + shift and s + shift + 8 <= CY:
            return f[l, s + shift : s + shift + 8, :]
        inside = (row + shift >= 0) & (row + shift < CY)
        return jnp.where(inside, pltpu.roll(u, (-shift) % 8, 0), 0.0)

    near, far = x_terms(u)
    lap = CENTRE * u + NEAR * (near + (shifted(-1) + shifted(1))) + FAR * (far + (shifted(-2) + shifted(2)))
    for layer, factor in factors:
        lap = lap + factor * f[layer, s : s + 8, :]
    return u, lap


def outer_laplace(f, l, factors):
    u = f[l]
    row = lax.broadcasted_iota(jnp.int32, u.shape, 0)

    def shifted(shift):
        return jnp.where((row + shift >= 0) & (row + shift < 8), pltpu.roll(u, (-shift) % 8, 0), 0.0)

    near, far = x_terms(u)
    lap = CENTRE * u + NEAR * (near + (shifted(-1) + shifted(1))) + FAR * (far + (shifted(-2) + shifted(2)))
    for layer, factor in factors:
        lap = lap + factor * f[layer]
    return u, lap


def pack_y(u_hbm, a_hbm, u1_hbm, a1_hbm, v_hbm, obs, h, g, own, outer, both, first_step, obs_v, row, sem):
    z0, _, yh, core = place_in_mesh()
    fetches = [pltpu.make_async_copy(obs, obs_v, sem.at[10])]
    for i, f in enumerate((u_hbm, a_hbm, u1_hbm, a1_hbm, v_hbm)):
        fetches.append(pltpu.make_async_copy(f.at[:, 0:8, :], outer.at[0, i], sem.at[2 * i]))
        fetches.append(pltpu.make_async_copy(f.at[:, CY - 8 : CY, :], outer.at[1, i], sem.at[2 * i + 1]))
    for fetch in fetches:
        fetch.start()
    for fetch in fetches:
        fetch.wait()
    for k in range(4):
        for t in range(2):
            row[0:1, 32 * k + 16 * t : 32 * k + 16 * t + 16] = obs_v[t : t + 1, :]
    slot = lax.broadcasted_iota(jnp.int32, (1, 128), 1) >> 5
    mine = jnp.where(slot == core * 2 + yh, row[0:1, :], 0.0)
    own[...] = mine
    both[:, :, 0:4, :] = outer[0, :, :, 0:4, :]
    both[:, :, 4:8, :] = outer[1, :, :, 4:8, :]

    def layer(l, carry):
        up, dn, iu, ia = sponge(z0 + l, range(4))
        factors = depth_factors(l)
        c = both[4, l] * RATIO
        c = c * c
        p, lap = outer_laplace(both.at[0], l, factors)
        first_step[0, l] = (2.0 * p - up * both[2, l] + c * lap) * iu
        q, lap = outer_laplace(both.at[1], l, factors)
        first_step[1, l] = (2.0 * q - dn * both[3, l] + c * lap) * ia
        return carry

    lax.fori_loop(0, CZ, layer, 0)

    def pack(dst, side):
        two = slice(6, 8) if side else slice(0, 2)
        for l in range(CZ):
            for t in range(5):
                b = 8 * (5 * l + t)
                for i in range(4):
                    if t == 4:
                        part = both[4, l, two, 128 * i : 128 * i + 128]
                    else:
                        f = both if i < 2 else first_step
                        part = f[i % 2, l, two, 128 * t : 128 * t + 128]
                    dst[b + 2 * i : b + 2 * i + 2, :] = part

    @pl.when(yh == 0)
    def _():
        pack(h, 1)
        pack(g, 0)

    @pl.when(yh != 0)
    def _():
        pack(h, 0)
        pack(g, 1)

    h[YROWS : YROWS + 8, :] = jnp.broadcast_to(mine, (8, 128))


def own_step(u, a, u1, a1, v, u0p, a0p):
    z0, _, _, _ = place_in_mesh()

    def layer(l, carry):
        up, dn, iu, ia = sponge(z0 + l, range(4))
        factors = depth_factors(l)
        for s in range(0, CY, 8):
            y = slice(s, s + 8)
            c = v[l, y, :] * RATIO
            c = c * c
            p, lap = partial_laplace(u, l, s, factors)
            u0p[l, y, :] = (2.0 * p - up * u1[l, y, :] + c * lap) * iu
            q, lap = partial_laplace(a, l, s, factors)
            a0p[l, y, :] = (2.0 * q - dn * a1[l, y, :] + c * lap) * ia
        return carry

    lax.fori_loop(0, CZ, layer, 0)


def pick_y(yh, rh, rg, low, high):
    @pl.when(yh == 0)
    def _():
        high(rh)
        low(rg)

    @pl.when(yh != 0)
    def _():
        low(rh)
        high(rg)


def beyond(u):
    row = lax.broadcasted_iota(jnp.int32, u.shape, 0)
    near = jnp.where(row == 3, pltpu.roll(u, 7, 0), 0.0) + jnp.where(row == 4, pltpu.roll(u, 1, 0), 0.0)
    far = jnp.where(row < 4, pltpu.roll(u, 6, 0), pltpu.roll(u, 2, 0))
    return NEAR * near + FAR * far


def edge_step(u, a, v, rh, rg, u0p, a0p, ut, at, zc, zb, pu, pa, pv, pu0, pa0):
    z0, _, yh, core = place_in_mesh()
    parts = (pu, pa, pu0, pa0)
    for part, block in zip(parts + (pv,), (u, a, u0p, a0p, v)):
        part[0, :, 4:6, :] = block[:, 0:2, :]
        part[1, :, 2:4, :] = block[:, CY - 2 : CY, :]

    def received(r, side, first):
        rows = slice(first, first + 2)
        for l in range(CZ):
            for t in range(5):
                b = 8 * (5 * l + t)
                for i in range(4):
                    part, k = (pv, i) if t == 4 else (parts[i], t)
                    part[side, l, rows, 128 * k : 128 * k + 128] = r[b + 2 * i : b + 2 * i + 2, :]

    pick_y(yh, rh, rg, lambda r: received(r, 0, 2), lambda r: received(r, 1, 4))

    def layer(l, carry):
        iu, ia = sponge(z0 + l, (2, 3))
        for side in range(2):
            c = pv[side, l] * RATIO
            c = c * c
            ut[side, l] = pu0[side, l] + (c * iu) * beyond(pu[side, l])
            at[side, l] = pa0[side, l] + (c * ia) * beyond(pa[side, l])
        return carry

    lax.fori_loop(0, CZ, layer, 0)
    ut[0, :, 0:2, :] = pu[0, :, 2:4, :]
    ut[0, :, 6:8, :] = pv[0, :, 2:4, :]
    ut[1, :, 6:8, :] = pu[1, :, 4:6, :]
    ut[1, :, 0:2, :] = pv[1, :, 4:6, :]

    def pack(dst, l):
        m = slice(l, l + 2)
        dst[:, 0:CY, :] = u[m]
        dst[:, CY : 2 * CY, :] = a[m]
        dst[:, 4 * CY : 5 * CY, :] = v[m]
        for b, p, t in ((2 * CY, u0p, ut), (3 * CY, a0p, at)):
            dst[:, b : b + CY, :] = p[m]
            dst[:, b : b + 2, :] = t[0, m, 4:6, :]
            dst[:, b + CY - 2 : b + CY, :] = t[1, m, 2:4, :]
        b = 5 * CY
        dst[:, b : b + 2, :] = pu[0, m, 2:4, :]
        dst[:, b + 2 : b + 4, :] = pu[1, m, 4:6, :]
        dst[:, b + 4 : b + 6, :] = pa[0, m, 2:4, :]
        dst[:, b + 6 : b + 8, :] = pa[1, m, 4:6, :]

    @pl.when(core == 0)
    def _():
        pack(zc, 2)
        pack(zb, 0)

    @pl.when(core != 0)
    def _():
        pack(zc, 0)
        pack(zb, 2)


def list_receivers(rec, short, long, bits, words_v, codes_v, words, codes, found, sem):
    z0, y0, _, _ = place_in_mesh()
    lz = rec[0:1, :] - z0
    ly = ((rec[1:2, :] - y0 + 16) & (NY - 1)) - 16
    x = rec[2:3, :]
    own_z = (lz >= 0) & (lz < CZ)
    own_y = (ly >= 0) & (ly < CY)
    near = (lz >= -2) & (lz < CZ + 2) & (ly >= -2) & (ly < CY + 2) & (own_z | own_y)
    row = ly + O
    number = lax.broadcasted_iota(jnp.int32, lz.shape, 1)
    codes_v[...] = (
        ((row & 7) * 128 + (x & 127)) | ((x >> 7) << 10) | ((row >> 3) << 12) | ((lz + 2) << 15) | (number << 18)
    )
    m = near.astype(jnp.int32)
    for i in range(32):
        bits[i : i + 1, :] = m[:, 128 * i : 128 * i + 128] << i
    words_v[...] = jnp.sum(bits[...], axis=0, keepdims=True)
    copies = [pltpu.make_async_copy(codes_v, codes, sem.at[0]), pltpu.make_async_copy(words_v, words, sem.at[1])]
    for copy in copies:
        copy.start()
    for copy in copies:
        copy.wait()

    def word_step(w, count):
        def bit_step(carry):
            word, count = carry
            low = word & (-word)
            found[0, count + 1] = codes[0, (31 - lax.clz(low)) * 128 + w]
            return word ^ low, count + 1

        return lax.while_loop(lambda carry: carry[0] != 0, bit_step, (words[0, w], count))[1]

    count = lax.fori_loop(0, 128, word_step, 0, unroll=8)
    found[0, 0] = count
    for k in range(GROUP - 1):
        found[0, count + 1 + k] = 0
    copy = pltpu.make_async_copy(found.at[:, 0:128], short, sem.at[0])
    copy.start()
    copy.wait()

    @pl.when(count > 128 - GROUP)
    def _():
        copy = pltpu.make_async_copy(found, long, sem.at[1])
        copy.start()
        copy.wait()


def fetch_list(short, long, found, sem):
    copy = pltpu.make_async_copy(short, found.at[:, 0:128], sem)
    copy.start()

    def finish():
        copy.wait()

        @pl.when(found[0, 0] > 128 - GROUP)
        def _():
            rest = pltpu.make_async_copy(long, found, sem)
            rest.start()
            rest.wait()

    return finish


def cell_place():
    return lax.broadcasted_iota(jnp.int32, (8, 128), 0) * 128 + lax.broadcasted_iota(jnp.int32, (8, 128), 1)


def cell_at(place, layer, row, x):
    rows = pl.ds(pl.multiple_of((row >> 3) << 3, 8), 8)
    cols = pl.ds(pl.multiple_of((x >> 7) << 7, 128), 128)
    return (layer, rows, cols), place == ((row & 7) * 128 + (x & 127))


def wave_step(
    u, a, u1, v, u0p, a0p, ut, at, rc, rb, src, amp, short, long,
    u2, u0o, w, gp, ep, a0f,
    uf, u0f, af, vf, ef, sf, u1s, corners, u2s, ws, gs, found, scales, sem, store_sem,
):
    e = O + CY
    z0, y0, yh, core = place_in_mesh()
    own = (slice(2, 6), slice(O, e), slice(None))
    into = [(u1, u1s), (u0p, u0f.at[own]), (a0p, a0f.at[own]), (u, uf.at[own]), (a, af.at[own]), (v, vf.at[own])]
    for j, r in enumerate((rc, rb)):
        k = 6 * (1 - core) if j == 0 else 6 * core
        for i, f in enumerate((uf, af, u0f, a0f, vf)):
            into.append((r.at[:, i * CY : (i + 1) * CY, :], f.at[pl.ds(k, 2), O:e, :]))
        into.append((r.at[:, 5 * CY : ZROWS, :], corners.at[j]))
    fetches = [pltpu.make_async_copy(part, whole, sem.at[i]) for i, (part, whole) in enumerate(into)]
    for fetch in fetches:
        fetch.start()
    finish = fetch_list(short, long, found, sem.at[len(into)])
    for l in range(CZ):
        sf[l] = jnp.zeros((CY, NX), jnp.float32)
    for fetch in fetches:
        fetch.wait()
    for f0, t in ((u0f, ut), (a0f, at)):
        f0[2:6, O - 2 : O + 2, :] = t[0, :, 2:6, :]
        f0[2:6, e - 2 : e + 2, :] = t[1, :, 2:6, :]
    uf[2:6, O - 2 : O, :] = ut[0, :, 0:2, :]
    uf[2:6, e : e + 2, :] = ut[1, :, 6:8, :]
    vf[2:6, O - 2 : O, :] = ut[0, :, 6:8, :]
    vf[2:6, e : e + 2, :] = ut[1, :, 0:2, :]

    def fill_corners(j, k):
        m = slice(k, k + 2)
        for i, f in enumerate((uf, af)):
            f[m, O - 2 : O, :] = corners[j, :, 4 * i : 4 * i + 2, :]
            f[m, e : e + 2, :] = corners[j, :, 4 * i + 2 : 4 * i + 4, :]

    @pl.when(core == 0)
    def _():
        fill_corners(1, 0)
        fill_corners(0, 6)

    @pl.when(core != 0)
    def _():
        fill_corners(0, 0)
        fill_corners(1, 6)

    lacks = ((0, None, 2), (1, 2, 3), (2, 1, 0), (3, None, 1), (4, None, 6), (5, 6, 7), (6, 5, 4), (7, None, 5))
    for k, near, far in lacks:
        edge = 2 <= k < 6
        iu, ia = sponge(z0 + k - 2, (2, 3))

        def rows(t, carry):
            s = pl.multiple_of(t * 8, 8)
            c = vf[k, pl.ds(s, 8), :] * RATIO
            c = c * c
            for f, f0, scale in ((uf, u0f, iu), (af, a0f, ia)):
                lap = FAR * f[far, pl.ds(s, 8), :]
                if near is not None:
                    lap = lap + NEAR * f[near, pl.ds(s, 8), :]
                f0[k, pl.ds(s, 8), :] = f0[k, pl.ds(s, 8), :] + (c * scale) * lap
            return carry

        first = O // 8
        lax.fori_loop(first - edge, first + CY // 8 + edge, rows, 0)

    place = cell_place()

    def add_source(i, carry):
        lz = src[0, i] - z0
        ly = ((src[1, i] - y0 + 16) & (NY - 1)) - 16
        own_z = (lz >= 0) & (lz < CZ)
        own_y = (ly >= 0) & (ly < CY)
        near = (lz >= -2) & (lz < CZ + 2) & (ly >= -2) & (ly < CY + 2) & (own_z | own_y)

        @pl.when(near)
        def _():
            at, hit = cell_at(place, lz + 2, ly + O, src[2, i])
            c = vf[at] * RATIO
            u0f[at] = u0f[at] + jnp.where(hit, (c * c) * (amp[0, i] * sponge(z0 + lz, (2,))[0]), 0.0)

        @pl.when(own_z & own_y)
        def _():
            at, hit = cell_at(place, lz, ly, src[2, i])
            sf[at] = sf[at] + jnp.where(hit, amp[1, i], 0.0)

        return carry

    lax.fori_loop(0, src.shape[1], add_source, 0)
    for l in range(CZ):
        ef[l + 2, O:e, :] = -sponge(z0 + l, (1,))[0] * af[l + 2, O:e, :]

    def sample(r, at, z, hit):
        a0f[at] = a0f[at] + jnp.where(hit, uf[at] * scales[0, z], 0.0)
        ef[at] = ef[at] + jnp.where(hit, u0f[at], 0.0)

    for k in range(8):
        scales[0, k] = sponge(z0 + k - 2, (3,))[0]
    finish()
    each_receiver(found, place, sample)

    stores = []
    for l in range(CZ):
        up, iu = sponge(z0 + l, (0, 2))
        for s in range(O, e, 8):
            y = slice(s - O, s - O + 8)
            vel = vf[l + 2, s : s + 8, :]
            c = vel * RATIO
            c = c * c
            un = uf[l + 2, s : s + 8, :]
            q, lap = laplace(u0f, l + 2, s)
            new = (2.0 * q - up * un + c * (lap + sf[l, y, :])) * iu
            u2s[l, y, :] = new
            slow = 2.0 / vel
            ws[l, y, :] = slow * (un - 2.0 * q + new)
            gs[l, y, :] = slow * af[l + 2, s : s + 8, :] * (u1s[l, y, :] - 2.0 * un + q)
        done = ((u2s.at[l], u2), (u0f.at[l + 2, O:e, :], u0o), (ws.at[l], w), (gs.at[l], gp), (ef.at[l + 2, O:e, :], ep))
        for i, (part, whole) in enumerate(done):
            stores.append(pltpu.make_async_copy(part, whole.at[l], store_sem.at[5 * l + i]))
            stores[-1].start()
    for store in stores:
        store.wait()


def each_receiver(found, place, one):
    count = found[0, 0]

    def group(b, carry):
        for k in range(GROUP):
            n = b * GROUP + k
            code = found[0, n + 1]
            z = (code >> 15) & 7
            rows = pl.ds(pl.multiple_of(((code >> 12) & 7) * 8, 8), 8)
            cols = pl.ds(pl.multiple_of(((code >> 10) & 3) * 128, 128), 128)
            one(code >> 18, (z, rows, cols), z, place == jnp.where(n < count, code & 1023, -1))
        return carry

    lax.fori_loop(0, (count + GROUP - 1) // GROUP, group, 0)


def adjoint_step(v, a0p, w, gp, ep, short, long, table, a2, a0o, grad, a0f, ef, vs, ws, gs, a2s, found, obs, scales, sem):
    own = (slice(2, 6), slice(O, O + CY), slice(None))
    into = ((table, obs), (ep, ef.at[own]), (v, vs), (w, ws), (gp, gs))
    fetches = [pltpu.make_async_copy(src, dst, sem.at[i]) for i, (src, dst) in enumerate(into)]
    finish = fetch_list(short, long, found, sem.at[6])
    for fetch in fetches:
        fetch.start()
    z0, _, _, _ = place_in_mesh()
    place = cell_place()
    for k in range(8):
        scales[0, k] = sponge(z0 + k - 2, (3,))[0]
        a0f[k] = a0p[k]
    finish()
    for fetch in fetches[:2]:
        fetch.wait()

    def subtract(r, at, z, hit):
        slot = (r >> 8) * 4 + ((r >> 5) & 3)
        col = ((r >> 7) & 1) * 64 + ((r >> 4) & 1) * 32 + (r & 15)
        first = obs[slot, col] * scales[0, z]
        second = obs[slot, col + 16]
        a0f[at] = a0f[at] - jnp.where(hit, first, 0.0)
        ef[at] = ef[at] - jnp.where(hit, second, 0.0)

    each_receiver(found, place, subtract)
    stores = [
        pltpu.make_async_copy(a0f.at[l + 2, O : O + CY, :], a0o.at[l], sem.at[7 + 3 * l + 2]) for l in range(CZ)
    ]
    for store in stores:
        store.start()
    for fetch in fetches[2:]:
        fetch.wait()

    for l in range(CZ):
        ia = sponge(z0 + l, (3,))[0]
        for s in range(O, O + CY, 8):
            y = slice(s - O, s - O + 8)
            c = vs[l, y, :] * RATIO
            c = c * c
            q, lap = laplace(a0f, l + 2, s)
            a2s[l, y, :] = (2.0 * q + ef[l + 2, s : s + 8, :] + c * lap) * ia
            gs[l, y, :] = gs[l, y, :] + ws[l, y, :] * q
        for i, (src, dst) in enumerate(((a2s.at[l], a2), (gs.at[l], grad))):
            stores.append(pltpu.make_async_copy(src, dst.at[l], sem.at[7 + 3 * l + i]))
            stores[-1].start()
    for store in stores:
        store.wait()


def f32(*shape):
    return jax.ShapeDtypeStruct(shape, jnp.float32)


def hbm(*args):
    return tuple(pltpu.with_memory_space_constraint(x, pltpu.HBM) for x in args)


def call(kernel, out_shape, in_specs, scratch_shapes=(), out_specs=None):
    return pl.pallas_call(
        kernel,
        out_shape=out_shape,
        in_specs=in_specs,
        out_specs=tuple(out_specs) if out_specs else (vmem(),) * len(out_shape),
        scratch_shapes=scratch_shapes,
        compiler_params=pltpu.CompilerParams(vmem_limit_bytes=VMEM_LIMIT),
        name=kernel.__name__,
    )


def swap(value, axis, size, first):
    pairs = [(i, (first + ((i - first) % size ^ 1)) % size) for i in range(size)]
    return lax.ppermute(value, axis, pairs)


def swap_open(value, axis, size):
    pairs = [(i, i + 1) for i in range(1, size - 1, 2)]
    return lax.ppermute(value, axis, pairs + [(j, i) for i, j in pairs])


def shards(u, u1, a, a1, v, obs, rec, src, amp):
    assert u.shape == (CZ, CY, NX)
    block, edge = f32(CZ, CY, NX), f32(2, CZ, 8, NX)
    block_hbm = pltpu.HBM(block.shape, block.dtype)
    frame, zpack = f32(8, FR, NX), f32(2, ZROWS, NX)
    part = pltpu.VMEM((2, CZ, 8, NX), jnp.float32)
    full = pltpu.VMEM((8, FR, NX), jnp.float32)
    whole = pltpu.VMEM((CZ, CY, NX), jnp.float32)
    entries = rec.shape[1] + 128
    found_smem = pltpu.SMEM((1, entries), jnp.int32)
    eight_smem = pltpu.SMEM((1, 8), jnp.float32)
    dmas = lambda n: pltpu.SemaphoreType.DMA((n,))

    h, g, own = call(
        pack_y,
        (f32(YROWS + 8, 128), f32(YROWS, 128), f32(1, 128)),
        [anywhere()] * 6,
        [pltpu.VMEM((2, 5, CZ, 8, NX), jnp.float32), pltpu.VMEM((5, CZ, 8, NX), jnp.float32), pltpu.VMEM((2, CZ, 8, NX), jnp.float32)]
        + [pltpu.VMEM((2, 16), jnp.float32), pltpu.VMEM((1, 128), jnp.float32), dmas(11)],
    )(*hbm(u, a, u1, a1, v, obs))
    rh = swap(h, GY, NY_DEV, 0)
    rg = swap(g, GY, NY_DEV, 1)
    two = own + rh[YROWS : YROWS + 1, :]

    short, long = call(
        list_receivers,
        (jax.ShapeDtypeStruct((1, 128), jnp.int32), jax.ShapeDtypeStruct((1, entries), jnp.int32)),
        [vmem()],
        [
            pltpu.VMEM((32, 128), jnp.int32),
            pltpu.VMEM((1, 128), jnp.int32),
            pltpu.VMEM(rec[:1].shape, jnp.int32),
            pltpu.SMEM((1, 128), jnp.int32),
            pltpu.SMEM(rec[:1].shape, jnp.int32),
            found_smem,
            dmas(2),
        ],
        [anywhere()] * 2,
    )(rec)

    u0p, a0p = call(own_step, (block, block), [vmem()] * 5)(u, a, u1, a1, v)
    two, u0p, a0p, short, long = lax.optimization_barrier((two, u0p, a0p, short, long))
    four = two + swap(two, "c", 2, 0)
    ut, at, zc, zb = call(
        edge_step,
        (edge,) * 2 + (pltpu.VMEM(zpack.shape, zpack.dtype),) * 2,
        [vmem()] * 7,
        [part] * 5,
    )(u, a, v, rh, rg, u0p, a0p)

    rc = swap(zc, GZ, NZ_DEV, 0)
    zb, four = lax.optimization_barrier((zb, four))
    rb = swap_open(zb, GZ, NZ_DEV)
    table = lax.all_to_all(jnp.broadcast_to(four, (64, 128)), ("yl", "z", "x"), 0, 0, tiled=True)

    u2, u0, w, gp, ep, a0f = call(
        wave_step,
        (block,) * 2 + (block_hbm,) * 3 + (frame,),
        [anywhere()] * 6 + [vmem()] * 2 + [anywhere()] * 2 + [smem()] * 2 + [anywhere()] * 2,
        [full] * 5
        + [whole] * 2
        + [pltpu.VMEM((2, 2, 8, NX), jnp.float32)]
        + [whole] * 3
        + [found_smem, eight_smem, dmas(19), dmas(20)],
        [anywhere()] * 5 + [vmem()],
    )(*hbm(u, a, u1, v), u0p, a0p, ut, at, *hbm(rc, rb, src, amp), short, long)

    a2, a0, grad = call(
        adjoint_step,
        (block,) * 3,
        [anywhere(), vmem()] + [anywhere()] * 6,
        [full] * 2 + [whole] * 4 + [found_smem, pltpu.SMEM((64, 128), jnp.float32), eight_smem, dmas(19)],
        [anywhere()] * 3,
    )(*hbm(v), a0f, *hbm(w, gp, ep), short, long, table)
    return u2, u0, a2, a0, grad


def solution(mesh):
    fine = Mesh(mesh.devices.reshape(2, 8, 2, 4, 2), ("yl", "z", "c", "x", "yh"))
    field = P(GZ, GY, None)
    return jax.shard_map(
        shards,
        mesh=fine,
        in_specs=(field,) * 5 + (P(None, GZ + GY), P(), P(), P()),
        out_specs=(field,) * 5,
        check_vma=False,
    )
```

```python
import jax
import jax.numpy as jnp
import numpy as np
from jax import lax
from jax.experimental import pallas as pl
from jax.experimental.pallas import tpu as pltpu
from jax.sharding import Mesh
from jax.sharding import PartitionSpec as P

CENTRE = -7.5
NEAR = 4.0 / 3.0
FAR = -1.0 / 12.0
RATIO = 0.1
DAMP = 0.3

GZ = ("yl", "z", "c")
GY = ("x", "yh")
O = 8
NZ_DEV, NY_DEV = 32, 8
CZ, CY, NX = 4, 32, 512
NZ, NY = NZ_DEV * CZ, NY_DEV * CY
FR = CY + 2 * O
VMEM_LIMIT = 8 * 1024 * 1024
ZROWS = 5 * CY + 8
YROWS = CZ * 5 * 8
GROUP = 4


def sponge_table():
    depth = np.arange(CZ + 1, dtype=np.float32) / np.float32(CZ)
    a = np.float32(DAMP) * (depth * depth)
    one = np.float32(1)
    return np.stack([one + a, one - a, one / (one - a), one / (one + a)]).astype(np.float32)


def sponge(z, which):
    into = jnp.minimum(jnp.maximum(jnp.maximum(CZ - z, z - (NZ - 1 - CZ)), 0), CZ)
    values = []
    for row in which:
        table = sponge_table()[row]
        value = jnp.float32(table[0])
        for k in range(1, CZ + 1):
            value = jnp.where(into == k, jnp.float32(table[k]), value)
        values.append(value)
    return values


def place_in_mesh():
    gz, gy = lax.axis_index(GZ), lax.axis_index(GY)
    return gz * CZ, gy * CY, lax.axis_index("yh"), lax.axis_index("c")


def smem():
    return pl.BlockSpec(memory_space=pltpu.SMEM)


def anywhere():
    return pl.BlockSpec(memory_space=pl.ANY)


def vmem():
    return pl.BlockSpec()


def x_terms(u):
    lane = lax.broadcasted_iota(jnp.int32, u.shape, 1)
    a = jnp.where(lane >= 1, pltpu.roll(u, 1, 1), 0.0)
    b = jnp.where(lane < NX - 1, pltpu.roll(u, NX - 1, 1), 0.0)
    c = jnp.where(lane >= 2, pltpu.roll(u, 2, 1), 0.0)
    d = jnp.where(lane < NX - 2, pltpu.roll(u, NX - 2, 1), 0.0)
    return a + b, c + d


def laplace(f, k, s):
    rows = lambda layer, shift: f[layer, s + shift : s + shift + 8, :]
    u = rows(k, 0)
    near, far = x_terms(u)
    near = near + ((rows(k, -1) + rows(k, 1)) + (rows(k - 1, 0) + rows(k + 1, 0)))
    far = far + ((rows(k, -2) + rows(k, 2)) + (rows(k - 2, 0) + rows(k + 2, 0)))
    return u, CENTRE * u + NEAR * near + FAR * far


def depth_factors(l):
    near_up = jnp.where(l >= 1, jnp.float32(NEAR), jnp.float32(0.0))
    near_dn = jnp.where(l < CZ - 1, jnp.float32(NEAR), jnp.float32(0.0))
    far_up = jnp.where(l >= 2, jnp.float32(FAR), jnp.float32(0.0))
    far_dn = jnp.where(l < CZ - 2, jnp.float32(FAR), jnp.float32(0.0))
    layers = jnp.maximum(l - 1, 0), jnp.minimum(l + 1, CZ - 1), jnp.maximum(l - 2, 0), jnp.minimum(l + 2, CZ - 1)
    return tuple(zip(layers, (near_up, near_dn, far_up, far_dn)))


def partial_laplace(f, l, s, factors):
    u = f[l, s : s + 8, :]
    row = lax.broadcasted_iota(jnp.int32, u.shape, 0) + s

    def shifted(shift):
        if 0 <= s + shift and s + shift + 8 <= CY:
            return f[l, s + shift : s + shift + 8, :]
        inside = (row + shift >= 0) & (row + shift < CY)
        return jnp.where(inside, pltpu.roll(u, (-shift) % 8, 0), 0.0)

    near, far = x_terms(u)
    lap = CENTRE * u + NEAR * (near + (shifted(-1) + shifted(1))) + FAR * (far + (shifted(-2) + shifted(2)))
    for layer, factor in factors:
        lap = lap + factor * f[layer, s : s + 8, :]
    return u, lap


def outer_laplace(f, l, factors):
    u = f[l]
    row = lax.broadcasted_iota(jnp.int32, u.shape, 0)

    def shifted(shift):
        return jnp.where((row + shift >= 0) & (row + shift < 8), pltpu.roll(u, (-shift) % 8, 0), 0.0)

    near, far = x_terms(u)
    lap = CENTRE * u + NEAR * (near + (shifted(-1) + shifted(1))) + FAR * (far + (shifted(-2) + shifted(2)))
    for layer, factor in factors:
        lap = lap + factor * f[layer]
    return u, lap


def pack_y(u_hbm, a_hbm, u1_hbm, a1_hbm, v_hbm, obs, h, g, own, outer, both, first_step, obs_v, row, sem):
    z0, _, yh, core = place_in_mesh()
    fetches = [pltpu.make_async_copy(obs, obs_v, sem.at[10])]
    for i, f in enumerate((u_hbm, a_hbm, u1_hbm, a1_hbm, v_hbm)):
        fetches.append(pltpu.make_async_copy(f.at[:, 0:8, :], outer.at[0, i], sem.at[2 * i]))
        fetches.append(pltpu.make_async_copy(f.at[:, CY - 8 : CY, :], outer.at[1, i], sem.at[2 * i + 1]))
    for fetch in fetches:
        fetch.start()
    for fetch in fetches:
        fetch.wait()
    for k in range(4):
        for t in range(2):
            row[0:1, 32 * k + 16 * t : 32 * k + 16 * t + 16] = obs_v[t : t + 1, :]
    slot = lax.broadcasted_iota(jnp.int32, (1, 128), 1) >> 5
    mine = jnp.where(slot == core * 2 + yh, row[0:1, :], 0.0)
    own[...] = mine
    both[:, :, 0:4, :] = outer[0, :, :, 0:4, :]
    both[:, :, 4:8, :] = outer[1, :, :, 4:8, :]

    def layer(l, carry):
        up, dn, iu, ia = sponge(z0 + l, range(4))
        factors = depth_factors(l)
        c = both[4, l] * RATIO
        c = c * c
        p, lap = outer_laplace(both.at[0], l, factors)
        first_step[0, l] = (2.0 * p - up * both[2, l] + c * lap) * iu
        q, lap = outer_laplace(both.at[1], l, factors)
        first_step[1, l] = (2.0 * q - dn * both[3, l] + c * lap) * ia
        return carry

    lax.fori_loop(0, CZ, layer, 0)

    def pack(dst, side):
        two = slice(6, 8) if side else slice(0, 2)
        for l in range(CZ):
            for t in range(5):
                b = 8 * (5 * l + t)
                for i in range(4):
                    if t == 4:
                        part = both[4, l, two, 128 * i : 128 * i + 128]
                    else:
                        f = both if i < 2 else first_step
                        part = f[i % 2, l, two, 128 * t : 128 * t + 128]
                    dst[b + 2 * i : b + 2 * i + 2, :] = part

    @pl.when(yh == 0)
    def _():
        pack(h, 1)
        pack(g, 0)

    @pl.when(yh != 0)
    def _():
        pack(h, 0)
        pack(g, 1)

    h[YROWS : YROWS + 8, :] = jnp.broadcast_to(mine, (8, 128))


def own_step(u, a, u1, a1, v, u0p, a0p):
    z0, _, _, _ = place_in_mesh()

    def layer(l, carry):
        up, dn, iu, ia = sponge(z0 + l, range(4))
        factors = depth_factors(l)
        for s in range(0, CY, 8):
            y = slice(s, s + 8)
            c = v[l, y, :] * RATIO
            c = c * c
            p, lap = partial_laplace(u, l, s, factors)
            u0p[l, y, :] = (2.0 * p - up * u1[l, y, :] + c * lap) * iu
            q, lap = partial_laplace(a, l, s, factors)
            a0p[l, y, :] = (2.0 * q - dn * a1[l, y, :] + c * lap) * ia
        return carry

    lax.fori_loop(0, CZ, layer, 0)


def pick_y(yh, rh, rg, low, high):
    @pl.when(yh == 0)
    def _():
        high(rh)
        low(rg)

    @pl.when(yh != 0)
    def _():
        low(rh)
        high(rg)


def beyond(u):
    row = lax.broadcasted_iota(jnp.int32, u.shape, 0)
    near = jnp.where(row == 3, pltpu.roll(u, 7, 0), 0.0) + jnp.where(row == 4, pltpu.roll(u, 1, 0), 0.0)
    far = jnp.where(row < 4, pltpu.roll(u, 6, 0), pltpu.roll(u, 2, 0))
    return NEAR * near + FAR * far


def edge_step(u, a, v, rh, rg, u0p, a0p, ut, at, zc, zb, pu, pa, pv, pu0, pa0):
    z0, _, yh, core = place_in_mesh()
    parts = (pu, pa, pu0, pa0)
    for part, block in zip(parts + (pv,), (u, a, u0p, a0p, v)):
        part[0, :, 4:6, :] = block[:, 0:2, :]
        part[1, :, 2:4, :] = block[:, CY - 2 : CY, :]

    def received(r, side, first):
        rows = slice(first, first + 2)
        for l in range(CZ):
            for t in range(5):
                b = 8 * (5 * l + t)
                for i in range(4):
                    part, k = (pv, i) if t == 4 else (parts[i], t)
                    part[side, l, rows, 128 * k : 128 * k + 128] = r[b + 2 * i : b + 2 * i + 2, :]

    pick_y(yh, rh, rg, lambda r: received(r, 0, 2), lambda r: received(r, 1, 4))

    def layer(l, carry):
        iu, ia = sponge(z0 + l, (2, 3))
        for side in range(2):
            c = pv[side, l] * RATIO
            c = c * c
            ut[side, l] = pu0[side, l] + (c * iu) * beyond(pu[side, l])
            at[side, l] = pa0[side, l] + (c * ia) * beyond(pa[side, l])
        return carry

    lax.fori_loop(0, CZ, layer, 0)
    ut[0, :, 0:2, :] = pu[0, :, 2:4, :]
    ut[0, :, 6:8, :] = pv[0, :, 2:4, :]
    ut[1, :, 6:8, :] = pu[1, :, 4:6, :]
    ut[1, :, 0:2, :] = pv[1, :, 4:6, :]

    def pack(dst, l):
        m = slice(l, l + 2)
        dst[:, 0:CY, :] = u[m]
        dst[:, CY : 2 * CY, :] = a[m]
        dst[:, 4 * CY : 5 * CY, :] = v[m]
        for b, p, t in ((2 * CY, u0p, ut), (3 * CY, a0p, at)):
            dst[:, b : b + CY, :] = p[m]
            dst[:, b : b + 2, :] = t[0, m, 4:6, :]
            dst[:, b + CY - 2 : b + CY, :] = t[1, m, 2:4, :]
        b = 5 * CY
        dst[:, b : b + 2, :] = pu[0, m, 2:4, :]
        dst[:, b + 2 : b + 4, :] = pu[1, m, 4:6, :]
        dst[:, b + 4 : b + 6, :] = pa[0, m, 2:4, :]
        dst[:, b + 6 : b + 8, :] = pa[1, m, 4:6, :]

    @pl.when(core == 0)
    def _():
        pack(zc, 2)
        pack(zb, 0)

    @pl.when(core != 0)
    def _():
        pack(zc, 0)
        pack(zb, 2)


def list_receivers(rec, short, long, bits, words_v, codes_v, words, codes, found, sem):
    z0, y0, _, _ = place_in_mesh()
    lz = rec[0:1, :] - z0
    ly = ((rec[1:2, :] - y0 + 16) & (NY - 1)) - 16
    x = rec[2:3, :]
    own_z = (lz >= 0) & (lz < CZ)
    own_y = (ly >= 0) & (ly < CY)
    near = (lz >= -2) & (lz < CZ + 2) & (ly >= -2) & (ly < CY + 2) & (own_z | own_y)
    row = ly + O
    number = lax.broadcasted_iota(jnp.int32, lz.shape, 1)
    codes_v[...] = (
        ((row & 7) * 128 + (x & 127)) | ((x >> 7) << 10) | ((row >> 3) << 12) | ((lz + 2) << 15) | (number << 18)
    )
    m = near.astype(jnp.int32)
    for i in range(32):
        bits[i : i + 1, :] = m[:, 128 * i : 128 * i + 128] << i
    words_v[...] = jnp.sum(bits[...], axis=0, keepdims=True)
    copies = [pltpu.make_async_copy(codes_v, codes, sem.at[0]), pltpu.make_async_copy(words_v, words, sem.at[1])]
    for copy in copies:
        copy.start()
    for copy in copies:
        copy.wait()

    def word_step(w, count):
        def bit_step(carry):
            word, count = carry
            low = word & (-word)
            found[0, count + 1] = codes[0, (31 - lax.clz(low)) * 128 + w]
            return word ^ low, count + 1

        return lax.while_loop(lambda carry: carry[0] != 0, bit_step, (words[0, w], count))[1]

    count = lax.fori_loop(0, 128, word_step, 0, unroll=32)
    found[0, 0] = count
    for k in range(GROUP - 1):
        found[0, count + 1 + k] = 0
    copy = pltpu.make_async_copy(found.at[:, 0:128], short, sem.at[0])
    copy.start()
    copy.wait()

    @pl.when(count > 128 - GROUP)
    def _():
        copy = pltpu.make_async_copy(found, long, sem.at[1])
        copy.start()
        copy.wait()


def fetch_list(short, long, found, sem):
    copy = pltpu.make_async_copy(short, found.at[:, 0:128], sem)
    copy.start()

    def finish():
        copy.wait()

        @pl.when(found[0, 0] > 128 - GROUP)
        def _():
            rest = pltpu.make_async_copy(long, found, sem)
            rest.start()
            rest.wait()

    return finish


def cell_place():
    return lax.broadcasted_iota(jnp.int32, (8, 128), 0) * 128 + lax.broadcasted_iota(jnp.int32, (8, 128), 1)


def cell_at(place, layer, row, x):
    rows = pl.ds(pl.multiple_of((row >> 3) << 3, 8), 8)
    cols = pl.ds(pl.multiple_of((x >> 7) << 7, 128), 128)
    return (layer, rows, cols), place == ((row & 7) * 128 + (x & 127))


def wave_step(
    u, a, u1, v, u0p, a0p, ut, at, rc, rb, src, amp, short, long,
    u2, u0o, w, gp, ep, a0f,
    uf, u0f, af, vf, ef, sf, u1s, corners, u2s, ws, gs, found, scales, sem, store_sem,
):
    e = O + CY
    z0, y0, yh, core = place_in_mesh()
    own = (slice(2, 6), slice(O, e), slice(None))
    into = [(u1, u1s), (u0p, u0f.at[own]), (a0p, a0f.at[own]), (u, uf.at[own]), (a, af.at[own]), (v, vf.at[own])]
    for j, r in enumerate((rc, rb)):
        k = 6 * (1 - core) if j == 0 else 6 * core
        for i, f in enumerate((uf, af, u0f, a0f, vf)):
            into.append((r.at[:, i * CY : (i + 1) * CY, :], f.at[pl.ds(k, 2), O:e, :]))
        into.append((r.at[:, 5 * CY : ZROWS, :], corners.at[j]))
    fetches = [pltpu.make_async_copy(part, whole, sem.at[i]) for i, (part, whole) in enumerate(into)]
    for fetch in fetches:
        fetch.start()
    finish = fetch_list(short, long, found, sem.at[len(into)])
    for l in range(CZ):
        sf[l] = jnp.zeros((CY, NX), jnp.float32)
    for fetch in fetches:
        fetch.wait()
    for f0, t in ((u0f, ut), (a0f, at)):
        f0[2:6, O - 2 : O + 2, :] = t[0, :, 2:6, :]
        f0[2:6, e - 2 : e + 2, :] = t[1, :, 2:6, :]
    uf[2:6, O - 2 : O, :] = ut[0, :, 0:2, :]
    uf[2:6, e : e + 2, :] = ut[1, :, 6:8, :]
    vf[2:6, O - 2 : O, :] = ut[0, :, 6:8, :]
    vf[2:6, e : e + 2, :] = ut[1, :, 0:2, :]

    def fill_corners(j, k):
        m = slice(k, k + 2)
        for i, f in enumerate((uf, af)):
            f[m, O - 2 : O, :] = corners[j, :, 4 * i : 4 * i + 2, :]
            f[m, e : e + 2, :] = corners[j, :, 4 * i + 2 : 4 * i + 4, :]

    @pl.when(core == 0)
    def _():
        fill_corners(1, 0)
        fill_corners(0, 6)

    @pl.when(core != 0)
    def _():
        fill_corners(0, 0)
        fill_corners(1, 6)

    lacks = ((0, None, 2), (1, 2, 3), (2, 1, 0), (3, None, 1), (4, None, 6), (5, 6, 7), (6, 5, 4), (7, None, 5))
    for k, near, far in lacks:
        edge = 2 <= k < 6
        iu, ia = sponge(z0 + k - 2, (2, 3))

        def rows(t, carry):
            s = pl.multiple_of(t * 8, 8)
            c = vf[k, pl.ds(s, 8), :] * RATIO
            c = c * c
            for f, f0, scale in ((uf, u0f, iu), (af, a0f, ia)):
                lap = FAR * f[far, pl.ds(s, 8), :]
                if near is not None:
                    lap = lap + NEAR * f[near, pl.ds(s, 8), :]
                f0[k, pl.ds(s, 8), :] = f0[k, pl.ds(s, 8), :] + (c * scale) * lap
            return carry

        first = O // 8
        lax.fori_loop(first - edge, first + CY // 8 + edge, rows, 0)

    place = cell_place()

    def add_source(i, carry):
        lz = src[0, i] - z0
        ly = ((src[1, i] - y0 + 16) & (NY - 1)) - 16
        own_z = (lz >= 0) & (lz < CZ)
        own_y = (ly >= 0) & (ly < CY)
        near = (lz >= -2) & (lz < CZ + 2) & (ly >= -2) & (ly < CY + 2) & (own_z | own_y)

        @pl.when(near)
        def _():
            at, hit = cell_at(place, lz + 2, ly + O, src[2, i])
            c = vf[at] * RATIO
            u0f[at] = u0f[at] + jnp.where(hit, (c * c) * (amp[0, i] * sponge(z0 + lz, (2,))[0]), 0.0)

        @pl.when(own_z & own_y)
        def _():
            at, hit = cell_at(place, lz, ly, src[2, i])
            sf[at] = sf[at] + jnp.where(hit, amp[1, i], 0.0)

        return carry

    lax.fori_loop(0, src.shape[1], add_source, 0)
    for l in range(CZ):
        ef[l + 2, O:e, :] = -sponge(z0 + l, (1,))[0] * af[l + 2, O:e, :]

    def sample(r, at, z, hit):
        a0f[at] = a0f[at] + jnp.where(hit, uf[at] * scales[0, z], 0.0)
        ef[at] = ef[at] + jnp.where(hit, u0f[at], 0.0)

    for k in range(8):
        scales[0, k] = sponge(z0 + k - 2, (3,))[0]
    finish()
    each_receiver(found, place, sample)

    stores = []
    for l in range(CZ):
        up, iu = sponge(z0 + l, (0, 2))
        for s in range(O, e, 8):
            y = slice(s - O, s - O + 8)
            vel = vf[l + 2, s : s + 8, :]
            c = vel * RATIO
            c = c * c
            un = uf[l + 2, s : s + 8, :]
            q, lap = laplace(u0f, l + 2, s)
            new = (2.0 * q - up * un + c * (lap + sf[l, y, :])) * iu
            u2s[l, y, :] = new
            slow = 2.0 / vel
            ws[l, y, :] = slow * (un - 2.0 * q + new)
            gs[l, y, :] = slow * af[l + 2, s : s + 8, :] * (u1s[l, y, :] - 2.0 * un + q)
        done = ((u2s.at[l], u2), (u0f.at[l + 2, O:e, :], u0o), (ws.at[l], w), (gs.at[l], gp), (ef.at[l + 2, O:e, :], ep))
        for i, (part, whole) in enumerate(done):
            stores.append(pltpu.make_async_copy(part, whole.at[l], store_sem.at[5 * l + i]))
            stores[-1].start()
    for store in stores:
        store.wait()


def each_receiver(found, place, one):
    count = found[0, 0]

    def group(b, carry):
        for k in range(GROUP):
            n = b * GROUP + k
            code = found[0, n + 1]
            z = (code >> 15) & 7
            rows = pl.ds(pl.multiple_of(((code >> 12) & 7) * 8, 8), 8)
            cols = pl.ds(pl.multiple_of(((code >> 10) & 3) * 128, 128), 128)
            one(code >> 18, (z, rows, cols), z, place == jnp.where(n < count, code & 1023, -1))
        return carry

    lax.fori_loop(0, (count + GROUP - 1) // GROUP, group, 0)


def adjoint_step(v, a0p, w, gp, ep, short, long, table, a2, a0o, grad, a0f, ef, vs, ws, gs, a2s, a0s, found, obs, scales, sem):
    own = (slice(2, 6), slice(O, O + CY), slice(None))
    into = ((table, obs), (ep, ef.at[own]), (v, vs), (w, ws), (gp, gs))
    fetches = [pltpu.make_async_copy(src, dst, sem.at[i]) for i, (src, dst) in enumerate(into)]
    finish = fetch_list(short, long, found, sem.at[6])
    for fetch in fetches:
        fetch.start()
    z0, _, _, _ = place_in_mesh()
    place = cell_place()
    for k in range(8):
        scales[0, k] = sponge(z0 + k - 2, (3,))[0]
        a0f[k] = a0p[k]
    finish()
    for fetch in fetches[:2]:
        fetch.wait()

    def subtract(r, at, z, hit):
        slot = (r >> 8) * 4 + ((r >> 5) & 3)
        col = ((r >> 7) & 1) * 64 + ((r >> 4) & 1) * 32 + (r & 15)
        first = obs[slot, col] * scales[0, z]
        second = obs[slot, col + 16]
        a0f[at] = a0f[at] - jnp.where(hit, first, 0.0)
        ef[at] = ef[at] - jnp.where(hit, second, 0.0)

    each_receiver(found, place, subtract)
    for fetch in fetches[2:]:
        fetch.wait()

    stores = []
    for l in range(CZ):
        ia = sponge(z0 + l, (3,))[0]
        for s in range(O, O + CY, 8):
            y = slice(s - O, s - O + 8)
            c = vs[l, y, :] * RATIO
            c = c * c
            q, lap = laplace(a0f, l + 2, s)
            a2s[l, y, :] = (2.0 * q + ef[l + 2, s : s + 8, :] + c * lap) * ia
            a0s[l, y, :] = q
            gs[l, y, :] = gs[l, y, :] + ws[l, y, :] * q
        for i, (src, dst) in enumerate(((a2s, a2), (a0s, a0o), (gs, grad))):
            stores.append(pltpu.make_async_copy(src.at[l], dst.at[l], sem.at[7 + 3 * l + i]))
            stores[-1].start()
    for store in stores:
        store.wait()


def f32(*shape):
    return jax.ShapeDtypeStruct(shape, jnp.float32)


def hbm(*args):
    return tuple(pltpu.with_memory_space_constraint(x, pltpu.HBM) for x in args)


def call(kernel, out_shape, in_specs, scratch_shapes=(), out_specs=None):
    return pl.pallas_call(
        kernel,
        out_shape=out_shape,
        in_specs=in_specs,
        out_specs=tuple(out_specs) if out_specs else (vmem(),) * len(out_shape),
        scratch_shapes=scratch_shapes,
        compiler_params=pltpu.CompilerParams(vmem_limit_bytes=VMEM_LIMIT),
        name=kernel.__name__,
    )


def swap(value, axis, size, first):
    pairs = [(i, (first + ((i - first) % size ^ 1)) % size) for i in range(size)]
    return lax.ppermute(value, axis, pairs)


def swap_open(value, axis, size):
    pairs = [(i, i + 1) for i in range(1, size - 1, 2)]
    return lax.ppermute(value, axis, pairs + [(j, i) for i, j in pairs])


def shards(u, u1, a, a1, v, obs, rec, src, amp):
    assert u.shape == (CZ, CY, NX)
    block, edge = f32(CZ, CY, NX), f32(2, CZ, 8, NX)
    block_hbm = pltpu.HBM(block.shape, block.dtype)
    frame, zpack = f32(8, FR, NX), f32(2, ZROWS, NX)
    part = pltpu.VMEM((2, CZ, 8, NX), jnp.float32)
    full = pltpu.VMEM((8, FR, NX), jnp.float32)
    whole = pltpu.VMEM((CZ, CY, NX), jnp.float32)
    entries = rec.shape[1] + 128
    found_smem = pltpu.SMEM((1, entries), jnp.int32)
    eight_smem = pltpu.SMEM((1, 8), jnp.float32)
    dmas = lambda n: pltpu.SemaphoreType.DMA((n,))

    h, g, own = call(
        pack_y,
        (f32(YROWS + 8, 128), f32(YROWS, 128), f32(1, 128)),
        [anywhere()] * 6,
        [pltpu.VMEM((2, 5, CZ, 8, NX), jnp.float32), pltpu.VMEM((5, CZ, 8, NX), jnp.float32), pltpu.VMEM((2, CZ, 8, NX), jnp.float32)]
        + [pltpu.VMEM((2, 16), jnp.float32), pltpu.VMEM((1, 128), jnp.float32), dmas(11)],
    )(*hbm(u, a, u1, a1, v, obs))
    rh = swap(h, GY, NY_DEV, 0)
    rg = swap(g, GY, NY_DEV, 1)
    two = own + rh[YROWS : YROWS + 1, :]

    short, long = call(
        list_receivers,
        (jax.ShapeDtypeStruct((1, 128), jnp.int32), jax.ShapeDtypeStruct((1, entries), jnp.int32)),
        [vmem()],
        [
            pltpu.VMEM((32, 128), jnp.int32),
            pltpu.VMEM((1, 128), jnp.int32),
            pltpu.VMEM(rec[:1].shape, jnp.int32),
            pltpu.SMEM((1, 128), jnp.int32),
            pltpu.SMEM(rec[:1].shape, jnp.int32),
            found_smem,
            dmas(2),
        ],
        [anywhere()] * 2,
    )(rec)

    u0p, a0p = call(own_step, (block, block), [vmem()] * 5)(u, a, u1, a1, v)
    two, u0p, a0p, short, long = lax.optimization_barrier((two, u0p, a0p, short, long))
    four = two + swap(two, "c", 2, 0)
    ut, at, zc, zb = call(
        edge_step,
        (edge,) * 2 + (pltpu.VMEM(zpack.shape, zpack.dtype),) * 2,
        [vmem()] * 7,
        [part] * 5,
    )(u, a, v, rh, rg, u0p, a0p)

    rc = swap(zc, GZ, NZ_DEV, 0)
    zb, four = lax.optimization_barrier((zb, four))
    rb = swap_open(zb, GZ, NZ_DEV)
    table = lax.all_to_all(jnp.broadcast_to(four, (64, 128)), ("yl", "z", "x"), 0, 0, tiled=True)

    u2, u0, w, gp, ep, a0f = call(
        wave_step,
        (block,) * 2 + (block_hbm,) * 3 + (frame,),
        [anywhere()] * 6 + [vmem()] * 2 + [anywhere()] * 2 + [smem()] * 2 + [anywhere()] * 2,
        [full] * 5
        + [whole] * 2
        + [pltpu.VMEM((2, 2, 8, NX), jnp.float32)]
        + [whole] * 3
        + [found_smem, eight_smem, dmas(19), dmas(20)],
        [anywhere()] * 5 + [vmem()],
    )(*hbm(u, a, u1, v), u0p, a0p, ut, at, *hbm(rc, rb, src, amp), short, long)

    a2, a0, grad = call(
        adjoint_step,
        (block,) * 3,
        [anywhere(), vmem()] + [anywhere()] * 6,
        [full] * 2 + [whole] * 5 + [found_smem, pltpu.SMEM((64, 128), jnp.float32), eight_smem, dmas(19)],
        [anywhere()] * 3,
    )(*hbm(v), a0f, *hbm(w, gp, ep), short, long, table)
    return u2, u0, a2, a0, grad


def solution(mesh):
    fine = Mesh(mesh.devices.reshape(2, 8, 2, 4, 2), ("yl", "z", "c", "x", "yh"))
    field = P(GZ, GY, None)
    return jax.shard_map(
        shards,
        mesh=fine,
        in_specs=(field,) * 5 + (P(None, GZ + GY), P(), P(), P()),
        out_specs=(field,) * 5,
        check_vma=False,
    )
```
